32 devices in a mesh: seq: 4 (over y, core), ctx: 8 (over z, x).
Axes of the slice: x: 2, y: 2, z: 4, core: 2. Of those that a mesh axis runs over, the one named last changes fastest.
Arguments:
- tokens: bfloat16 [4, 1024, 1536], P('seq', 'ctx'), may hold values from -6 to 6
- lengths: int32 [4], P('seq'), may hold values from 640 to 1024, as said below
- attn_gain: bfloat16 [1536], P(('seq', 'ctx')), may hold values from 0.099609375 to 1.8984375
- qkv_weight: bfloat16 [1536, 2048], P(('seq', 'ctx')), may hold values from -0.15625 to 0.15625
- qkv_bias: bfloat16 [2048], P(('seq', 'ctx')), may hold values from -3 to 3
- out_weight: bfloat16 [1536, 1536], P(('seq', 'ctx')), may hold values from -3.390625 to 3.390625
- mlp_gain: bfloat16 [1536], P(('seq', 'ctx')), may hold values from 0.099609375 to 1.8984375
- gate_weight: bfloat16 [1536, 8960], P(('seq', 'ctx')), may hold values from -0.15625 to 0.15625
- up_weight: bfloat16 [1536, 8960], P(('seq', 'ctx')), may hold values from -0.15625 to 0.15625
- down_weight: bfloat16 [8960, 1536], P(('seq', 'ctx')), may hold values from -0.0625 to 0.0625
- out_grad: bfloat16 [4, 1024, 1536], P('seq', 'ctx'), may hold values from -6 to 6
Outputs:
- output: bfloat16 [4, 1024, 1536], P('seq', 'ctx')
- input_grad: bfloat16 [4, 1024, 1536], P('seq', 'ctx')
- attn_gain_grad: float32 [1536], P(('seq', 'ctx'))
- qkv_weight_grad: float32 [1536, 2048], P(('seq', 'ctx'))
- qkv_bias_grad: float32 [1792], P(('seq', 'ctx'))
- out_weight_grad: float32 [1536, 1536], P(('seq', 'ctx'))
- mlp_gain_grad: float32 [1536], P(('seq', 'ctx'))
- gate_weight_grad: float32 [1536, 8960], P(('seq', 'ctx'))
- up_weight_grad: float32 [1536, 8960], P(('seq', 'ctx'))
- down_weight_grad: float32 [8960, 1536], P(('seq', 'ctx'))
- value_bias_grad: float32 [256], P(('seq', 'ctx'))
The draws below stay inside these ranges and needn't reach their ends.
Inputs may be any that keep to these rules, and one draw needn't show every extreme that they name: `lengths`: each length is a multiple of 128; in every draw at least one sequence has length exactly 1024 and at least one is shorter.
All inputs are finite; a program needn't handle non-finite values.
Results may differ from the reference program's by a relative error of at most 0.025.
Values may be sent and summed in bfloat16 or wider, within the bound.
A program may use at most 512 MiB of HBM per device.

```python
import math
import jax
import jax.numpy as jnp
from jax import lax

D = 1536
HEADS = 12
KV_HEADS = 2
HEAD = 128
FF = 8960
SEQ_LEN = 1024
SEQS = 4
QDIM = 1536
KVDIM = 256
QKV = 2048


def draw_lengths(key, part):
    key = jax.random.fold_in(key, 7)
    first_key, second_key, third_key, fourth_key = jax.random.split(key, 4)
    choices_count = max(2, SEQ_LEN // 256)
    shortened = jax.random.randint(first_key, (SEQS,), 0, choices_count) * 128
    longest = jax.random.randint(second_key, (), 0, SEQS)
    shorter = (longest + 1 + jax.random.randint(third_key, (), 0, SEQS - 1)) % SEQS
    forced = jax.random.randint(fourth_key, (), 1, choices_count) * 128
    index_row = jnp.arange(SEQS)
    shortened = jnp.where(index_row == shorter, forced, shortened)
    shortened = jnp.where(index_row == longest, 0, shortened)
    return (SEQ_LEN - shortened).astype(jnp.int32)


def shard_levels(rng, extent, pieces, low, high):
    level, own = 1.0, jax.random.fold_in(rng, 6)
    for position, blocks in pieces:
        heights = jnp.exp(jax.random.uniform(jax.random.fold_in(own, position), (blocks,), jnp.float32, low / len(pieces), high / len(pieces)))
        level = level * jnp.repeat(heights, extent[position] // blocks).reshape([-1 if axis == position else 1 for axis in range(len(extent))])
    return level


def bell_draw(stream_key, shape, scale, reach, shards=(), kind=jnp.bfloat16):
    entries = jax.random.normal(stream_key, shape, jnp.float32) * scale
    if len(shards) > 0:
        entries = shard_levels(stream_key, shape, shards, -0.22, 0.18) * entries
    return jnp.clip(entries, min=-reach, max=reach).astype(kind)


def setup_inputs(seed: int = 0) -> dict:
    arg_keys = jax.random.split(jax.random.key(seed), 12)
    return {
        "tokens": bell_draw(arg_keys[0], (SEQS, SEQ_LEN, D), 1.0, 6.0, ((0, 4), (1, 8))),
        "lengths": draw_lengths(jax.random.fold_in(arg_keys[11], 71), 0),
        "attn_gain": jnp.clip(1.0 + 0.18 * jax.random.normal(arg_keys[2], (D,), jnp.float32), 0.099609375, 1.8984375).astype(jnp.bfloat16),
        "qkv_weight": bell_draw(arg_keys[3], (D, QKV), D ** -0.5, 0.15625, ((0, 32),)),
        "qkv_bias": bell_draw(arg_keys[4], (QKV,), 0.5, 3.0, ((0, 32),)),
        "out_weight": bell_draw(arg_keys[5], (QDIM, D), (0.2 * (SEQ_LEN // 128) ** 0.5), 3.390625, ((0, 32),)),
        "mlp_gain": jnp.clip(1.0 + 0.18 * jax.random.normal(arg_keys[6], (D,), jnp.float32), 0.099609375, 1.8984375).astype(jnp.bfloat16),
        "gate_weight": bell_draw(arg_keys[7], (D, FF), D ** -0.5, 0.15625, ((0, 32),)),
        "up_weight": bell_draw(arg_keys[8], (D, FF), D ** -0.5, 0.15625, ((0, 32),)),
        "down_weight": bell_draw(arg_keys[9], (FF, D), FF ** -0.5, 0.0625, ((0, 32),)),
        "out_grad": bell_draw(arg_keys[10], (SEQS, SEQ_LEN, D), 1.0, 6.0, ((0, 4), (1, 8))),
    }


EPSILON = 1e-06
ROPE_BASE = 1000000.0
MASKED = -1e+30
HIGHEST = lax.Precision.HIGHEST

@jax.custom_vjp
def low(v):
    return lax.optimization_barrier(v.astype(jnp.bfloat16)).astype(jnp.float32)

@jax.custom_vjp
def low_back(v):
    return v

def low_keep(v):
    return (low(v), None)

def low_pass(kept, grad):
    return (grad,)

def back_keep(v):
    return (v, None)

def back_low(kept, grad):
    return (low(grad),)
low.defvjp(low_keep, low_pass)
low_back.defvjp(back_keep, back_low)

def product(left, right):
    return jnp.dot(left, right, precision=HIGHEST, preferred_element_type=jnp.float32)

def rms_scale(values, gain):
    return values * lax.rsqrt(lax.optimization_barrier(jnp.mean(values * values, axis=-1, keepdims=True)) + EPSILON) * gain

def rotate(values, positions):
    half_width = values.shape[-1] // 2
    frequency = ROPE_BASE ** (-jnp.arange(half_width, dtype=jnp.float32) * 2.0 / values.shape[-1])
    angles = positions[:, None] * frequency[None, :]
    cosine = jnp.cos(angles)[:, None, :]
    sine_part = jnp.sin(angles)[:, None, :]
    first_half = values[..., :half_width]
    second = values[..., half_width:]
    return jnp.concatenate([first_half * cosine - second * sine_part, second * cosine + first_half * sine_part], axis=-1)

def layer_forward(inputs, seq_length, attn_gain, qkv_weight, qkv_bias, out_weight, mlp_gain, gate_weight, up_weight, down_weight):
    total_rows = inputs.shape[0]
    group_size = HEADS // KV_HEADS
    positions = jnp.arange(total_rows, dtype=jnp.int32)
    pos_float = positions.astype(jnp.float32)
    living = (positions < seq_length).astype(jnp.float32)
    normed_one = low(rms_scale(inputs, attn_gain))
    project = low_back(product(normed_one, qkv_weight) + qkv_bias)
    queries = project[:, :QDIM].reshape(total_rows, HEADS, HEAD)
    keys = project[:, QDIM:QDIM + KVDIM].reshape(total_rows, KV_HEADS, HEAD)
    values = low(project[:, QDIM + KVDIM:].reshape(total_rows, KV_HEADS, HEAD))
    queries = low(rotate(queries, pos_float)).reshape(total_rows, KV_HEADS, group_size, HEAD)
    keys = low(rotate(keys, pos_float))
    block_rows = math.gcd(512, total_rows)
    blocks = total_rows // block_rows
    query_blocks = queries.reshape(blocks, block_rows, KV_HEADS, group_size, HEAD)
    starts = jnp.arange(blocks, dtype=jnp.int32) * block_rows
    scale_factor = HEAD ** (-0.5)

    @jax.checkpoint
    def attend(block_item):
        query_block, start_row = block_item
        scores = low_back(jnp.einsum('qgha,kga->ghqk', query_block, keys, precision=HIGHEST) * scale_factor)
        row_pos = start_row + jnp.arange(block_rows, dtype=jnp.int32)
        allowed = (positions[None, :] <= row_pos[:, None]) & (positions[None, :] < seq_length)
        scores = jnp.where(allowed, scores, MASKED)
        largest = lax.optimization_barrier(jnp.max(scores, axis=-1, keepdims=True))
        exponent = jnp.exp(scores - largest)
        attn_probs = low(exponent / lax.optimization_barrier(jnp.sum(exponent, axis=-1, keepdims=True)))
        return jnp.einsum('ghqk,kga->qgha', attn_probs, values, precision=HIGHEST)
    attended = lax.map(attend, (query_blocks, starts)).reshape(total_rows, QDIM)
    attended = low_back(low(attended))
    branch_out = low_back(product(attended, out_weight))
    middle = inputs + branch_out
    normed_two = low(rms_scale(middle, mlp_gain))
    gate_pre = low_back(product(normed_two, gate_weight))
    up_pre = low_back(product(normed_two, up_weight))
    activated = low(gate_pre * jax.nn.sigmoid(gate_pre) * up_pre)
    return (middle + product(activated, down_weight)) * living[:, None]

def reference(tokens, lengths, attn_gain, qkv_weight, qkv_bias, out_weight, mlp_gain, gate_weight, up_weight, down_weight, out_grad):
    weights = tuple((weight.astype(jnp.float32) for weight in (attn_gain, qkv_weight, qkv_bias, out_weight, mlp_gain, gate_weight, up_weight, down_weight)))

    def per_sequence(running, element):
        seq_rows, seq_length, cotangent = element

        def forward(rows_in, *params):
            return layer_forward(rows_in, seq_length, *params)
        result, pullback = jax.vjp(forward, seq_rows, *weights)
        gradients = pullback(cotangent)
        updated = tuple((total + grad_part for total, grad_part in zip(running, gradients[1:])))
        return (updated, (result.astype(jnp.bfloat16), gradients[0].astype(jnp.bfloat16)))
    initial = tuple((jnp.zeros_like(weight) for weight in weights))
    totals, (outputs, input_grads) = lax.scan(per_sequence, initial, (tokens.astype(jnp.float32), lengths, out_grad.astype(jnp.float32)))
    qk_width = QDIM + KVDIM
    return (outputs, input_grads, totals[0], totals[1], totals[2][:qk_width], totals[3], totals[4], totals[5], totals[6], totals[7], totals[2][qk_width:])
```

```python
import jax
import jax.numpy as jnp
from jax import lax
from jax.sharding import PartitionSpec as P

HEADS = 12
KV_HEADS = 2
HEAD = 128
QDIM = 1536
KVDIM = 256
GROUP = HEADS // KV_HEADS

EPSILON = 1e-06
ROPE_BASE = 1000000.0
MASKED = -1e30
SCALE = HEAD ** (-0.5)
BF = jnp.bfloat16
F32 = jnp.float32
BOTH = ("seq", "ctx")


def product(left, right):
    return jnp.dot(left, right, preferred_element_type=F32)


def contract_rows(left, right):
    return lax.dot_general(left, right, (((0,), (0,)), ((), ())), preferred_element_type=F32)


def contract_cols(left, right):
    return lax.dot_general(left, right, (((1,), (1,)), ((), ())), preferred_element_type=F32)


def inverse_rms(values):
    return lax.rsqrt(jnp.mean(values * values, axis=-1, keepdims=True) + EPSILON)


def rms_back(values, inverse, scaled_grad):
    inner = jnp.mean(scaled_grad * values, axis=-1, keepdims=True)
    return inverse * scaled_grad - values * (inverse * inverse * inverse) * inner


def rope_tables(positions):
    half = HEAD // 2
    frequency = ROPE_BASE ** (-jnp.arange(half, dtype=F32) * 2.0 / HEAD)
    angles = positions.astype(F32)[:, None] * frequency[None, :]
    return jnp.cos(angles), jnp.sin(angles)


def rotate(values, cosine, sine):
    half = HEAD // 2
    first, second = values[..., :half], values[..., half:]
    cosine, sine = cosine[:, None, :], sine[:, None, :]
    return jnp.concatenate([first * cosine - second * sine, second * cosine + first * sine], -1)


def gather(values, axes):
    return lax.all_gather(values, axes, axis=0, tiled=True)


def scatter(values, axes):
    return lax.psum_scatter(values, axes, scatter_dimension=0, tiled=True)


def shards(
    tokens,
    lengths,
    attn_gain,
    qkv_weight,
    qkv_bias,
    out_weight,
    mlp_gain,
    gate_weight,
    up_weight,
    down_weight,
    out_grad,
):
    seqs, parts = lax.axis_size("seq"), lax.axis_size("ctx")
    inputs = tokens[0].astype(F32)
    rows, width = inputs.shape
    owned, hidden = gate_weight.shape
    piece = down_weight.shape[0]
    chunk = hidden // parts
    length = lengths[0]
    positions = lax.axis_index("ctx") * rows + jnp.arange(rows, dtype=jnp.int32)
    living = (positions < length).astype(F32)[:, None]
    cosine, sine = rope_tables(positions)

    gain_one = attn_gain.astype(F32)[:, None]
    gain_two = mlp_gain.astype(F32)[:, None]
    qkv_all = gather((qkv_weight.astype(F32) * gain_one).astype(BF), BOTH)
    bias_all = gather(qkv_bias, BOTH).astype(F32)
    out_all = gather(out_weight, BOTH)

    def to_chunks(weight):
        scaled = (weight.astype(F32) * gain_two).astype(BF)
        return scaled.reshape(owned, seqs, parts, piece).transpose(2, 0, 1, 3)

    both = jnp.stack([to_chunks(gate_weight), to_chunks(up_weight)], axis=1)
    both = lax.all_to_all(both.reshape(parts, 2, owned, chunk), "ctx", 0, 0)
    both = lax.all_gather(both, "seq", axis=0)
    gate_chunk = both[:, :, 0].reshape(width, chunk)
    up_chunk = both[:, :, 1].reshape(width, chunk)
    down_chunk = gather(down_weight, "seq")
    cotangent = out_grad[0].astype(F32) * living
    cot_all = gather(cotangent.astype(BF), "ctx")

    inverse_one = inverse_rms(inputs)
    normed_one = (inputs * inverse_one).astype(BF)
    project = product(normed_one, qkv_all) + bias_all
    queries = rotate(project[:, :QDIM].reshape(rows, HEADS, HEAD), cosine, sine).astype(BF)
    own_keys = rotate(
        project[:, QDIM : QDIM + KVDIM].reshape(rows, KV_HEADS, HEAD), cosine, sine
    ).astype(BF)
    own_values = project[:, QDIM + KVDIM :].astype(BF).reshape(rows, KV_HEADS, HEAD)
    keys, values = gather(own_keys, "ctx"), gather(own_values, "ctx")
    key_pos = jnp.arange(rows * parts, dtype=jnp.int32)
    allowed = (key_pos[None, :] <= positions[:, None]) & (key_pos[None, :] < length)
    grouped = queries.reshape(rows, KV_HEADS, GROUP, HEAD)
    scores = jnp.einsum("qgha,kga->ghqk", grouped, keys, preferred_element_type=F32) * SCALE
    scores = jnp.where(allowed, scores, MASKED)
    largest = jnp.max(scores, axis=-1, keepdims=True)
    exponent = jnp.exp(scores - largest)
    summed = jnp.sum(exponent, axis=-1, keepdims=True)
    probs = exponent / summed
    probs_low = probs.astype(BF)
    attended = jnp.einsum("ghqk,kga->qgha", probs_low, values, preferred_element_type=F32)
    attended = attended.reshape(rows, QDIM).astype(BF)
    middle = inputs + product(attended, out_all)

    inverse_two = inverse_rms(middle)
    normed_two = gather((middle * inverse_two).astype(BF), "ctx")
    gate_pre = product(normed_two, gate_chunk)
    up_pre = product(normed_two, up_chunk)
    sig = jax.nn.sigmoid(gate_pre)
    activated = (gate_pre * sig * up_pre).astype(BF)
    grad_act = contract_cols(cot_all, down_chunk)
    grad_gate = (grad_act * up_pre * (sig + gate_pre * sig * (1.0 - sig))).astype(BF)
    grad_up = (grad_act * gate_pre * sig).astype(BF)
    scaled_two = contract_cols(grad_gate, gate_chunk) + contract_cols(grad_up, up_chunk)
    scaled_two = scatter(scaled_two.astype(BF), "ctx").astype(F32)
    branch = scatter(product(activated, down_chunk).astype(BF), "ctx").astype(F32)
    output = ((middle + branch) * living).astype(BF)
    grad_down = scatter(contract_rows(activated, cot_all).astype(BF), "seq").astype(F32)
    raw = jnp.stack([contract_rows(normed_two, grad_gate), contract_rows(normed_two, grad_up)], 1)
    raw = scatter(raw.astype(BF), "seq").reshape(parts, owned, 2, chunk)
    raw = lax.all_to_all(raw, "ctx", 0, 0).astype(F32)
    raw = raw.reshape(parts, owned, 2, seqs, piece).transpose(2, 1, 3, 0, 4)
    raw = raw.reshape(2, owned, hidden)
    grad_mlp_gain = jnp.sum(raw[0] * gate_weight.astype(F32) + raw[1] * up_weight.astype(F32), 1)

    grad_middle = cotangent + rms_back(middle, inverse_two, scaled_two)
    grad_branch = grad_middle.astype(BF)
    grad_out = scatter(contract_rows(attended, grad_branch).astype(BF), BOTH).astype(F32)
    grad_mixed = contract_cols(grad_branch, out_all).astype(BF)
    grad_mixed = grad_mixed.reshape(rows, KV_HEADS, GROUP, HEAD)
    grad_probs = jnp.einsum("qgha,kga->ghqk", grad_mixed, values, preferred_element_type=F32)
    inner = jnp.sum(probs * grad_probs, axis=-1, keepdims=True)
    grad_scores = (probs * (grad_probs - inner)).astype(BF)
    grad_q = jnp.einsum("ghqk,kga->qgha", grad_scores, keys, preferred_element_type=F32) * SCALE
    grad_k = jnp.einsum("ghqk,qgha->kga", grad_scores, grouped, preferred_element_type=F32) * SCALE
    grad_v = jnp.einsum("ghqk,qgha->kga", probs_low, grad_mixed, preferred_element_type=F32)
    grad_k = scatter(grad_k.astype(BF), "ctx").astype(F32)
    grad_v = scatter(grad_v.astype(BF), "ctx").astype(F32)
    grad_q = rotate(grad_q.reshape(rows, HEADS, HEAD), cosine, -sine).reshape(rows, QDIM)
    grad_k = rotate(grad_k, cosine, -sine).reshape(rows, KVDIM)
    grad_project = jnp.concatenate([grad_q, grad_k, grad_v.reshape(rows, KVDIM)], axis=1)
    grad_project = grad_project.astype(BF)
    raw_qkv = scatter(contract_rows(normed_one, grad_project).astype(BF), BOTH).astype(F32)
    grad_attn_gain = jnp.sum(raw_qkv * qkv_weight.astype(F32), axis=1)
    grad_bias = jnp.sum(grad_project.astype(F32), axis=0)
    qk_width = QDIM + KVDIM
    grad_qk_bias = scatter(grad_bias[:qk_width], BOTH)
    grad_value_bias = scatter(grad_bias[qk_width:], BOTH)
    scaled_one = contract_cols(grad_project, qkv_all)
    grad_inputs = (grad_middle + rms_back(inputs, inverse_one, scaled_one)).astype(BF)
    return (
        output[None],
        grad_inputs[None],
        grad_attn_gain,
        raw_qkv * gain_one,
        grad_qk_bias,
        grad_out,
        grad_mlp_gain,
        raw[0] * gain_two,
        raw[1] * gain_two,
        grad_down,
        grad_value_bias,
    )


def solution(mesh):
    rows, vector = P(BOTH, None), P(BOTH)
    token = P("seq", "ctx", None)
    return jax.shard_map(
        shards,
        mesh=mesh,
        in_specs=(token, P("seq"), vector, rows, vector, rows, vector, rows, rows, rows, token),
        out_specs=(token, token, vector, rows, vector, rows, vector, rows, rows, rows, vector),
        check_vma=False,
    )
```

```python
import functools

import jax
import jax.numpy as jnp
import numpy as np
from jax import lax
from jax.experimental import pallas as pl
from jax.experimental.pallas import tpu as pltpu
from jax.sharding import PartitionSpec as P

HEADS = 12
KV_HEADS = 2
HEAD = 128
QDIM = 1536
KVDIM = 256
GROUP = HEADS // KV_HEADS

EPSILON = 1e-06
ROPE_BASE = 1000000.0
MASKED = -1e30
SCALE = HEAD ** (-0.5)
BF = jnp.bfloat16
F32 = jnp.float32
BOTH = ("seq", "ctx")


DMA = pltpu.SemaphoreType.DMA
MESH = pl.DeviceIdType.MESH


def product(left, right):
    return jnp.dot(left, right, preferred_element_type=F32)


def contract_rows(left, right):
    return lax.dot_general(left, right, (((0,), (0,)), ((), ())), preferred_element_type=F32)


def contract_cols(left, right):
    return lax.dot_general(left, right, (((1,), (1,)), ((), ())), preferred_element_type=F32)


def inverse_rms(values):
    return lax.rsqrt(jnp.mean(values * values, axis=-1, keepdims=True) + EPSILON)


def rms_back(values, inverse, scaled_grad):
    inner = jnp.mean(scaled_grad * values, axis=-1, keepdims=True)
    return inverse * scaled_grad - values * (inverse * inverse * inverse) * inner


def rope_tables(positions):
    half = HEAD // 2
    frequency = ROPE_BASE ** (-jnp.arange(half, dtype=F32) * 2.0 / HEAD)
    angles = positions.astype(F32)[:, None] * frequency[None, :]
    return jnp.cos(angles), jnp.sin(angles)


def rotate(values, cosine, sine):
    half = HEAD // 2
    first, second = values[..., :half], values[..., half:]
    cosine, sine = cosine[:, None, :], sine[:, None, :]
    return jnp.concatenate([first * cosine - second * sine, second * cosine + first * sine], -1)


def gather(values, axes):
    return lax.all_gather(values, axes, axis=0, tiled=True)


def scatter(values, axes):
    return lax.psum_scatter(values, axes, scatter_dimension=0, tiled=True)


def plain_shards(
    tokens,
    lengths,
    attn_gain,
    qkv_weight,
    qkv_bias,
    out_weight,
    mlp_gain,
    gate_weight,
    up_weight,
    down_weight,
    out_grad,
):
    seqs, parts = lax.axis_size("seq"), lax.axis_size("ctx")
    inputs = tokens[0].astype(F32)
    rows, width = inputs.shape
    owned, hidden = gate_weight.shape
    piece = down_weight.shape[0]
    chunk = hidden // parts
    length = lengths[0]
    positions = lax.axis_index("ctx") * rows + jnp.arange(rows, dtype=jnp.int32)
    living = (positions < length).astype(F32)[:, None]
    cosine, sine = rope_tables(positions)

    gain_one = attn_gain.astype(F32)[:, None]
    gain_two = mlp_gain.astype(F32)[:, None]
    qkv_all = gather((qkv_weight.astype(F32) * gain_one).astype(BF), BOTH)
    bias_all = gather(qkv_bias, BOTH).astype(F32)
    out_all = gather(out_weight, BOTH)

    def to_chunks(weight):
        scaled = (weight.astype(F32) * gain_two).astype(BF)
        return scaled.reshape(owned, seqs, parts, piece).transpose(2, 0, 1, 3)

    both = jnp.stack([to_chunks(gate_weight), to_chunks(up_weight)], axis=1)
    both = lax.all_to_all(both.reshape(parts, 2, owned, chunk), "ctx", 0, 0)
    both = lax.all_gather(both, "seq", axis=0)
    gate_chunk = both[:, :, 0].reshape(width, chunk)
    up_chunk = both[:, :, 1].reshape(width, chunk)
    down_chunk = gather(down_weight, "seq")
    cotangent = out_grad[0].astype(F32) * living
    cot_all = gather(cotangent.astype(BF), "ctx")

    inverse_one = inverse_rms(inputs)
    normed_one = (inputs * inverse_one).astype(BF)
    project = product(normed_one, qkv_all) + bias_all
    queries = rotate(project[:, :QDIM].reshape(rows, HEADS, HEAD), cosine, sine).astype(BF)
    own_keys = rotate(
        project[:, QDIM : QDIM + KVDIM].reshape(rows, KV_HEADS, HEAD), cosine, sine
    ).astype(BF)
    own_values = project[:, QDIM + KVDIM :].astype(BF).reshape(rows, KV_HEADS, HEAD)
    keys, values = gather(own_keys, "ctx"), gather(own_values, "ctx")
    key_pos = jnp.arange(rows * parts, dtype=jnp.int32)
    allowed = (key_pos[None, :] <= positions[:, None]) & (key_pos[None, :] < length)
    grouped = queries.reshape(rows, KV_HEADS, GROUP, HEAD)
    scores = jnp.einsum("qgha,kga->ghqk", grouped, keys, preferred_element_type=F32) * SCALE
    scores = jnp.where(allowed, scores, MASKED)
    largest = jnp.max(scores, axis=-1, keepdims=True)
    exponent = jnp.exp(scores - largest)
    summed = jnp.sum(exponent, axis=-1, keepdims=True)
    probs = exponent / summed
    probs_low = probs.astype(BF)
    attended = jnp.einsum("ghqk,kga->qgha", probs_low, values, preferred_element_type=F32)
    attended = attended.reshape(rows, QDIM).astype(BF)
    middle = inputs + product(attended, out_all)

    inverse_two = inverse_rms(middle)
    normed_two = gather((middle * inverse_two).astype(BF), "ctx")
    gate_pre = product(normed_two, gate_chunk)
    up_pre = product(normed_two, up_chunk)
    sig = jax.nn.sigmoid(gate_pre)
    activated = (gate_pre * sig * up_pre).astype(BF)
    grad_act = contract_cols(cot_all, down_chunk)
    grad_gate = (grad_act * up_pre * (sig + gate_pre * sig * (1.0 - sig))).astype(BF)
    grad_up = (grad_act * gate_pre * sig).astype(BF)
    scaled_two = contract_cols(grad_gate, gate_chunk) + contract_cols(grad_up, up_chunk)
    scaled_two = scatter(scaled_two.astype(BF), "ctx").astype(F32)
    branch = scatter(product(activated, down_chunk).astype(BF), "ctx").astype(F32)
    output = ((middle + branch) * living).astype(BF)
    grad_down = scatter(contract_rows(activated, cot_all).astype(BF), "seq").astype(F32)
    raw = jnp.stack([contract_rows(normed_two, grad_gate), contract_rows(normed_two, grad_up)], 1)
    raw = scatter(raw.astype(BF), "seq").reshape(parts, owned, 2, chunk)
    raw = lax.all_to_all(raw, "ctx", 0, 0).astype(F32)
    raw = raw.reshape(parts, owned, 2, seqs, piece).transpose(2, 1, 3, 0, 4)
    raw = raw.reshape(2, owned, hidden)
    grad_mlp_gain = jnp.sum(raw[0] * gate_weight.astype(F32) + raw[1] * up_weight.astype(F32), 1)

    grad_middle = cotangent + rms_back(middle, inverse_two, scaled_two)
    grad_branch = grad_middle.astype(BF)
    grad_out = scatter(contract_rows(attended, grad_branch).astype(BF), BOTH).astype(F32)
    grad_mixed = contract_cols(grad_branch, out_all).astype(BF)
    grad_mixed = grad_mixed.reshape(rows, KV_HEADS, GROUP, HEAD)
    grad_probs = jnp.einsum("qgha,kga->ghqk", grad_mixed, values, preferred_element_type=F32)
    inner = jnp.sum(probs * grad_probs, axis=-1, keepdims=True)
    grad_scores = (probs * (grad_probs - inner)).astype(BF)
    grad_q = jnp.einsum("ghqk,kga->qgha", grad_scores, keys, preferred_element_type=F32) * SCALE
    grad_k = jnp.einsum("ghqk,qgha->kga", grad_scores, grouped, preferred_element_type=F32) * SCALE
    grad_v = jnp.einsum("ghqk,qgha->kga", probs_low, grad_mixed, preferred_element_type=F32)
    grad_k = scatter(grad_k.astype(BF), "ctx").astype(F32)
    grad_v = scatter(grad_v.astype(BF), "ctx").astype(F32)
    grad_q = rotate(grad_q.reshape(rows, HEADS, HEAD), cosine, -sine).reshape(rows, QDIM)
    grad_k = rotate(grad_k, cosine, -sine).reshape(rows, KVDIM)
    grad_project = jnp.concatenate([grad_q, grad_k, grad_v.reshape(rows, KVDIM)], axis=1)
    grad_project = grad_project.astype(BF)
    raw_qkv = scatter(contract_rows(normed_one, grad_project).astype(BF), BOTH).astype(F32)
    grad_attn_gain = jnp.sum(raw_qkv * qkv_weight.astype(F32), axis=1)
    grad_bias = jnp.sum(grad_project.astype(F32), axis=0)
    qk_width = QDIM + KVDIM
    grad_qk_bias = scatter(grad_bias[:qk_width], BOTH)
    grad_value_bias = scatter(grad_bias[qk_width:], BOTH)
    scaled_one = contract_cols(grad_project, qkv_all)
    grad_inputs = (grad_middle + rms_back(inputs, inverse_one, scaled_one)).astype(BF)
    return (
        output[None],
        grad_inputs[None],
        grad_attn_gain,
        raw_qkv * gain_one,
        grad_qk_bias,
        grad_out,
        grad_mlp_gain,
        raw[0] * gain_two,
        raw[1] * gain_two,
        grad_down,
        grad_value_bias,
    )


class Place:
    def __init__(self, n):
        self.n = n
        self.s, self.c = lax.axis_index("seq"), lax.axis_index("ctx")
        self.me = self.s * n + self.c
        self.core = lax.rem(self.s, 2)
        self.sib = self.s + 1 - 2 * self.core
        self.far = lax.rem(self.s + 2, 4)
        half = self.c // 2
        self.pos = half + lax.rem(self.c, 2) * (n - 1 - 2 * half)
        self.nxt, self.prv = self.at(1), self.at(-1)
    def at(self, offset):
        p = lax.rem(self.pos + offset + 2 * self.n, self.n)
        return 2 * p + (p // (self.n // 2)) * (2 * self.n - 1 - 4 * p)

def send(src, dst, ssem, rsem, seq, ctx):
    copy = pltpu.make_async_remote_copy(src, dst, ssem, rsem, device_id=(seq, ctx), device_id_type=MESH)
    copy.start()

def arrived(dst, rsem, place):
    pltpu.make_async_remote_copy(dst, dst, rsem, rsem, device_id=(place.s, place.c), device_id_type=MESH).wait_recv()

def sent(src, ssem, place):
    pltpu.make_async_remote_copy(src, src, ssem, ssem, device_id=(place.s, place.c), device_id_type=MESH).wait_send()

def enter(place, whole_group=True):
    barrier = pltpu.get_barrier_semaphore()
    def greet(d, z):
        pl.semaphore_signal(barrier, inc=1, device_id=(place.s, lax.rem(place.c + d, place.n)), device_id_type=MESH)
        return z
    lax.fori_loop(1, place.n, greet, 0)
    pl.semaphore_signal(barrier, inc=1, device_id=(place.sib, place.c), device_id_type=MESH)
    pl.semaphore_signal(barrier, inc=1, device_id=(place.far, place.c), device_id_type=MESH)
    pl.semaphore_wait(barrier, place.n + 1)


def rope(values, table_c, table_s):
    return values * table_c + pltpu.roll(values, HEAD // 2, 1) * table_s

def forward_kernel(n, length_ref, x_ref, og_ref, qkv, outw, gu, down, tables,
                   gu_all, down_all, cot_all, n2_all, qkv_all, out_all, kv_all, q_out, att_out, mid_out,
                   qkv_v, out_v, xh_v, cot_v, kv_v, q_v, att_v, mid_v, n2_v, tab_v,
                   local, save, q_recv, q_ring, q_sib, q_far, o_recv, o_ring, o_far, o_sib,
                   g_recv, g_send, g_far, g_sib, d_recv, d_far, d_sib, c_recv, c_ring,
                   k_recv, k_ring, n_recv, n_ring):
    pc = Place(n)
    me, s, c = pc.me, pc.s, pc.c
    rows, width = x_ref.shape
    owned, piece = gu.shape[2], down.shape[0]
    ohalf, chalf = outw.shape[1] // 2, width // 2
    steps = n - 1
    length = length_ref[0]
    ways = ((0, -1, pc.nxt), (1, 1, pc.prv))

    def o_slot(i, f): return out_v.at[i, :, pl.ds(f * ohalf, ohalf)]
    def half_of(ref, f): return ref.at[:, pl.ds(f * chalf, chalf)]
    def c_slot(i, f): return cot_all.at[i, :, pl.ds(f * chalf, chalf)]
    def n_slot(i, f): return n2_all.at[i, :, pl.ds(f * chalf, chalf)]
    def k_slot(i, f): return kv_v.at[i, :, pl.ds(f * KVDIM, KVDIM)]
    def g_slot(i): return gu_all.at[:, pl.ds(pl.multiple_of(i * owned, owned), owned), :]
    def d_slot(i): return down_all.at[pl.ds(pl.multiple_of(i * piece, piece), piece), :]

    enter(pc)
    first = pl.multiple_of(c * rows, rows)
    lc = [pltpu.make_async_copy(a, b, local.at[i]) for i, (a, b) in enumerate((
        (qkv, qkv_v.at[me]), (outw, out_v.at[me]), (gu.at[c], g_slot(me)), (down, d_slot(s)),
        (tables.at[:, pl.ds(first, rows), :], tab_v)))]
    for copy in lc: copy.start()
    send(qkv, qkv_v.at[me], q_far.at[0], q_recv.at[me], pc.far, c)
    send(qkv, qkv_v.at[me], q_sib.at[me], q_recv.at[me], pc.sib, c)
    for f, _, to in ways:
        src = outw.at[:, pl.ds(f * ohalf, ohalf)]
        send(src, o_slot(me, f), o_ring.at[f, c], o_recv.at[f, me], s, to)
        send(src, o_slot(me, f), o_far.at[f, c], o_recv.at[f, me], pc.far, c)
        send(src, o_slot(me, f), o_sib.at[f, me], o_recv.at[f, me], pc.sib, c)
    send(down, d_slot(s), d_far.at[0], d_recv.at[s], pc.far, c)
    send(down, d_slot(s), d_sib.at[s], d_recv.at[s], pc.sib, c)
    x = x_ref[...].astype(F32)
    xh_v[...] = (x * inverse_rms(x)).astype(BF)
    slot_pos = c * rows + lax.broadcasted_iota(jnp.int32, (rows, width), 0)
    cot_v[...] = jnp.where(slot_pos < length, og_ref[...].astype(F32), 0.0).astype(BF)
    other = pc.far * n + c
    arrived(qkv_v.at[other], q_recv.at[other], pc)
    lc[0].wait()
    for f, _, to in ways:
        i = (2 * f + pc.core) * n + c
        send(qkv_v.at[i], qkv_v.at[i], q_ring.at[f, c], q_recv.at[i], s, to)
    send(qkv_v.at[other], qkv_v.at[other], q_sib.at[other], q_recv.at[other], pc.sib, c)

    def turn_q(t, z):
        for f, sign, to in ways:
            src = pc.at(sign * (t + 1))
            i = (2 * f + pc.core) * n + src
            arrived(qkv_v.at[i], q_recv.at[i], pc)
            @pl.when(t < steps - 1)
            def _():
                send(qkv_v.at[i], qkv_v.at[i], q_ring.at[f, src], q_recv.at[i], s, to)
            send(qkv_v.at[i], qkv_v.at[i], q_sib.at[i], q_recv.at[i], pc.sib, c)
        for f, sign, to in ways:
            src = pc.at(sign * (t + 1))
            j = s * n + src
            arrived(o_slot(j, f), o_recv.at[f, j], pc)
            @pl.when(t < steps - 1)
            def _():
                send(o_slot(j, f), o_slot(j, f), o_ring.at[f, src], o_recv.at[f, j], s, to)
            send(o_slot(j, f), o_slot(j, f), o_far.at[f, src], o_recv.at[f, j], pc.far, c)
            send(o_slot(j, f), o_slot(j, f), o_sib.at[f, j], o_recv.at[f, j], pc.sib, c)
        return z
    lax.fori_loop(0, steps, turn_q, 0)

    own_cot = pltpu.make_async_copy(cot_v, cot_all.at[c], local.at[5])
    own_cot.start()
    for f, _, to in ways:
        send(half_of(cot_v, f), c_slot(c, f), c_ring.at[f, c], c_recv.at[f, c], s, to)
    def feed(d, z):
        to = lax.rem(c + d, n)
        send(gu.at[to], g_slot(me), g_send.at[to], g_recv.at[me], s, to)
        return z
    lax.fori_loop(1, n, feed, 0)
    send(gu.at[c], g_slot(me), g_far.at[c], g_recv.at[me], pc.far, c)
    send(gu.at[c], g_slot(me), g_sib.at[me], g_recv.at[me], pc.sib, c)

    def rest_q(t, z):
        for plane in range(2):
            i = (2 * plane + 1 - pc.core) * n + t
            arrived(qkv_v.at[i], q_recv.at[i], pc)
        return z
    lax.fori_loop(0, n, rest_q, 0)
    lc[4].wait()
    owners = 4 * n
    qk = QDIM + 2 * KVDIM
    tile = 256
    xh = xh_v[...]
    def bias_of(j):
        parts = []
        for k in range(tile // 128):
            d = 2 * (2 * j + k)
            row = qkv_v[d, 0:1, qk : qk + 128] + qkv_v[d + 1, 0:1, qk : qk + 128]
            parts.append(row)
        return jnp.concatenate(parts, 1).astype(F32)
    def project(j):
        w = qkv_v[:, :, pl.ds(pl.multiple_of(j * tile, tile), tile)].reshape(owners * owned, tile)
        return product(xh, w) + bias_of(j)
    tc, ts = tab_v[0], tab_v[1]
    keys = project(QDIM // tile)
    for k in range(KV_HEADS):
        kv_v[c, :, k * HEAD : (k + 1) * HEAD] = rope(keys[:, k * HEAD : (k + 1) * HEAD], tc, ts).astype(BF)
    kv_v[c, :, KVDIM:] = project(QDIM // tile + 1).astype(BF)
    for f, _, to in ways:
        send(k_slot(c, f), k_slot(c, f), k_ring.at[f, c], k_recv.at[f, c], s, to)
    def queries(j, z):
        p = project(j)
        for k in range(tile // HEAD):
            q_v[j * (tile // HEAD) + k] = rope(p[:, k * HEAD : (k + 1) * HEAD], tc, ts).astype(BF)
        return z
    lax.fori_loop(0, QDIM // tile, queries, 0)
    q_save = pltpu.make_async_copy(qkv_v, qkv_all, save.at[0])
    q_save.start()
    q_save2 = pltpu.make_async_copy(q_v, q_out, save.at[1])
    q_save2.start()
    def turn_k(t, z):
        for f, sign, to in ways:
            src = pc.at(sign * (t + 1))
            arrived(k_slot(src, f), k_recv.at[f, src], pc)
            @pl.when(t < steps - 1)
            def _():
                send(k_slot(src, f), k_slot(src, f), k_ring.at[f, src], k_recv.at[f, src], s, to)
        for f, sign, to in ways:
            src = pc.at(sign * (t + 1))
            arrived(c_slot(src, f), c_recv.at[f, src], pc)
            @pl.when(t < steps - 1)
            def _():
                send(c_slot(src, f), c_slot(src, f), c_ring.at[f, src], c_recv.at[f, src], s, to)
        return z
    lax.fori_loop(0, steps, turn_k, 0)
    kv_save = pltpu.make_async_copy(kv_v, kv_all, save.at[2])
    kv_save.start()

    total = n * rows
    at_row = c * rows + lax.broadcasted_iota(jnp.int32, (rows, total), 0)
    at_col = lax.broadcasted_iota(jnp.int32, (rows, total), 1)
    allowed = (at_col <= at_row) & (at_col < length)
    def head(h, z):
        col = pl.multiple_of(h // GROUP * HEAD, HEAD)
        key = kv_v[:, :, pl.ds(col, HEAD)].reshape(total, HEAD)
        val = kv_v[:, :, pl.ds(pl.multiple_of(KVDIM + col, HEAD), HEAD)].reshape(total, HEAD)
        scores = jnp.where(allowed, contract_cols(q_v[h], key) * SCALE, MASKED)
        e = jnp.exp(scores - jnp.max(scores, axis=1, keepdims=True))
        probs = (e / jnp.sum(e, axis=1, keepdims=True)).astype(BF)
        att_v[:, pl.ds(pl.multiple_of(h * HEAD, HEAD), HEAD)] = product(probs, val).astype(BF)
        return z
    lax.fori_loop(0, HEADS, head, 0)
    a_save = pltpu.make_async_copy(att_v, att_out, save.at[3])
    a_save.start()

    def across_o(t, z):
        for f, sign, to in ways:
            j = pc.far * n + pc.at(sign * t)
            arrived(o_slot(j, f), o_recv.at[f, j], pc)
            send(o_slot(j, f), o_slot(j, f), o_sib.at[f, j], o_recv.at[f, j], pc.sib, c)
        return z
    lax.fori_loop(0, n, across_o, 0)
    def rest_o(t, z):
        for plane in range(2):
            i = (2 * plane + 1 - pc.core) * n + t
            for f in range(2): arrived(o_slot(i, f), o_recv.at[f, i], pc)
        return z
    lax.fori_loop(0, n, rest_o, 0)
    lc[1].wait()
    o_save = pltpu.make_async_copy(out_v, out_all, save.at[4])
    o_save.start()
    att = att_v[...]
    def mix(j, z):
        cols = pl.ds(pl.multiple_of(j * tile, tile), tile)
        w = out_v[:, :, cols].reshape(owners * owned, tile)
        mid_v[:, cols] = x_ref[:, cols].astype(F32) + product(att, w)
        return z
    lax.fori_loop(0, width // tile, mix, 0)
    m_save = pltpu.make_async_copy(mid_v, mid_out, save.at[5])
    m_save.start()
    mid = mid_v[...]
    n2_v[...] = (mid * inverse_rms(mid)).astype(BF)
    own_n2 = pltpu.make_async_copy(n2_v, n2_all.at[c], local.at[6])
    own_n2.start()
    for f, _, to in ways:
        send(half_of(n2_v, f), n_slot(c, f), n_ring.at[f, c], n_recv.at[f, c], s, to)
    def turn_n(t, z):
        for f, sign, to in ways:
            src = pc.at(sign * (t + 1))
            arrived(n_slot(src, f), n_recv.at[f, src], pc)
            @pl.when(t < steps - 1)
            def _():
                send(n_slot(src, f), n_slot(src, f), n_ring.at[f, src], n_recv.at[f, src], s, to)
        src = lax.rem(c + n - 1 - t, n)
        k = s * n + src
        arrived(g_slot(k), g_recv.at[k], pc)
        send(g_slot(k), g_slot(k), g_far.at[src], g_recv.at[k], pc.far, c)
        send(g_slot(k), g_slot(k), g_sib.at[k], g_recv.at[k], pc.sib, c)
        return z
    lax.fori_loop(0, steps, turn_n, 0)
    arrived(d_slot(pc.far), d_recv.at[pc.far], pc)
    send(d_slot(pc.far), d_slot(pc.far), d_sib.at[pc.far], d_recv.at[pc.far], pc.sib, c)
    def across(t, z):
        k = pc.far * n + lax.rem(c + n - t, n)
        arrived(g_slot(k), g_recv.at[k], pc)
        send(g_slot(k), g_slot(k), g_sib.at[k], g_recv.at[k], pc.sib, c)
        return z
    lax.fori_loop(0, n, across, 0)
    for plane in range(2):
        row = 2 * plane + 1 - pc.core
        arrived(d_slot(row), d_recv.at[row], pc)
        def rest(t, z):
            i = row * n + t
            arrived(g_slot(i), g_recv.at[i], pc)
            return z
        lax.fori_loop(0, n, rest, 0)
    for copy in lc[2:4] + [own_cot, own_n2, q_save, q_save2, kv_save, a_save, o_save, m_save]: copy.wait()
    o_any = outw.at[:, pl.ds(0, ohalf)]
    sent(qkv, q_far.at[0], pc)
    sent(down, d_far.at[0], pc)
    for plane in range(2):
        row = 2 * plane + pc.core
        sent(down, d_sib.at[row], pc)
        def tail(t, z):
            i = row * n + t
            sent(qkv, q_sib.at[i], pc)
            sent(gu.at[0], g_sib.at[i], pc)
            for f in range(2): sent(o_any, o_sib.at[f, i], pc)
            return z
        lax.fori_loop(0, n, tail, 0)
    def tail2(t, z):
        src = lax.rem(c + t, n)
        sent(gu.at[0], g_far.at[src], pc)
        for f in range(2): sent(o_any, o_far.at[f, src], pc)
        @pl.when(t > 0)
        def _():
            sent(gu.at[0], g_send.at[src], pc)
        return z
    lax.fori_loop(0, n, tail2, 0)
    def tail3(t, z):
        for f, sign, _ in ways:
            src = pc.at(sign * t)
            sent(qkv, q_ring.at[f, src], pc)
            sent(o_any, o_ring.at[f, src], pc)
            sent(half_of(cot_v, f), c_ring.at[f, src], pc)
            sent(half_of(n2_v, f), n_ring.at[f, src], pc)
            sent(k_slot(c, f), k_ring.at[f, src], pc)
        return z
    lax.fori_loop(0, steps, tail3, 0)

def forward_call(n, length, x, og, qkv, outw, gu, down, tables):
    N = 4 * n
    owned, piece = gu.shape[2], down.shape[0]
    rows, width = x.shape
    S = jax.ShapeDtypeStruct
    shapes = [S((2, N * owned, gu.shape[3]), BF), S((4 * piece, width), BF), S((n, rows, width), BF),
              S((n, rows, width), BF), S((N,) + qkv.shape, BF), S((N,) + outw.shape, BF),
              S((n, rows, 2 * KVDIM), BF), S((HEADS, rows, HEAD), BF), S((rows, QDIM), BF), S((rows, width), F32)]
    anys = pl.BlockSpec(memory_space=pl.ANY)
    vmem = pl.BlockSpec(memory_space=pltpu.VMEM)
    V = pltpu.VMEM
    scratch = [V((N,) + qkv.shape, BF), V((N,) + outw.shape, BF), V((rows, width), BF), V((rows, width), BF),
               V((n, rows, 2 * KVDIM), BF), V((HEADS, rows, HEAD), BF), V((rows, QDIM), BF), V((rows, width), F32),
               V((rows, width), BF), V((2, rows, HEAD), F32),
               DMA((7,)), DMA((6,)), DMA((N,)), DMA((2, n)), DMA((N,)), DMA((1,)), DMA((2, N)), DMA((2, n)), DMA((2, n)), DMA((2, N)),
               DMA((N,)), DMA((n,)), DMA((n,)), DMA((N,)), DMA((4,)), DMA((1,)), DMA((4,)), DMA((2, n)), DMA((2, n)),
               DMA((2, n)), DMA((2, n)), DMA((2, n)), DMA((2, n))]
    return pl.pallas_call(
        functools.partial(forward_kernel, n),
        out_shape=shapes,
        in_specs=[pl.BlockSpec(memory_space=pltpu.SMEM), vmem, vmem] + [anys] * 5,
        out_specs=[anys] * len(shapes),
        scratch_shapes=scratch,
        compiler_params=pltpu.CompilerParams(collective_id=0, has_side_effects=True, vmem_limit_bytes=48 * 2**20),
    )(length, x, og, qkv, outw, gu, down, tables)


def ffn_kernel(n, gu_all, down_all, cot_all, n2_all, u_own, o_own, graw, ddown,
               gu_v, down_v, cot_v, n2_v, act_v, gg_v, gp_v, ub, ob, dgu_v, dd_v, r0g, r1g, r0d, r1d,
               load, rows_in, u_recv, u_send, o_recv, o_send, gs0, gr0, gs1, gr1, gs2, gr2, ds0, dr0, ds1, dr1):
    pc = Place(n)
    s, c = pc.s, pc.c
    _, rows, width = n2_all.shape
    chunk = gu_all.shape[2]
    half = rows // 2
    steps = n - 1
    ways = ((0, -1, pc.nxt), (1, 1, pc.prv))
    weights = [pltpu.make_async_copy(gu_all, gu_v, load.at[0]), pltpu.make_async_copy(down_all, down_v, load.at[1])]
    def fetch(t, z):
        for f, sign, _ in ways:
            q = pc.at(sign * (t + 1))
            part = pl.ds(f * half, half)
            pltpu.make_async_copy(n2_all.at[q, part, :], n2_v.at[t, part, :], rows_in.at[0, f, t]).start()
            pltpu.make_async_copy(cot_all.at[q, part, :], cot_v.at[t, part, :], rows_in.at[1, f, t]).start()
        return z
    lax.fori_loop(0, 1, fetch, 0)
    for w in weights: w.start()
    lax.fori_loop(1, n, fetch, 0)
    enter(pc)
    for w in weights: w.wait()
    tile = 384
    def slot(buf, f, i): return buf.at[f, i]
    def step(t, z):
        for f in range(2):
            part = pl.ds(f * half, half)
            pltpu.make_async_copy(n2_all.at[0, part, :], n2_v.at[t, part, :], rows_in.at[0, f, t]).wait()
            pltpu.make_async_copy(cot_all.at[0, part, :], cot_v.at[t, part, :], rows_in.at[1, f, t]).wait()
        def hidden(j, y):
            cols = pl.ds(pl.multiple_of(j * tile, tile), tile)
            gate = product(n2_v[t], gu_v[0, :, cols])
            up = product(n2_v[t], gu_v[1, :, cols])
            grad = contract_cols(cot_v[t], down_v[cols, :])
            sig = jax.nn.sigmoid(gate)
            gs = gate * sig
            act_v[t, :, cols] = (gs * up).astype(BF)
            gg_v[t, :, cols] = (grad * up * (sig + gs * (1.0 - sig))).astype(BF)
            gp_v[t, :, cols] = (grad * gs).astype(BF)
            return y
        lax.fori_loop(0, chunk // tile, hidden, 0)
        here = lax.rem(t + n - 1, n)
        @pl.when(t > 0)
        def _():
            for f in range(2): arrived(slot(ub, f, here), u_recv.at[f, here], pc)
        def wide(j, y):
            cols = pl.ds(pl.multiple_of(j * tile, tile), tile)
            u = contract_cols(gg_v[t], gu_v[0, cols, :]) + contract_cols(gp_v[t], gu_v[1, cols, :])
            o = product(act_v[t], down_v[:, cols])
            for f in range(2):
                mine = slice(f * half, (f + 1) * half)
                before = jnp.where(t > 0, ub[f, here, :, cols].astype(F32), 0.0)
                both = u[mine] + before
                ub[f, here, :, cols] = both.astype(BF)
                u_own[mine, cols] = both
                ob[f, t, :, cols] = o[mine].astype(BF)
            return y
        lax.fori_loop(0, width // tile, wide, 0)
        @pl.when(t < steps)
        def _():
            for f, _, to in ways:
                send(slot(ub, f, here), slot(ub, f, t), u_send.at[f, t], u_recv.at[f, t], s, to)
        return z
    lax.fori_loop(0, n, step, 0)

    all_rows = n * rows
    plane = gu_all.shape[1] // 4
    piece = down_all.shape[0] // 4
    owned = plane // n
    core, y = pc.core, s // 2
    def turn_o(t):
        for f, _, to in ways:
            if t == 0:
                send(ob.at[f, 0], ob.at[f, n], o_send.at[f, 0], o_recv.at[f, 0], s, to)
            else:
                here = n + t - 1
                arrived(ob.at[f, here], o_recv.at[f, t - 1], pc)
                ob[f, here] = (ob[f, here].astype(F32) + ob[f, t].astype(F32)).astype(BF)
                if t < steps:
                    send(ob.at[f, here], ob.at[f, n + t], o_send.at[f, t], o_recv.at[f, t], s, to)
                else:
                    o_own[f * half : (f + 1) * half, :] = ob[f, here].astype(F32)
    def cols_of(j): return pl.ds(j * tile, tile)
    wide_pieces = [(0, j, a) for j in range(chunk // tile) for a in range(2)]
    down_pieces = [(1, j, 0) for j in range(width // tile)]
    def compute(p):
        kind, j, a = p
        if kind == 0:
            lhs, rhs = n2_v[...].reshape(all_rows, width), (gg_v, gp_v)[a]
            grad = contract_rows(lhs, rhs[:, :, cols_of(j)].reshape(all_rows, tile))
            dgu_v[a, :, :, :, cols_of(j)] = grad.astype(BF).reshape(2, 2, plane, tile)
            send(dgu_v.at[a, :, 1 - core, :, cols_of(j)], r0g.at[a, :, :, cols_of(j)],
                 gs0.at[a, j], gr0.at[a, j], pc.sib, c)
        else:
            grad = contract_rows(act_v[...].reshape(all_rows, chunk), cot_v[:, :, cols_of(j)].reshape(all_rows, tile))
            dd_v[:, :, :, cols_of(j)] = grad.astype(BF).reshape(2, 2, piece, tile)
            send(dd_v.at[:, 1 - core, :, cols_of(j)], r0d.at[:, :, cols_of(j)], ds0.at[j], dr0.at[j], pc.sib, c)
    def add_core(p):
        kind, j, a = p
        cols = cols_of(j)
        if kind == 0:
            arrived(r0g.at[a, :, :, cols], gr0.at[a, j], pc)
            for k in range(2):
                r0g[a, k, :, cols] = (r0g[a, k, :, cols].astype(F32) + dgu_v[a, k, core, :, cols].astype(F32)).astype(BF)
            send(r0g.at[a, 1 - y, :, cols], r1g.at[a, :, cols], gs1.at[a, j], gr1.at[a, j], pc.far, c)
        else:
            arrived(r0d.at[:, :, cols], dr0.at[j], pc)
            for k in range(2):
                r0d[k, :, cols] = (r0d[k, :, cols].astype(F32) + dd_v[k, core, :, cols].astype(F32)).astype(BF)
            send(r0d.at[1 - y, :, cols], r1d.at[:, cols], ds1.at[j], dr1.at[j], pc.far, c)
    def add_far(p):
        kind, j, a = p
        cols = cols_of(j)
        if kind == 0:
            arrived(r1g.at[a, :, cols], gr1.at[a, j], pc)
            r1g[a, :, cols] = (r1g[a, :, cols].astype(F32) + r0g[a, y, :, cols].astype(F32)).astype(BF)
            def hand(d, z):
                to = lax.rem(c + d, n)
                src = r1g.at[a, pl.ds(pl.multiple_of(to * owned, owned), owned), cols]
                send(src, graw.at[c, a, :, cols], gs2.at[a, j, to], gr2.at[a, j, c], s, to)
                return z
            lax.fori_loop(1, n, hand, 0)
            mine = r1g.at[a, pl.ds(pl.multiple_of(c * owned, owned), owned), cols]
            pltpu.make_async_copy(mine, graw.at[c, a, :, cols], gs2.at[a, j, c]).start()
        else:
            arrived(r1d.at[:, cols], dr1.at[j], pc)
            ddown[:, cols] = r1d[:, cols].astype(F32) + r0d[y, :, cols].astype(F32)
    order = wide_pieces + down_pieces
    turn_o(0)
    for i, p in enumerate(order):
        compute(p)
        if i: add_core(order[i - 1])
        if i in (3, 7): turn_o(1 + i // 4)
    add_core(order[-1])
    for i, p in enumerate(order):
        add_far(p)
        if i < steps - 2: turn_o(3 + i)
    for kind, j, a in order:
        cols = cols_of(j)
        if kind == 0:
            sent(r0g.at[a, :, :, cols], gs0.at[a, j], pc)
            sent(r1g.at[a, :, cols], gs1.at[a, j], pc)
            block = graw.at[c, a, :, cols]
            def last(d, z):
                k = lax.rem(c + d, n)
                arrived(graw.at[k, a, :, cols], gr2.at[a, j, k], pc)
                sent(block, gs2.at[a, j, k], pc)
                return z
            lax.fori_loop(1, n, last, 0)
            pltpu.make_async_copy(r1g.at[a, pl.ds(0, owned), cols], block, gs2.at[a, j, c]).wait()
        else:
            sent(r0d.at[:, :, cols], ds0.at[j], pc)
            sent(r1d.at[:, cols], ds1.at[j], pc)
    def tail(t, z):
        for f in range(2):
            sent(ub.at[f, 0], u_send.at[f, t], pc)
            sent(ob.at[f, 0], o_send.at[f, t], pc)
        return z
    lax.fori_loop(0, steps, tail, 0)

def ffn_call(n, gu_all, down_all, cot_all, n2_all):
    S, V = jax.ShapeDtypeStruct, pltpu.VMEM
    _, rows, width = n2_all.shape
    chunk = gu_all.shape[2]
    half = rows // 2
    plane, piece = gu_all.shape[1] // 4, down_all.shape[0] // 4
    a, b = chunk // 384, width // 384
    anys = pl.BlockSpec(memory_space=pl.ANY)
    vmem = pl.BlockSpec(memory_space=pltpu.VMEM)
    return pl.pallas_call(
        functools.partial(ffn_kernel, n),
        out_shape=[S((rows, width), F32), S((rows, width), F32), S((n, 2, plane // n, chunk), BF), S((piece, width), F32)],
        in_specs=[anys] * 4,
        out_specs=[vmem, vmem, anys, vmem],
        scratch_shapes=[V(gu_all.shape, BF), V(down_all.shape, BF), V(cot_all.shape, BF), V(n2_all.shape, BF)]
        + [V((n, rows, chunk), BF)] * 3 + [V((2, n, half, width), BF), V((2, 2 * n, half, width), BF)]
        + [V((2, 2, 2, plane, chunk), BF), V((2, 2, piece, width), BF), V((2, 2, plane, chunk), BF), V((2, plane, chunk), BF),
           V((2, piece, width), BF), V((piece, width), BF)]
        + [DMA((2,)), DMA((2, 2, n)), DMA((2, n)), DMA((2, n)), DMA((2, n)), DMA((2, n))]
        + [DMA((2, a))] * 4 + [DMA((2, a, n))] * 2 + [DMA((b,))] * 4,
        compiler_params=pltpu.CompilerParams(collective_id=1, has_side_effects=True, vmem_limit_bytes=62 * 2**20),
    )(gu_all, down_all, cot_all, n2_all)


def add_low(left, right):
    return (left.astype(F32) + right.astype(F32)).astype(BF)

class Reduce:
    def __init__(self, pc, far_first, p, r0, r1, r2, r3, ss, rs, i):
        self.pc, self.far_first, self.p = pc, far_first, p
        self.r0, self.r1, self.r2, self.r3, self.ss, self.rs, self.i = r0, r1, r2, r3, ss, rs, i
        self.y, self.x, self.z = pc.s // 2, lax.rem(pc.c, 2), pc.c // 2
        self.xp = pc.c + 1 - 2 * self.x
    def go(self, k, src, dst, seq, ctx):
        send(src, dst, self.ss.at[self.i, k], self.rs.at[self.i, k], seq, ctx)
    def come(self, k, dst):
        arrived(dst, self.rs.at[self.i, k], self.pc)
    def stage0(self):
        pc = self.pc
        self.go(0, self.p.at[:, 1 - pc.core], self.r0, pc.sib, pc.c)
    def stage1(self):
        pc, r0 = self.pc, self.r0
        self.come(0, r0)
        r0[...] = add_low(r0[...], self.p[:, pc.core])
        if self.far_first: self.go(1, r0.at[1 - self.y], self.r1, pc.far, pc.c)
        else: self.go(1, r0.at[:, :, 1 - self.x], self.r1, pc.s, self.xp)
    def stage2(self):
        pc, r0, r1 = self.pc, self.r0, self.r1
        self.come(1, r1)
        if self.far_first:
            r1[...] = add_low(r1[...], r0[self.y])
            self.go(2, r1.at[:, 1 - self.x], self.r2, pc.s, self.xp)
        else:
            r1[...] = add_low(r1[...], r0[:, :, self.x])
            self.go(2, r1.at[1 - self.y], self.r2, pc.far, pc.c)
    def stage3(self):
        pc, r1, r2, n = self.pc, self.r1, self.r2, self.pc.n
        self.come(2, r2)
        r2[...] = add_low(r2[...], r1[:, self.x] if self.far_first else r1[self.y])
        def hand(d, w):
            to = lax.rem(self.z + d, n // 2)
            send(r2.at[to], self.r3.at[self.z], self.ss.at[self.i, 2 + d], self.rs.at[self.i, 2 + d], pc.s, 2 * to + self.x)
            return w
        lax.fori_loop(1, n // 2, hand, 0)
    def stage4(self):
        n = self.pc.n
        total = self.r2[self.z].astype(F32)
        for d in range(1, n // 2):
            src = lax.rem(self.z + n // 2 - d, n // 2)
            arrived(self.r3.at[src], self.rs.at[self.i, 2 + d], self.pc)
            total = total + self.r3[src].astype(F32)
        return total
    def finish(self):
        sent(self.r0, self.ss.at[self.i, 0], self.pc)
        sent(self.r1, self.ss.at[self.i, 1], self.pc)
        sent(self.r2, self.ss.at[self.i, 2], self.pc)
        for d in range(1, self.pc.n // 2):
            sent(self.r2.at[0], self.ss.at[self.i, 2 + d], self.pc)

def backward_kernel(n, length_ref, x_ref, og_ref, mid_ref, u_ref, o_ref, att_ref, q_ref, kv_ref, qkv_ref, out_ref, tables,
                    y_out, dx_out, dout_out, dqkv_out,
                    tab_v, gm_v, gb_v, dm_v, gp_v, p_v, gs_v, dkv_v, kx, kz, *rest):
    pieces = 6
    bufs, (local, kxs, kxr, kzs, kzr, ss, rs) = rest[: 5 * pieces], rest[5 * pieces :]
    pc = Place(n)
    s, c = pc.s, pc.c
    rows, width = x_ref.shape
    total = n * rows
    length = length_ref[0]
    x, z = lax.rem(c, 2), c // 2
    xp = c + 1 - 2 * x
    red = [Reduce(pc, i % 2 == 0, *bufs[5 * i : 5 * i + 5], ss, rs, i) for i in range(pieces)]
    tab = pltpu.make_async_copy(tables.at[:, pl.ds(pl.multiple_of(c * rows, rows), rows), :], tab_v, local.at[0])
    tab.start()
    enter(pc)
    pos = c * rows + lax.broadcasted_iota(jnp.int32, (rows, width), 0)
    live = pos < length
    mid = mid_ref[...]
    gm = jnp.where(live, og_ref[...].astype(F32), 0.0) + rms_back(mid, inverse_rms(mid), u_ref[...])
    gm_v[...] = gm
    gb_v[...] = gm.astype(BF)
    y_out[...] = jnp.where(live, mid + o_ref[...], 0.0).astype(BF)
    owned = out_ref.shape[1]
    owners = 4 * n
    def mix(j, w):
        weight = out_ref[pl.ds(j * 8, 8)].reshape(8 * owned, width)
        r = contract_cols(gb_v[...], weight).astype(BF)
        for k in range(8 * owned // HEAD):
            dm_v[j * (8 * owned // HEAD) + k] = r[:, k * HEAD : (k + 1) * HEAD]
        return w
    lax.fori_loop(0, owners // 8, mix, 0)
    gb = gb_v[...]
    for i in range(2):
        w = width // 2
        grad = contract_rows(att_ref[...], gb[:, i * w : (i + 1) * w])
        red[i].p[...] = grad.astype(BF).reshape(red[i].p.shape)
        red[i].stage0()
    tab.wait()
    tc, ts = tab_v[0], tab_v[1]

    at_row = c * rows + lax.broadcasted_iota(jnp.int32, (rows, total), 0)
    at_col = lax.broadcasted_iota(jnp.int32, (rows, total), 1)
    allowed = (at_col <= at_row) & (at_col < length)
    def group(g):
        key = kv_ref[:, :, g * HEAD : (g + 1) * HEAD].reshape(total, HEAD)
        val = kv_ref[:, :, KVDIM + g * HEAD : KVDIM + (g + 1) * HEAD].reshape(total, HEAD)
        def head(i, w):
            h = g * GROUP + i
            part = pl.ds(pl.multiple_of(i * rows, rows), rows)
            scores = jnp.where(allowed, contract_cols(q_ref[h], key) * SCALE, MASKED)
            e = jnp.exp(scores - jnp.max(scores, axis=1, keepdims=True))
            probs = e / jnp.sum(e, axis=1, keepdims=True)
            gprobs = contract_cols(dm_v[h], val)
            inner = jnp.sum(probs * gprobs, axis=1, keepdims=True)
            gs = (probs * (gprobs - inner)).astype(BF)
            p_v[part, :] = probs.astype(BF)
            gs_v[part, :] = gs
            dq = product(gs, key) * SCALE
            gp_v[:, pl.ds(pl.multiple_of(h * HEAD, HEAD), HEAD)] = (dq * tc - pltpu.roll(dq, HEAD // 2, 1) * ts).astype(BF)
            return w
        lax.fori_loop(0, GROUP, head, 0)
        mine = slice(g * GROUP, (g + 1) * GROUP)
        dk = contract_rows(gs_v[...], q_ref[mine].reshape(GROUP * rows, HEAD)) * SCALE
        dv = contract_rows(p_v[...], dm_v[mine].reshape(GROUP * rows, HEAD))
        lanes = slice(g * 2 * HEAD, g * 2 * HEAD + 2 * HEAD)
        dkv_v[:, :, :, lanes] = jnp.concatenate([dk, dv], 1).astype(BF).reshape(n // 2, 2, rows, 2 * HEAD)
        send(dkv_v.at[:, 1 - x, :, lanes], kx.at[:, :, lanes], kxs.at[g], kxr.at[g], s, xp)
    def kv_x(g):
        lanes = slice(g * 2 * HEAD, g * 2 * HEAD + 2 * HEAD)
        arrived(kx.at[:, :, lanes], kxr.at[g], pc)
        kx[:, :, lanes] = add_low(kx[:, :, lanes], dkv_v[:, x, :, lanes])
        for d in range(1, n // 2):
            to = lax.rem(z + d, n // 2)
            send(kx.at[to, :, lanes], kz.at[z, :, lanes], kzs.at[g, d], kzr.at[g, d], s, 2 * to + x)
    def kv_z(g):
        lanes = slice(g * 2 * HEAD, g * 2 * HEAD + 2 * HEAD)
        sumkv = kx[z, :, lanes].astype(F32)
        for d in range(1, n // 2):
            src = lax.rem(z + n // 2 - d, n // 2)
            arrived(kz.at[src, :, lanes], kzr.at[g, d], pc)
            sumkv = sumkv + kz[src, :, lanes].astype(F32)
        dk, dv = sumkv[:, :HEAD], sumkv[:, HEAD:]
        k0, v0 = QDIM + g * HEAD, QDIM + KVDIM + g * HEAD
        gp_v[:, k0 : k0 + HEAD] = (dk * tc - pltpu.roll(dk, HEAD // 2, 1) * ts).astype(BF)
        gp_v[:, v0 : v0 + HEAD] = dv.astype(BF)
    xin = x_ref[...].astype(F32)
    inverse = inverse_rms(xin)
    def joint(i, first, w):
        xh = (x_ref[...].astype(F32) * inverse).astype(BF)
        grad = contract_rows(xh, gp_v[:, first : first + w]).astype(BF)
        shape = red[i].p.shape[:-1] + (w,)
        red[i].p[..., :w] = grad.reshape(shape)
    group(0)
    red[0].stage1(); red[1].stage1()
    group(1)
    kv_x(0)
    red[0].stage2(); red[1].stage2()
    third = QDIM // 3
    for i in range(3):
        joint(2 + i, i * third, third)
        red[2 + i].stage0()
        if i == 0: kv_x(1)
    red[0].stage3(); red[1].stage3()
    red[2].stage1(); red[3].stage1(); red[4].stage1()
    kv_z(0); kv_z(1)
    joint(5, QDIM, 2 * KVDIM)
    sums = jnp.sum(gp_v[...].astype(F32), axis=0, keepdims=True)
    p5 = red[5].p
    qk_width = QDIM + KVDIM
    at = lax.broadcasted_iota(jnp.int32, (owned, HEAD), 0)
    for d in range(owners):
        tiles = (qk_width // owners * d // HEAD, qk_width // owners * d // HEAD + 1, (qk_width + KVDIM // owners * d) // HEAD)
        part = jnp.zeros((owned, HEAD), F32)
        for k, t in enumerate(tiles):
            part = jnp.where(at == k, sums[:, t * HEAD : t * HEAD + HEAD], part)
        plane = d // n
        p5[plane // 2, plane % 2, d % n // 2, d % 2, :, 2 * KVDIM :] = part.astype(BF)
    red[5].stage0()
    red[2].stage2(); red[3].stage2(); red[4].stage2()
    red[5].stage1()
    qk = QDIM + 2 * KVDIM
    gp = gp_v[...]
    def back(j, w):
        weight = qkv_ref[pl.ds(j * 8, 8), :, :qk].reshape(8 * owned, qk)
        cols = pl.ds(pl.multiple_of(j * 8 * owned, 8 * owned), 8 * owned)
        dx_out[:, cols] = contract_cols(gp, weight)
        return w
    lax.fori_loop(0, owners // 8, back, 0)
    red[2].stage3(); red[3].stage3(); red[4].stage3()
    red[5].stage2()
    dx_out[...] = gm_v[...] + rms_back(x_ref[...].astype(F32), inverse, dx_out[...])
    for i in range(2):
        dout_out[:, i * (width // 2) : (i + 1) * (width // 2)] = red[i].stage4()
    red[5].stage3()
    for i in range(3):
        dqkv_out[:, i * third : (i + 1) * third] = red[2 + i].stage4()
    dqkv_out[:, QDIM:] = red[5].stage4()
    for r in red: r.finish()
    for g in range(2):
        lanes = slice(g * 2 * HEAD, g * 2 * HEAD + 2 * HEAD)
        sent(kx.at[:, :, lanes], kxs.at[g], pc)
        for d in range(1, n // 2): sent(kx.at[0, :, lanes], kzs.at[g, d], pc)

def backward_call(n, length, x, og, mid, u, o, att, q, kv, qkv_all, out_all, tables):
    S, V = jax.ShapeDtypeStruct, pltpu.VMEM
    rows, width = x.shape
    owned = qkv_all.shape[1]
    anys = pl.BlockSpec(memory_space=pl.ANY)
    vmem = pl.BlockSpec(memory_space=pltpu.VMEM)
    m = n // 2
    scratch = [V((2, rows, HEAD), F32), V((rows, width), F32), V((rows, width), BF), V((HEADS, rows, HEAD), BF),
               V((rows, QDIM + 2 * KVDIM), BF), V((GROUP * rows, n * rows), BF), V((GROUP * rows, n * rows), BF),
               V((m, 2, rows, 2 * KVDIM), BF), V((m, rows, 2 * KVDIM), BF), V((m, rows, 2 * KVDIM), BF)]
    for i, w in enumerate((width // 2, width // 2, QDIM // 3, QDIM // 3, QDIM // 3, 2 * KVDIM + HEAD)):
        one = (m, 2, owned, w) if i % 2 == 0 else (2, m, owned, w)
        scratch += [V((2, 2, m, 2, owned, w), BF), V((2, m, 2, owned, w), BF), V(one, BF), V((m, owned, w), BF), V((m, owned, w), BF)]
    scratch += [DMA((1,)), DMA((2,)), DMA((2,)), DMA((2, m)), DMA((2, m)), DMA((6, 2 + m)), DMA((6, 2 + m))]
    return pl.pallas_call(
        functools.partial(backward_kernel, n),
        out_shape=[S((rows, width), BF), S((rows, width), F32), S((owned, width), F32), S((owned, qkv_all.shape[2]), F32)],
        in_specs=[pl.BlockSpec(memory_space=pltpu.SMEM)] + [vmem] * 10 + [anys],
        out_specs=[vmem] * 4,
        scratch_shapes=scratch,
        compiler_params=pltpu.CompilerParams(collective_id=2, has_side_effects=True, vmem_limit_bytes=62 * 2**20),
    )(length, x, og, mid, u, o, att, q, kv, qkv_all, out_all, tables)


def kernel_shards(
    tokens,
    lengths,
    attn_gain,
    qkv_weight,
    qkv_bias,
    out_weight,
    mlp_gain,
    gate_weight,
    up_weight,
    down_weight,
    out_grad,
):
    seqs, parts = lax.axis_size("seq"), lax.axis_size("ctx")
    rows, width = tokens.shape[1:]
    owned, hidden = gate_weight.shape
    piece = down_weight.shape[0]
    padded = -(-piece // 32) * 32
    owners = seqs * parts
    me = lax.axis_index("seq") * parts + lax.axis_index("ctx")
    gain_one = attn_gain.astype(F32)[:, None]
    gain_two = mlp_gain.astype(F32)[:, None]
    half = HEAD // 2
    frequency = np.float32(ROPE_BASE) ** (-np.arange(half, dtype=np.float32) * np.float32(2.0 / HEAD))
    angles = np.arange(rows * parts, dtype=np.float32)[:, None] * frequency.astype(np.float32)[None, :]
    cosine, sine = np.cos(angles), np.sin(angles)
    tables = jnp.asarray(np.stack([np.concatenate([cosine, cosine], 1), np.concatenate([-sine, sine], 1)]), F32)
    share = qkv_bias.shape[0]
    extra = jnp.zeros((owned, HEAD), BF)
    extra = lax.dynamic_update_slice(extra, qkv_bias[None], (0, lax.rem(me, HEAD // share) * share))
    joint = jnp.concatenate([(qkv_weight.astype(F32) * gain_one).astype(BF), extra], axis=1)

    def to_chunks(weight):
        scaled = (weight.astype(F32) * gain_two).astype(BF).reshape(owned, seqs, parts, piece)
        scaled = jnp.pad(scaled, ((0, 0), (0, 0), (0, 0), (0, padded - piece)))
        return scaled.transpose(2, 0, 1, 3).reshape(parts, owned, seqs * padded)

    both = jnp.stack([to_chunks(gate_weight), to_chunks(up_weight)], axis=1)
    down = jnp.pad(down_weight, ((0, padded - piece), (0, 0)))
    x, og = tokens[0], out_grad[0]
    gu_all, down_all, cot_all, n2_all, qkv_all, out_all, kv_all, q, att, mid = forward_call(
        parts, lengths, x, og, joint, out_weight, both, down, tables
    )
    u, o, raw, grad_down = ffn_call(parts, gu_all, down_all, cot_all, n2_all)
    output, grad_inputs, grad_out, raw_qkv = backward_call(
        parts, lengths, x, og, mid, u, o, att, q, kv_all, qkv_all, out_all, tables
    )
    raw = raw.reshape(parts, 2, owned, seqs, padded)[..., :piece].transpose(1, 2, 3, 0, 4)
    raw = raw.reshape(2, owned, hidden).astype(F32)
    grad_mlp_gain = jnp.sum(raw[0] * gate_weight.astype(F32) + raw[1] * up_weight.astype(F32), 1)
    qk = QDIM + 2 * KVDIM
    bias_rows, raw_qkv = raw_qkv[:3, qk:], raw_qkv[:, :qk]
    grad_attn_gain = jnp.sum(raw_qkv * qkv_weight.astype(F32), axis=1)
    per, per_value = (QDIM + KVDIM) // owners, KVDIM // owners
    grad_qk_bias = lax.dynamic_slice_in_dim(bias_rows[:2].reshape(2 * HEAD), lax.rem(per * me, HEAD), per)
    grad_value_bias = lax.dynamic_slice_in_dim(bias_rows[2], lax.rem(per_value * me, HEAD), per_value)
    return (
        output[None],
        grad_inputs.astype(BF)[None],
        grad_attn_gain,
        raw_qkv * gain_one,
        grad_qk_bias,
        grad_out,
        grad_mlp_gain,
        raw[0] * gain_two,
        raw[1] * gain_two,
        grad_down[:piece],
        grad_value_bias,
    )


def solution(mesh):
    seqs, parts = mesh.shape["seq"], mesh.shape["ctx"]
    tiled = seqs == 4 and parts == 8 and 1536 // (seqs * parts) % 16 == 0
    rows, vector = P(BOTH, None), P(BOTH)
    token = P("seq", "ctx", None)
    return jax.shard_map(
        kernel_shards if tiled else plain_shards,
        mesh=mesh,
        in_specs=(token, P("seq"), vector, rows, vector, rows, vector, rows, rows, rows, token),
        out_specs=(token, token, vector, rows, vector, rows, vector, rows, rows, rows, vector),
        check_vma=False,
    )
```

```python
import functools

import jax
import jax.numpy as jnp
import numpy as np
from jax import lax
from jax.experimental import pallas as pl
from jax.experimental.pallas import tpu as pltpu
from jax.sharding import PartitionSpec as P

HEADS = 12
KV_HEADS = 2
HEAD = 128
QDIM = 1536
KVDIM = 256
GROUP = HEADS // KV_HEADS

EPSILON = 1e-06
ROPE_BASE = 1000000.0
MASKED = -1e30
SCALE = HEAD ** (-0.5)
BF = jnp.bfloat16
F32 = jnp.float32
BOTH = ("seq", "ctx")


DMA = pltpu.SemaphoreType.DMA
MESH = pl.DeviceIdType.MESH


def product(left, right):
    return jnp.dot(left, right, preferred_element_type=F32)


def contract_rows(left, right):
    return lax.dot_general(left, right, (((0,), (0,)), ((), ())), preferred_element_type=F32)


def contract_cols(left, right):
    return lax.dot_general(left, right, (((1,), (1,)), ((), ())), preferred_element_type=F32)


def inverse_rms(values):
    return lax.rsqrt(jnp.mean(values * values, axis=-1, keepdims=True) + EPSILON)


def rms_back(values, inverse, scaled_grad):
    inner = jnp.mean(scaled_grad * values, axis=-1, keepdims=True)
    return inverse * scaled_grad - values * (inverse * inverse * inverse) * inner


def rope_tables(positions):
    half = HEAD // 2
    frequency = ROPE_BASE ** (-jnp.arange(half, dtype=F32) * 2.0 / HEAD)
    angles = positions.astype(F32)[:, None] * frequency[None, :]
    return jnp.cos(angles), jnp.sin(angles)


def rotate(values, cosine, sine):
    half = HEAD // 2
    first, second = values[..., :half], values[..., half:]
    cosine, sine = cosine[:, None, :], sine[:, None, :]
    return jnp.concatenate([first * cosine - second * sine, second * cosine + first * sine], -1)


def gather(values, axes):
    return lax.all_gather(values, axes, axis=0, tiled=True)


def scatter(values, axes):
    return lax.psum_scatter(values, axes, scatter_dimension=0, tiled=True)


def plain_shards(
    tokens,
    lengths,
    attn_gain,
    qkv_weight,
    qkv_bias,
    out_weight,
    mlp_gain,
    gate_weight,
    up_weight,
    down_weight,
    out_grad,
):
    seqs, parts = lax.axis_size("seq"), lax.axis_size("ctx")
    inputs = tokens[0].astype(F32)
    rows, width = inputs.shape
    owned, hidden = gate_weight.shape
    piece = down_weight.shape[0]
    chunk = hidden // parts
    length = lengths[0]
    positions = lax.axis_index("ctx") * rows + jnp.arange(rows, dtype=jnp.int32)
    living = (positions < length).astype(F32)[:, None]
    cosine, sine = rope_tables(positions)

    gain_one = attn_gain.astype(F32)[:, None]
    gain_two = mlp_gain.astype(F32)[:, None]
    qkv_all = gather((qkv_weight.astype(F32) * gain_one).astype(BF), BOTH)
    bias_all = gather(qkv_bias, BOTH).astype(F32)
    out_all = gather(out_weight, BOTH)

    def to_chunks(weight):
        scaled = (weight.astype(F32) * gain_two).astype(BF)
        return scaled.reshape(owned, seqs, parts, piece).transpose(2, 0, 1, 3)

    both = jnp.stack([to_chunks(gate_weight), to_chunks(up_weight)], axis=1)
    both = lax.all_to_all(both.reshape(parts, 2, owned, chunk), "ctx", 0, 0)
    both = lax.all_gather(both, "seq", axis=0)
    gate_chunk = both[:, :, 0].reshape(width, chunk)
    up_chunk = both[:, :, 1].reshape(width, chunk)
    down_chunk = gather(down_weight, "seq")
    cotangent = out_grad[0].astype(F32) * living
    cot_all = gather(cotangent.astype(BF), "ctx")

    inverse_one = inverse_rms(inputs)
    normed_one = (inputs * inverse_one).astype(BF)
    project = product(normed_one, qkv_all) + bias_all
    queries = rotate(project[:, :QDIM].reshape(rows, HEADS, HEAD), cosine, sine).astype(BF)
    own_keys = rotate(
        project[:, QDIM : QDIM + KVDIM].reshape(rows, KV_HEADS, HEAD), cosine, sine
    ).astype(BF)
    own_values = project[:, QDIM + KVDIM :].astype(BF).reshape(rows, KV_HEADS, HEAD)
    keys, values = gather(own_keys, "ctx"), gather(own_values, "ctx")
    key_pos = jnp.arange(rows * parts, dtype=jnp.int32)
    allowed = (key_pos[None, :] <= positions[:, None]) & (key_pos[None, :] < length)
    grouped = queries.reshape(rows, KV_HEADS, GROUP, HEAD)
    scores = jnp.einsum("qgha,kga->ghqk", grouped, keys, preferred_element_type=F32) * SCALE
    scores = jnp.where(allowed, scores, MASKED)
    largest = jnp.max(scores, axis=-1, keepdims=True)
    exponent = jnp.exp(scores - largest)
    summed = jnp.sum(exponent, axis=-1, keepdims=True)
    probs = exponent / summed
    probs_low = probs.astype(BF)
    attended = jnp.einsum("ghqk,kga->qgha", probs_low, values, preferred_element_type=F32)
    attended = attended.reshape(rows, QDIM).astype(BF)
    middle = inputs + product(attended, out_all)

    inverse_two = inverse_rms(middle)
    normed_two = gather((middle * inverse_two).astype(BF), "ctx")
    gate_pre = product(normed_two, gate_chunk)
    up_pre = product(normed_two, up_chunk)
    sig = jax.nn.sigmoid(gate_pre)
    activated = (gate_pre * sig * up_pre).astype(BF)
    grad_act = contract_cols(cot_all, down_chunk)
    grad_gate = (grad_act * up_pre * (sig + gate_pre * sig * (1.0 - sig))).astype(BF)
    grad_up = (grad_act * gate_pre * sig).astype(BF)
    scaled_two = contract_cols(grad_gate, gate_chunk) + contract_cols(grad_up, up_chunk)
    scaled_two = scatter(scaled_two.astype(BF), "ctx").astype(F32)
    branch = scatter(product(activated, down_chunk).astype(BF), "ctx").astype(F32)
    output = ((middle + branch) * living).astype(BF)
    grad_down = scatter(contract_rows(activated, cot_all).astype(BF), "seq").astype(F32)
    raw = jnp.stack([contract_rows(normed_two, grad_gate), contract_rows(normed_two, grad_up)], 1)
    raw = scatter(raw.astype(BF), "seq").reshape(parts, owned, 2, chunk)
    raw = lax.all_to_all(raw, "ctx", 0, 0).astype(F32)
    raw = raw.reshape(parts, owned, 2, seqs, piece).transpose(2, 1, 3, 0, 4)
    raw = raw.reshape(2, owned, hidden)
    grad_mlp_gain = jnp.sum(raw[0] * gate_weight.astype(F32) + raw[1] * up_weight.astype(F32), 1)

    grad_middle = cotangent + rms_back(middle, inverse_two, scaled_two)
    grad_branch = grad_middle.astype(BF)
    grad_out = scatter(contract_rows(attended, grad_branch).astype(BF), BOTH).astype(F32)
    grad_mixed = contract_cols(grad_branch, out_all).astype(BF)
    grad_mixed = grad_mixed.reshape(rows, KV_HEADS, GROUP, HEAD)
    grad_probs = jnp.einsum("qgha,kga->ghqk", grad_mixed, values, preferred_element_type=F32)
    inner = jnp.sum(probs * grad_probs, axis=-1, keepdims=True)
    grad_scores = (probs * (grad_probs - inner)).astype(BF)
    grad_q = jnp.einsum("ghqk,kga->qgha", grad_scores, keys, preferred_element_type=F32) * SCALE
    grad_k = jnp.einsum("ghqk,qgha->kga", grad_scores, grouped, preferred_element_type=F32) * SCALE
    grad_v = jnp.einsum("ghqk,qgha->kga", probs_low, grad_mixed, preferred_element_type=F32)
    grad_k = scatter(grad_k.astype(BF), "ctx").astype(F32)
    grad_v = scatter(grad_v.astype(BF), "ctx").astype(F32)
    grad_q = rotate(grad_q.reshape(rows, HEADS, HEAD), cosine, -sine).reshape(rows, QDIM)
    grad_k = rotate(grad_k, cosine, -sine).reshape(rows, KVDIM)
    grad_project = jnp.concatenate([grad_q, grad_k, grad_v.reshape(rows, KVDIM)], axis=1)
    grad_project = grad_project.astype(BF)
    raw_qkv = scatter(contract_rows(normed_one, grad_project).astype(BF), BOTH).astype(F32)
    grad_attn_gain = jnp.sum(raw_qkv * qkv_weight.astype(F32), axis=1)
    grad_bias = jnp.sum(grad_project.astype(F32), axis=0)
    qk_width = QDIM + KVDIM
    grad_qk_bias = scatter(grad_bias[:qk_width], BOTH)
    grad_value_bias = scatter(grad_bias[qk_width:], BOTH)
    scaled_one = contract_cols(grad_project, qkv_all)
    grad_inputs = (grad_middle + rms_back(inputs, inverse_one, scaled_one)).astype(BF)
    return (
        output[None],
        grad_inputs[None],
        grad_attn_gain,
        raw_qkv * gain_one,
        grad_qk_bias,
        grad_out,
        grad_mlp_gain,
        raw[0] * gain_two,
        raw[1] * gain_two,
        grad_down,
        grad_value_bias,
    )


class Place:
    def __init__(self, n):
        self.n = n
        self.s, self.c = lax.axis_index("seq"), lax.axis_index("ctx")
        self.me = self.s * n + self.c
        self.core = lax.rem(self.s, 2)
        self.sib = self.s + 1 - 2 * self.core
        self.far = lax.rem(self.s + 2, 4)
        half = self.c // 2
        self.pos = half + lax.rem(self.c, 2) * (n - 1 - 2 * half)
        self.nxt, self.prv = self.at(1), self.at(-1)
    def at(self, offset):
        p = lax.rem(self.pos + offset + 2 * self.n, self.n)
        return 2 * p + (p // (self.n // 2)) * (2 * self.n - 1 - 4 * p)

def send(src, dst, ssem, rsem, seq, ctx):
    copy = pltpu.make_async_remote_copy(src, dst, ssem, rsem, device_id=(seq, ctx), device_id_type=MESH)
    copy.start()

def arrived(dst, rsem, place):
    pltpu.make_async_remote_copy(dst, dst, rsem, rsem, device_id=(place.s, place.c), device_id_type=MESH).wait_recv()

def sent(src, ssem, place):
    pltpu.make_async_remote_copy(src, src, ssem, ssem, device_id=(place.s, place.c), device_id_type=MESH).wait_send()

def enter(place, whole_group=True):
    barrier = pltpu.get_barrier_semaphore()
    def greet(d, z):
        pl.semaphore_signal(barrier, inc=1, device_id=(place.s, lax.rem(place.c + d, place.n)), device_id_type=MESH)
        return z
    lax.fori_loop(1, place.n, greet, 0)
    pl.semaphore_signal(barrier, inc=1, device_id=(place.sib, place.c), device_id_type=MESH)
    pl.semaphore_signal(barrier, inc=1, device_id=(place.far, place.c), device_id_type=MESH)
    pl.semaphore_wait(barrier, place.n + 1)


def add_low(left, right):
    return (left.astype(F32) + right.astype(F32)).astype(BF)

class RingGather:
    def __init__(self, pc, slots, ssem, rsem, index=None):
        self.pc, self.slots, self.ssem, self.rsem, self.index = pc, slots, ssem, rsem, index
        self.steps, self.half = pc.n // 2, slots.shape[2] // 2
        self.ways = ((0, -1, pc.nxt), (1, 1, pc.prv))
    def slot(self, offset):
        return self.index[offset] if self.index else self.pc.at(offset)
    def part(self, ref, f, t):
        return ref if t < self.steps - 1 else ref.at[:, pl.ds(f * self.half, self.half)]
    def hop(self, t, own=None):
        for f, sign, to in self.ways:
            src = self.slots.at[self.slot(sign * t)] if own is None else own
            there = self.slots.at[self.slot(sign * (t + 1) if self.index else sign * t)]
            send(self.part(src, f, t), self.part(there, f, t), self.ssem.at[f, t], self.rsem.at[f, t], self.pc.s, to)
    def turn(self, t):
        for f, sign, _ in self.ways:
            arrived(self.part(self.slots.at[self.slot(sign * (t + 1))], f, t), self.rsem.at[f, t], self.pc)
        if t + 1 < self.steps: self.hop(t + 1)
    def finish(self):
        for f in range(2):
            for t in range(self.steps): sent(self.part(self.slots.at[0], f, t), self.ssem.at[f, t], self.pc)

class RingSum:
    def __init__(self, pc, term, index, held_half, held, ssem, rsem, out):
        self.pc, self.term, self.index, self.out = pc, term, index, out
        self.held_half, self.held, self.ssem, self.rsem = held_half, held, ssem, rsem
        self.steps, self.half = pc.n // 2, term.shape[2] // 2
    def turn(self, t):
        pc, ahead = self.pc, self.steps - t
        for f, sign, to in ((0, 1, pc.nxt), (1, -1, pc.prv)):
            cols = slice(f * self.half, (f + 1) * self.half)
            i = self.index[sign * ahead]
            if t == 1:
                arrived(self.held_half.at[f], self.rsem.at[f, 0], pc)
                self.term[i, :, cols] = add_low(self.term[i, :, cols], self.held_half[f])
            elif t > 1:
                arrived(self.held.at[f, t - 2], self.rsem.at[f, t - 1], pc)
                if t < self.steps: self.term[i] = add_low(self.term[i], self.held[f, t - 2])
            if t == 0:
                src, dst = self.term.at[i, :, pl.ds(f * self.half, self.half)], self.held_half.at[f]
            elif t < self.steps:
                src, dst = self.term.at[i], self.held.at[f, t - 1]
            if t < self.steps: send(src, dst, self.ssem.at[f, t], self.rsem.at[f, t], pc.s, to)
        if t == self.steps:
            i = self.index[0]
            self.out[...] = self.term[i].astype(F32) + self.held[0, t - 2].astype(F32) + self.held[1, t - 2].astype(F32)
    def finish(self):
        for f in range(2):
            sent(self.held_half.at[f], self.ssem.at[f, 0], self.pc)
            for t in range(1, self.steps): sent(self.held.at[f, 0], self.ssem.at[f, t], self.pc)

class Spread:
    def __init__(self, pc, x_first, w, ss, rs, i):
        self.pc, self.x_first, self.w, self.ss, self.rs, self.i = pc, x_first, w, ss, rs, i
        self.y, self.x, self.z = pc.s // 2, lax.rem(pc.c, 2), pc.c // 2
        self.xp = pc.c + 1 - 2 * self.x
        self.deep = pc.n // 2
    def go(self, k, part, seq, ctx):
        send(part, part, self.ss.at[self.i, k], self.rs.at[self.i, k], seq, ctx)
    def come(self, k, part):
        arrived(part, self.rs.at[self.i, k], self.pc)
    def both(self, k, part, sib_k, seq, ctx, sib_part):
        self.go(k, part, seq, ctx)
        self.go(sib_k, sib_part, self.pc.sib, self.pc.c)
    def begin(self):
        own = self.w.at[self.y, self.pc.core, self.z, self.x]
        for d in range(1, self.deep):
            self.go(d - 1, own, self.pc.s, 2 * lax.rem(self.z + d, self.deep) + self.x)
    def stage1(self):
        pc, w, y, x = self.pc, self.w, self.y, self.x
        for d in range(1, self.deep):
            self.come(d - 1, w.at[y, pc.core, lax.rem(self.z + self.deep - d, self.deep), x])
        column = w.at[y, pc.core, :, x]
        if self.x_first: self.both(self.deep, column, self.deep + 2, pc.s, self.xp, column)
        else: self.both(self.deep, column, self.deep + 2, pc.far, pc.c, column)
    def stage2(self):
        pc, w, y, x = self.pc, self.w, self.y, self.x
        if self.x_first:
            new = w.at[y, pc.core, :, 1 - x]
            self.come(self.deep, new)
            self.both(self.deep + 1, w.at[y, pc.core], self.deep + 3, pc.far, pc.c, new)
        else:
            new = w.at[1 - y, pc.core, :, x]
            self.come(self.deep, new)
            self.both(self.deep + 1, w.at[:, pc.core, :, x], self.deep + 3, pc.s, self.xp, new)
    def stage3(self):
        pc, w, y, x = self.pc, self.w, self.y, self.x
        new = w.at[1 - y, pc.core] if self.x_first else w.at[:, pc.core, :, 1 - x]
        self.come(self.deep + 1, new)
        self.go(self.deep + 4, new, pc.sib, pc.c)
    def stage4(self):
        pc, w, y, x = self.pc, self.w, self.y, self.x
        other = 1 - pc.core
        self.come(self.deep + 2, w.at[y, other, :, x])
        self.come(self.deep + 3, w.at[y, other, :, 1 - x] if self.x_first else w.at[1 - y, other, :, x])
        self.come(self.deep + 4, w.at[1 - y, other] if self.x_first else w.at[:, other, :, 1 - x])
    def finish(self):
        w, four = self.w, self.w.at[0, 0, :, 0]
        eight = w.at[0, 0] if self.x_first else w.at[:, 0, :, 0]
        for d in range(1, self.deep): sent(w.at[0, 0, 0, 0], self.ss.at[self.i, d - 1], self.pc)
        for k, part in enumerate((four, eight, four, four, eight)): sent(part, self.ss.at[self.i, self.deep + k], self.pc)

def windows(n, piece, padded):
    for part in range(n):
        for plane in range(4):
            whole, packed = (plane * n + part) * piece, plane * padded
            first, packed_first = whole // 128 * 128, packed // 128 * 128
            span = -(-(whole + piece) // 128) * 128 - first
            packed_span = -(-(packed + piece) // 128) * 128 - packed_first
            yield part, whole - first, packed - packed_first, first, span, packed_first, packed_span

def shift_lanes(block, span, shift):
    if block.shape[1] < span:
        block = jnp.concatenate([block, jnp.zeros((block.shape[0], span - block.shape[1]), block.dtype)], 1)
    shift = shift % block.shape[1]
    return pltpu.roll(block, shift, 1) if shift else block

def place_back(raw, a, out):
    n, _, owned, chunk = raw.shape
    piece, padded = out.shape[1] // (4 * n), chunk // 4
    for part, at, packed_at, first, span, packed_first, packed_span in windows(n, piece, padded):
        block = raw[part, a, :, packed_first : packed_first + packed_span].astype(F32)
        block = shift_lanes(block, span, at - packed_at)[:, :span]
        lane = lax.broadcasted_iota(jnp.int32, block.shape, 1)
        here = (lane >= at) & (lane < at + piece)
        out[:, first : first + span] = jnp.where(here, block, out[:, first : first + span])

def place_out(weight, gain, a, packs):
    n, _, owned, chunk = packs.shape
    piece, padded = weight.shape[1] // (4 * n), chunk // 4
    for part in range(n): packs[part, a] = jnp.zeros((owned, chunk), BF)
    for part, at, packed_at, first, span, packed_first, packed_span in windows(n, piece, padded):
        block = weight[:, first : first + span].astype(F32) * gain
        block = shift_lanes(block, packed_span, packed_at - at)[:, :packed_span]
        lane = lax.broadcasted_iota(jnp.int32, block.shape, 1)
        here = (lane >= packed_at) & (lane < packed_at + piece)
        before = packs[part, a, :, packed_first : packed_first + packed_span].astype(F32)
        packs[part, a, :, packed_first : packed_first + packed_span] = jnp.where(here, block, before).astype(BF)


def rope(values, table_c, table_s):
    return values * table_c + pltpu.roll(values, HEAD // 2, 1) * table_s

def forward_kernel(n, length_ref, x_ref, og_ref, qw_ref, g1_ref, b_ref, gate_ref, up_ref, g2_ref, down, outw, tables,
                   gu_all, down_all, cot_all, qkv_all, out_all, kv_all, q_out, att_out, mid_out, n2_out,
                   w_kv, w_q0, w_q1, w_q2, w_o0, w_o1, xh_v, cot_v, kv_v, q_v, tab_v, pack_v,
                   local, save, ss, rs, g_recv, g_send, g_far, g_sib, d_recv, d_far, d_sib, c_recv, c_send,
                   kz_s, kz_r, kx_s, kx_r):
    pc = Place(n)
    me, s, c = pc.me, pc.s, pc.c
    y, x, z, xp = s // 2, lax.rem(c, 2), c // 2, c + 1 - 2 * lax.rem(c, 2)
    rows, width = x_ref.shape
    owned, piece = qw_ref.shape[0], down.shape[0]
    length = length_ref[0]
    third, owners, deep = QDIM // 3, 4 * n, n // 2

    def g_slot(i): return gu_all.at[:, pl.ds(pl.multiple_of(i * owned, owned), owned), :]
    def d_slot(i): return down_all.at[pl.ds(pl.multiple_of(i * piece, piece), piece), :]

    spreads = [Spread(pc, i % 2 == 0, w, ss, rs, i) for i, w in enumerate((w_kv, w_q0, w_q1, w_q2, w_o0, w_o1))]
    kvs, q0, q1, q2, o0, o1 = spreads
    cring = RingGather(pc, cot_all, c_send, c_recv)
    ohalf = width // 2
    lc = [pltpu.make_async_copy(a, b, local.at[i]) for i, (a, b) in enumerate((
        (outw.at[:, pl.ds(0, ohalf)], w_o0.at[y, pc.core, z, x]), (outw.at[:, pl.ds(ohalf, ohalf)], w_o1.at[y, pc.core, z, x]),
        (down, d_slot(s)), (tables.at[:, pl.ds(pl.multiple_of(c * rows, rows), rows), :], tab_v)))]
    for copy in lc: copy.start()
    g1 = g1_ref[...]
    def scaled(first, w): return (qw_ref[:, first : first + w].astype(F32) * g1).astype(BF)
    w_kv[y, pc.core, z, x, :, : 2 * KVDIM] = scaled(QDIM, 2 * KVDIM)
    share = b_ref.shape[1]
    bias = b_ref[...].astype(F32)
    rest = jnp.zeros((1, HEAD - share), F32)
    odd = lax.rem(me, 2) == 1
    row = jnp.where(odd, jnp.concatenate([rest, bias], 1), jnp.concatenate([bias, rest], 1))
    first_row = lax.broadcasted_iota(jnp.int32, (owned, HEAD), 0) == 0
    w_kv[y, pc.core, z, x, :, 2 * KVDIM :] = jnp.where(first_row, row, 0.0).astype(BF)
    for i, w in enumerate((w_q0, w_q1, w_q2)): w[y, pc.core, z, x] = scaled(i * third, third)
    slot_pos = c * rows + lax.broadcasted_iota(jnp.int32, (rows, width), 0)
    cot_v[...] = jnp.where(slot_pos < length, og_ref[...].astype(F32), 0.0).astype(BF)
    enter(pc)
    def gu_turn(t):
        k = s * n + lax.rem(c + n - t, n)
        arrived(g_slot(k), g_recv.at[k], pc)
        send(g_slot(k), g_slot(k), g_far.at[lax.rem(c + n - t, n)], g_recv.at[k], pc.far, c)
        send(g_slot(k), g_slot(k), g_sib.at[k], g_recv.at[k], pc.sib, c)
    for p in (kvs, q0, q1, q2): p.begin()
    send(down, d_slot(s), d_far.at[0], d_recv.at[s], pc.far, c)
    send(down, d_slot(s), d_sib.at[s], d_recv.at[s], pc.sib, c)
    own_cot = pltpu.make_async_copy(cot_v, cot_all.at[c], local.at[4])
    own_cot.start()
    xf = x_ref[...].astype(F32)
    xh_v[...] = (xf * inverse_rms(xf)).astype(BF)
    g2 = g2_ref[...]
    place_out(gate_ref, g2, 0, pack_v)
    kvs.stage1()
    q0.stage1()
    place_out(up_ref, g2, 1, pack_v)
    q1.stage1()
    kvs.stage2()
    own_gu = pltpu.make_async_copy(pack_v.at[c], g_slot(me), local.at[5])
    own_gu.start()
    def feed(d, v):
        to = lax.rem(c + d, n)
        send(pack_v.at[to], g_slot(me), g_send.at[to], g_recv.at[me], s, to)
        return v
    q2.stage1()
    lax.fori_loop(1, n, feed, 0)
    q0.stage2()
    kvs.stage3()
    q1.stage2()
    lc[0].wait(); lc[1].wait()
    o0.begin(); o1.begin()
    q2.stage2()
    q0.stage3()
    q1.stage3()
    q2.stage3()
    send(pack_v.at[c], g_slot(me), g_far.at[c], g_recv.at[me], pc.far, c)
    send(pack_v.at[c], g_slot(me), g_sib.at[me], g_recv.at[me], pc.sib, c)
    kvs.stage4()
    lc[3].wait()
    tc, ts = tab_v[0], tab_v[1]
    xh = xh_v[...]
    def bias_of(tile):
        d = 2 * tile
        def part(i):
            plane, place = i // n, i % n
            return w_kv[plane // 2, plane % 2, place // 2, place % 2, 0:1, 2 * KVDIM :].astype(F32)
        return part(d) + part(d + 1)
    kv = product(xh, w_kv[..., : 2 * KVDIM].reshape(owners * owned, 2 * KVDIM))
    for k in range(2 * KV_HEADS):
        lanes = slice(k * HEAD, (k + 1) * HEAD)
        one = kv[:, lanes] + bias_of(QDIM // HEAD + k)
        kv_v[z, x, :, lanes] = (rope(one, tc, ts) if k < KV_HEADS else one).astype(BF)
    own_kv = kv_v.at[z, x]
    for d in range(1, deep):
        send(own_kv, own_kv, kz_s.at[d], kz_r.at[d], s, 2 * lax.rem(z + d, deep) + x)
    send(own_kv, own_kv, kx_s.at[0], kx_r.at[0], s, xp)
    o0.stage1(); o1.stage1()
    for i, p in enumerate((q0, q1, q2)):
        p.stage4()
        r = product(xh, p.w[...].reshape(owners * owned, third))
        for k in range(third // HEAD):
            h = i * (third // HEAD) + k
            q_v[h] = rope(r[:, k * HEAD : (k + 1) * HEAD] + bias_of(h), tc, ts).astype(BF)
    for d in range(1, deep):
        block = kv_v.at[lax.rem(z + deep - d, deep), x]
        arrived(block, kz_r.at[d], pc)
        send(block, block, kx_s.at[d], kx_r.at[d], s, xp)
    cring.hop(0, cot_v)
    o0.stage2(); o1.stage2()
    saves = [pltpu.make_async_copy(q_v, q_out, save.at[0])]
    for i, (p, first) in enumerate(((kvs, QDIM), (q0, 0), (q1, third), (q2, 2 * third))):
        saves.append(pltpu.make_async_copy(p.w, qkv_all.at[:, :, :, :, :, pl.ds(first, p.w.shape[5])], save.at[1 + i]))
    for copy in saves: copy.start()
    for d in range(deep):
        arrived(kv_v.at[lax.rem(z + deep - d, deep), 1 - x], kx_r.at[d], pc)

    total = n * rows
    at_row = c * rows + lax.broadcasted_iota(jnp.int32, (rows, total), 0)
    at_col = lax.broadcasted_iota(jnp.int32, (rows, total), 1)
    allowed = (at_col <= at_row) & (at_col < length)
    def heads(first, count):
        def head(h, v):
            col = pl.multiple_of(h // GROUP * HEAD, HEAD)
            key = kv_v[:, :, :, pl.ds(col, HEAD)].reshape(total, HEAD)
            val = kv_v[:, :, :, pl.ds(pl.multiple_of(KVDIM + col, HEAD), HEAD)].reshape(total, HEAD)
            scores = jnp.where(allowed, contract_cols(q_v[h], key) * SCALE, MASKED)
            e = jnp.exp(scores - jnp.max(scores, axis=1, keepdims=True))
            probs = (e / jnp.sum(e, axis=1, keepdims=True)).astype(BF)
            att_out[:, pl.ds(pl.multiple_of(h * HEAD, HEAD), HEAD)] = product(probs, val).astype(BF)
            return v
        lax.fori_loop(first, first + count, head, 0)
    gu_turn(1); gu_turn(2)
    o0.stage3(); o1.stage3()
    heads(0, GROUP)
    gu_turn(3); gu_turn(4)
    cring.turn(0)
    heads(GROUP, GROUP)
    gu_turn(5); gu_turn(6); gu_turn(7)
    o0.stage4(); o1.stage4()
    saves2 = [pltpu.make_async_copy(kv_v, kv_all, save.at[5])]
    for i, p in enumerate((o0, o1)):
        saves2.append(pltpu.make_async_copy(p.w, out_all.at[:, :, :, :, :, pl.ds(i * ohalf, ohalf)], save.at[6 + i]))
    for copy in saves2: copy.start()
    cring.turn(1)
    att = att_out[...]
    for i, p in enumerate((o0, o1)):
        lanes = slice(i * ohalf, (i + 1) * ohalf)
        mid_out[:, lanes] = x_ref[:, lanes].astype(F32) + product(att, p.w[...].reshape(owners * owned, ohalf))
    mid = mid_out[...]
    n2_out[...] = (mid * inverse_rms(mid)).astype(BF)
    cring.turn(2)
    arrived(d_slot(pc.far), d_recv.at[pc.far], pc)
    send(d_slot(pc.far), d_slot(pc.far), d_sib.at[pc.far], d_recv.at[pc.far], pc.sib, c)
    def across(t, v):
        k = pc.far * n + lax.rem(c + n - t, n)
        arrived(g_slot(k), g_recv.at[k], pc)
        send(g_slot(k), g_slot(k), g_sib.at[k], g_recv.at[k], pc.sib, c)
        return v
    lax.fori_loop(0, n, across, 0)
    cring.turn(3)
    for plane in range(2):
        other = 2 * plane + 1 - pc.core
        arrived(d_slot(other), d_recv.at[other], pc)
        def come(t, v):
            i = other * n + t
            arrived(g_slot(i), g_recv.at[i], pc)
            return v
        lax.fori_loop(0, n, come, 0)
    for copy in [lc[2], own_cot, own_gu] + saves + saves2: copy.wait()
    for p in spreads: p.finish()
    cring.finish()
    for d in range(1, deep): sent(own_kv, kz_s.at[d], pc)
    for d in range(deep): sent(own_kv, kx_s.at[d], pc)
    sent(down, d_far.at[0], pc)
    block = pack_v.at[0]
    for plane in range(2):
        own = 2 * plane + pc.core
        sent(down, d_sib.at[own], pc)
        def tail(t, v):
            sent(block, g_sib.at[own * n + t], pc)
            return v
        lax.fori_loop(0, n, tail, 0)
    def tail2(t, v):
        src = lax.rem(c + t, n)
        sent(block, g_far.at[src], pc)
        @pl.when(t > 0)
        def _():
            sent(block, g_send.at[src], pc)
        return v
    lax.fori_loop(0, n, tail2, 0)

def forward_call(n, length, x, og, qkv, gain_one, bias, gate, up, gain_two, outw, down, tables):
    N, m = 4 * n, n // 2
    rows, width = x.shape
    owned, piece = qkv.shape[0], down.shape[0]
    chunk = 4 * piece
    S, V = jax.ShapeDtypeStruct, pltpu.VMEM
    joint = QDIM + 2 * KVDIM + HEAD
    shapes = [S((2, N * owned, chunk), BF), S((4 * piece, width), BF), S((n, rows, width), BF),
              S((2, 2, m, 2, owned, joint), BF), S((2, 2, m, 2, owned, width), BF), S((m, 2, rows, 2 * KVDIM), BF),
              S((HEADS, rows, HEAD), BF), S((rows, QDIM), BF), S((rows, width), F32), S((rows, width), BF)]
    anys = pl.BlockSpec(memory_space=pl.ANY)
    vmem = pl.BlockSpec(memory_space=pltpu.VMEM)
    scratch = [V((2, 2, m, 2, owned, w), BF) for w in (2 * KVDIM + HEAD,) + (QDIM // 3,) * 3 + (width // 2,) * 2]
    scratch += [V((rows, width), BF), V((rows, width), BF), V((m, 2, rows, 2 * KVDIM), BF), V((HEADS, rows, HEAD), BF),
                V((2, rows, HEAD), F32), V((n, 2, owned, chunk), BF),
                DMA((6,)), DMA((8,)), DMA((6, m + 5)), DMA((6, m + 5)), DMA((N,)), DMA((n,)), DMA((n,)), DMA((N,)),
                DMA((4,)), DMA((1,)), DMA((4,)), DMA((2, m)), DMA((2, m)), DMA((m,)), DMA((m,)), DMA((m,)), DMA((m,))]
    return pl.pallas_call(
        functools.partial(forward_kernel, n),
        out_shape=shapes,
        in_specs=[pl.BlockSpec(memory_space=pltpu.SMEM)] + [vmem] * 9 + [anys] * 2,
        out_specs=[anys] * 7 + [vmem] * 3,
        scratch_shapes=scratch,
        compiler_params=pltpu.CompilerParams(collective_id=0, has_side_effects=True, vmem_limit_bytes=56 * 2**20),
    )(length, x, og, qkv, gain_one, bias, gate, up, gain_two, down, outw, tables)


def ffn_kernel(n, n2_ref, gu_all, down_all, cot_all, u_own, o_own, gsum, ddown,
               gu_v, down_v, cot_v, n2_v, act_v, gg_v, gp_v, ut, uhh, uh, ot, ohh, oh, dgu_v, dd_v, r0g, r1g, r0d, r1d,
               load, rows_in, n_recv, n_send, u_recv, u_send, o_recv, o_send, gs0, gr0, gs1, gr1, save, ds0, dr0, ds1, dr1):
    pc = Place(n)
    s, c = pc.s, pc.c
    _, rows, width = cot_all.shape
    chunk = gu_all.shape[2]
    pairs = n // 2
    weights = [pltpu.make_async_copy(gu_all, gu_v, load.at[0]), pltpu.make_async_copy(down_all, down_v, load.at[1])]
    offsets = [o for j in range(1, pairs) for o in (-j, j)] + [pairs, 0]
    index = {o: i for i, o in enumerate(offsets)}
    index[-pairs] = index[pairs]
    fetch = [pltpu.make_async_copy(cot_all.at[pc.at(o)], cot_v.at[i], rows_in.at[i]) for i, o in enumerate(offsets)]
    for w in weights: w.start()
    for f in fetch: f.start()
    n2_v[index[0]] = n2_ref[...]
    nring = RingGather(pc, n2_v, n_send, n_recv, index)
    uring = RingSum(pc, ut, index, uhh, uh, u_send, u_recv, u_own)
    oring = RingSum(pc, ot, index, ohh, oh, o_send, o_recv, o_own)
    enter(pc)
    nring.hop(0)
    for w in weights: w.wait()
    tall = 2 * rows
    def forward(j):
        pair = slice(2 * j, 2 * j + 2)
        normed = n2_v[pair].reshape(tall, width)
        gate = product(normed, gu_v[0])
        up = product(normed, gu_v[1])
        sig = jax.nn.sigmoid(gate)
        gs = gate * sig
        act = (gs * up).astype(BF)
        act_v[pair] = act.reshape(2, rows, chunk)
        gp_v[pair] = gs.astype(BF).reshape(2, rows, chunk)
        gg_v[pair] = (up * (sig + gs * (1.0 - sig))).astype(BF).reshape(2, rows, chunk)
        ot[pair] = product(act, down_v[...]).astype(BF).reshape(2, rows, width)
    def backward(j):
        pair = slice(2 * j, 2 * j + 2)
        grad = contract_cols(cot_v[pair].reshape(tall, width), down_v[...])
        gg = (grad * gg_v[pair].reshape(tall, chunk).astype(F32)).astype(BF)
        gp = (grad * gp_v[pair].reshape(tall, chunk).astype(F32)).astype(BF)
        gg_v[pair] = gg.reshape(2, rows, chunk)
        gp_v[pair] = gp.reshape(2, rows, chunk)
        ut[pair] = (contract_cols(gg, gu_v[0]) + contract_cols(gp, gu_v[1])).astype(BF).reshape(2, rows, width)

    all_rows = n * rows
    plane = gu_all.shape[1] // 4
    piece = down_all.shape[0] // 4
    core, y = pc.core, s // 2
    tile = 384
    def cols_of(j): return pl.ds(j * tile, tile)
    wide_pieces = [(0, j, a) for j in range(chunk // tile) for a in range(2)]
    down_pieces = [(1, j, 0) for j in range(width // tile)]
    def compute(p):
        kind, j, a = p
        if kind == 0:
            lhs, rhs = n2_v[...].reshape(all_rows, width), (gg_v, gp_v)[a]
            grad = contract_rows(lhs, rhs[:, :, cols_of(j)].reshape(all_rows, tile))
            dgu_v[a, :, :, :, cols_of(j)] = grad.astype(BF).reshape(2, 2, plane, tile)
            send(dgu_v.at[a, :, 1 - core, :, cols_of(j)], r0g.at[a, :, :, cols_of(j)],
                 gs0.at[a, j], gr0.at[a, j], pc.sib, c)
        else:
            grad = contract_rows(act_v[...].reshape(all_rows, chunk), cot_v[:, :, cols_of(j)].reshape(all_rows, tile))
            dd_v[:, :, :, cols_of(j)] = grad.astype(BF).reshape(2, 2, piece, tile)
            send(dd_v.at[:, 1 - core, :, cols_of(j)], r0d.at[:, :, cols_of(j)], ds0.at[j], dr0.at[j], pc.sib, c)
    def add_core(p):
        kind, j, a = p
        cols = cols_of(j)
        if kind == 0:
            arrived(r0g.at[a, :, :, cols], gr0.at[a, j], pc)
            for k in range(2):
                r0g[a, k, :, cols] = add_low(r0g[a, k, :, cols], dgu_v[a, k, core, :, cols])
            send(r0g.at[a, 1 - y, :, cols], r1g.at[a, :, cols], gs1.at[a, j], gr1.at[a, j], pc.far, c)
        else:
            arrived(r0d.at[:, :, cols], dr0.at[j], pc)
            for k in range(2):
                r0d[k, :, cols] = add_low(r0d[k, :, cols], dd_v[k, core, :, cols])
            send(r0d.at[1 - y, :, cols], r1d.at[:, cols], ds1.at[j], dr1.at[j], pc.far, c)
    saves = []
    def add_far(p):
        kind, j, a = p
        cols = cols_of(j)
        if kind == 0:
            arrived(r1g.at[a, :, cols], gr1.at[a, j], pc)
            r1g[a, :, cols] = add_low(r1g[a, :, cols], r0g[a, y, :, cols])
            copy = pltpu.make_async_copy(r1g.at[a, :, cols], gsum.at[a, :, cols], save.at[a, j])
            copy.start()
            saves.append(copy)
        else:
            arrived(r1d.at[:, cols], dr1.at[j], pc)
            ddown[:, cols] = r1d[:, cols].astype(F32) + r0d[y, :, cols].astype(F32)
    for j in range(pairs):
        nring.turn(j)
        forward(j)
    for f in fetch: f.wait()
    backward(3)
    uring.turn(0)
    oring.turn(0)
    compute(down_pieces[0])
    compute(down_pieces[1])
    add_core(down_pieces[0])
    backward(2)
    uring.turn(1)
    add_core(down_pieces[1])
    compute(down_pieces[2])
    backward(1)
    uring.turn(2)
    add_core(down_pieces[2])
    compute(down_pieces[3])
    backward(0)
    uring.turn(3)
    add_core(down_pieces[3])
    oring.turn(1)
    for i, p in enumerate(wide_pieces):
        compute(p)
        if i: add_core(wide_pieces[i - 1])
    add_core(wide_pieces[-1])
    uring.turn(4)
    oring.turn(2)
    for p in down_pieces: add_far(p)
    for i, p in enumerate(wide_pieces):
        add_far(p)
        if i == 1: oring.turn(3)
    oring.turn(4)
    for kind, j, a in wide_pieces + down_pieces:
        cols = cols_of(j)
        if kind == 0:
            sent(r0g.at[a, :, :, cols], gs0.at[a, j], pc)
            sent(r1g.at[a, :, cols], gs1.at[a, j], pc)
        else:
            sent(r0d.at[:, :, cols], ds0.at[j], pc)
            sent(r1d.at[:, cols], ds1.at[j], pc)
    for copy in saves: copy.wait()
    nring.finish()
    uring.finish()
    oring.finish()

def ffn_call(n, n2, gu_all, down_all, cot_all):
    S, V = jax.ShapeDtypeStruct, pltpu.VMEM
    _, rows, width = cot_all.shape
    chunk = gu_all.shape[2]
    plane, piece = gu_all.shape[1] // 4, down_all.shape[0] // 4
    a, b = chunk // 384, width // 384
    anys = pl.BlockSpec(memory_space=pl.ANY)
    vmem = pl.BlockSpec(memory_space=pltpu.VMEM)
    held = [V((2, rows, width // 2), BF), V((2, n // 2 - 1, rows, width), BF)]
    return pl.pallas_call(
        functools.partial(ffn_kernel, n),
        out_shape=[S((rows, width), F32), S((rows, width), F32), S((2, plane, chunk), BF), S((piece, width), F32)],
        in_specs=[vmem] + [anys] * 3,
        out_specs=[vmem, vmem, anys, vmem],
        scratch_shapes=[V(gu_all.shape, BF), V(down_all.shape, BF), V(cot_all.shape, BF), V(cot_all.shape, BF)]
        + [V((n, rows, chunk), BF)] * 3 + [V((n, rows, width), BF)] + held + [V((n, rows, width), BF)] + held
        + [V((2, 2, 2, plane, chunk), BF), V((2, 2, piece, width), BF), V((2, 2, plane, chunk), BF), V((2, plane, chunk), BF),
           V((2, piece, width), BF), V((piece, width), BF)]
        + [DMA((2,)), DMA((n,))] + [DMA((2, n // 2))] * 6
        + [DMA((2, a))] * 5 + [DMA((b,))] * 4,
        compiler_params=pltpu.CompilerParams(collective_id=1, has_side_effects=True, vmem_limit_bytes=63 * 2**20),
    )(n2, gu_all, down_all, cot_all)


class Reduce:
    def __init__(self, pc, far_first, p, r0, r1, r2, r3, ss, rs, i):
        self.pc, self.far_first, self.p = pc, far_first, p
        self.r0, self.r1, self.r2, self.r3, self.ss, self.rs, self.i = r0, r1, r2, r3, ss, rs, i
        self.y, self.x, self.z = pc.s // 2, lax.rem(pc.c, 2), pc.c // 2
        self.xp = pc.c + 1 - 2 * self.x
    def go(self, k, src, dst, seq, ctx):
        send(src, dst, self.ss.at[self.i, k], self.rs.at[self.i, k], seq, ctx)
    def come(self, k, dst):
        arrived(dst, self.rs.at[self.i, k], self.pc)
    def stage0(self):
        pc = self.pc
        self.go(0, self.p.at[:, 1 - pc.core], self.r0, pc.sib, pc.c)
    def stage1(self):
        pc, r0 = self.pc, self.r0
        self.come(0, r0)
        r0[...] = add_low(r0[...], self.p[:, pc.core])
        if self.far_first: self.go(1, r0.at[1 - self.y], self.r1, pc.far, pc.c)
        else: self.go(1, r0.at[:, :, 1 - self.x], self.r1, pc.s, self.xp)
    def stage2(self):
        pc, r0, r1 = self.pc, self.r0, self.r1
        self.come(1, r1)
        if self.far_first:
            r1[...] = add_low(r1[...], r0[self.y])
            self.go(2, r1.at[:, 1 - self.x], self.r2, pc.s, self.xp)
        else:
            r1[...] = add_low(r1[...], r0[:, :, self.x])
            self.go(2, r1.at[1 - self.y], self.r2, pc.far, pc.c)
    def stage3(self):
        pc, r1, r2, n = self.pc, self.r1, self.r2, self.pc.n
        self.come(2, r2)
        r2[...] = add_low(r2[...], r1[:, self.x] if self.far_first else r1[self.y])
        def hand(d, w):
            to = lax.rem(self.z + d, n // 2)
            send(r2.at[to], self.r3.at[self.z], self.ss.at[self.i, 2 + d], self.rs.at[self.i, 2 + d], pc.s, 2 * to + self.x)
            return w
        lax.fori_loop(1, n // 2, hand, 0)
    def stage4(self):
        n = self.pc.n
        total = self.r2[self.z].astype(F32)
        for d in range(1, n // 2):
            src = lax.rem(self.z + n // 2 - d, n // 2)
            arrived(self.r3.at[src], self.rs.at[self.i, 2 + d], self.pc)
            total = total + self.r3[src].astype(F32)
        return total
    def finish(self):
        sent(self.r0, self.ss.at[self.i, 0], self.pc)
        sent(self.r1, self.ss.at[self.i, 1], self.pc)
        sent(self.r2, self.ss.at[self.i, 2], self.pc)
        for d in range(1, self.pc.n // 2):
            sent(self.r2.at[0], self.ss.at[self.i, 2 + d], self.pc)

def backward_kernel(n, length_ref, x_ref, og_ref, mid_ref, u_ref, o_ref, att_ref, q_ref, kv_ref, qkv_ref, out_ref, gate_ref, up_ref, gain_ref, tables, gsum,
                    y_out, dx_out, dout_out, dqkv_out, dgate_out, dup_out, dgain_out,
                    tab_v, gm_v, gb_v, dm_v, gp_v, p_v, gs_v, dkv_v, kx, kz, raw_v, *rest):
    pieces = 6
    bufs, (local, kxs, kxr, kzs, kzr, gss, grs, ss, rs) = rest[: 5 * pieces], rest[5 * pieces :]
    pc = Place(n)
    s, c = pc.s, pc.c
    rows, width = x_ref.shape
    total = n * rows
    length = length_ref[0]
    x, z = lax.rem(c, 2), c // 2
    xp = c + 1 - 2 * x
    red = [Reduce(pc, i % 2 == 0, *bufs[5 * i : 5 * i + 5], ss, rs, i) for i in range(pieces)]
    tab = pltpu.make_async_copy(tables.at[:, pl.ds(pl.multiple_of(c * rows, rows), rows), :], tab_v, local.at[0])
    tab.start()
    enter(pc)
    owned = out_ref.shape[1]
    def g_rows(i): return gsum.at[:, pl.ds(pl.multiple_of(i * owned, owned), owned), :]
    own_raw = pltpu.make_async_copy(g_rows(c), raw_v.at[c], local.at[1])
    own_raw.start()
    def feed(d, w):
        to = lax.rem(c + d, n)
        send(g_rows(to), raw_v.at[c], gss.at[to], grs.at[c], s, to)
        return w
    pos = c * rows + lax.broadcasted_iota(jnp.int32, (rows, width), 0)
    live = pos < length
    mid = mid_ref[...]
    gm = jnp.where(live, og_ref[...].astype(F32), 0.0) + rms_back(mid, inverse_rms(mid), u_ref[...])
    gm_v[...] = gm
    gb_v[...] = gm.astype(BF)
    y_out[...] = jnp.where(live, mid + o_ref[...], 0.0).astype(BF)
    owners = 4 * n
    def mix(j, w):
        weight = out_ref[pl.ds(j * 8, 8)].reshape(8 * owned, width)
        r = contract_cols(gb_v[...], weight).astype(BF)
        for k in range(8 * owned // HEAD):
            dm_v[j * (8 * owned // HEAD) + k] = r[:, k * HEAD : (k + 1) * HEAD]
        return w
    lax.fori_loop(0, owners // 8, mix, 0)
    gb = gb_v[...]
    for i in range(2):
        w = width // 2
        grad = contract_rows(att_ref[...], gb[:, i * w : (i + 1) * w])
        red[i].p[...] = grad.astype(BF).reshape(red[i].p.shape)
        red[i].stage0()
    lax.fori_loop(1, n, feed, 0)
    tab.wait()
    tc, ts = tab_v[0], tab_v[1]

    at_row = c * rows + lax.broadcasted_iota(jnp.int32, (rows, total), 0)
    at_col = lax.broadcasted_iota(jnp.int32, (rows, total), 1)
    allowed = (at_col <= at_row) & (at_col < length)
    def group(g):
        key = kv_ref[:, :, g * HEAD : (g + 1) * HEAD].reshape(total, HEAD)
        val = kv_ref[:, :, KVDIM + g * HEAD : KVDIM + (g + 1) * HEAD].reshape(total, HEAD)
        def head(i, w):
            h = g * GROUP + i
            part = pl.ds(pl.multiple_of(i * rows, rows), rows)
            scores = jnp.where(allowed, contract_cols(q_ref[h], key) * SCALE, MASKED)
            e = jnp.exp(scores - jnp.max(scores, axis=1, keepdims=True))
            probs = e / jnp.sum(e, axis=1, keepdims=True)
            gprobs = contract_cols(dm_v[h], val)
            inner = jnp.sum(probs * gprobs, axis=1, keepdims=True)
            gs = (probs * (gprobs - inner)).astype(BF)
            p_v[part, :] = probs.astype(BF)
            gs_v[part, :] = gs
            dq = product(gs, key) * SCALE
            gp_v[:, pl.ds(pl.multiple_of(h * HEAD, HEAD), HEAD)] = (dq * tc - pltpu.roll(dq, HEAD // 2, 1) * ts).astype(BF)
            return w
        lax.fori_loop(0, GROUP, head, 0)
        mine = slice(g * GROUP, (g + 1) * GROUP)
        dk = contract_rows(gs_v[...], q_ref[mine].reshape(GROUP * rows, HEAD)) * SCALE
        dv = contract_rows(p_v[...], dm_v[mine].reshape(GROUP * rows, HEAD))
        lanes = slice(g * 2 * HEAD, g * 2 * HEAD + 2 * HEAD)
        dkv_v[:, :, :, lanes] = jnp.concatenate([dk, dv], 1).astype(BF).reshape(n // 2, 2, rows, 2 * HEAD)
        send(dkv_v.at[:, 1 - x, :, lanes], kx.at[:, :, lanes], kxs.at[g], kxr.at[g], s, xp)
    def kv_x(g):
        lanes = slice(g * 2 * HEAD, g * 2 * HEAD + 2 * HEAD)
        arrived(kx.at[:, :, lanes], kxr.at[g], pc)
        kx[:, :, lanes] = add_low(kx[:, :, lanes], dkv_v[:, x, :, lanes])
        for d in range(1, n // 2):
            to = lax.rem(z + d, n // 2)
            send(kx.at[to, :, lanes], kz.at[z, :, lanes], kzs.at[g, d], kzr.at[g, d], s, 2 * to + x)
    def kv_z(g):
        lanes = slice(g * 2 * HEAD, g * 2 * HEAD + 2 * HEAD)
        sumkv = kx[z, :, lanes].astype(F32)
        for d in range(1, n // 2):
            src = lax.rem(z + n // 2 - d, n // 2)
            arrived(kz.at[src, :, lanes], kzr.at[g, d], pc)
            sumkv = sumkv + kz[src, :, lanes].astype(F32)
        dk, dv = sumkv[:, :HEAD], sumkv[:, HEAD:]
        k0, v0 = QDIM + g * HEAD, QDIM + KVDIM + g * HEAD
        gp_v[:, k0 : k0 + HEAD] = (dk * tc - pltpu.roll(dk, HEAD // 2, 1) * ts).astype(BF)
        gp_v[:, v0 : v0 + HEAD] = dv.astype(BF)
    xin = x_ref[...].astype(F32)
    inverse = inverse_rms(xin)
    def joint(i, first, w):
        xh = (x_ref[...].astype(F32) * inverse).astype(BF)
        grad = contract_rows(xh, gp_v[:, first : first + w]).astype(BF)
        shape = red[i].p.shape[:-1] + (w,)
        red[i].p[..., :w] = grad.reshape(shape)
    group(0)
    red[0].stage1(); red[1].stage1()
    group(1)
    kv_x(0)
    red[0].stage2(); red[1].stage2()
    third = QDIM // 3
    for i in range(3):
        joint(2 + i, i * third, third)
        red[2 + i].stage0()
        if i == 0: kv_x(1)
    red[0].stage3(); red[1].stage3()
    red[2].stage1(); red[3].stage1(); red[4].stage1()
    kv_z(0); kv_z(1)
    joint(5, QDIM, 2 * KVDIM)
    sums = jnp.sum(gp_v[...].astype(F32), axis=0, keepdims=True)
    p5 = red[5].p
    qk_width = QDIM + KVDIM
    at = lax.broadcasted_iota(jnp.int32, (owned, HEAD), 0)
    for d in range(owners):
        tiles = (qk_width // owners * d // HEAD, qk_width // owners * d // HEAD + 1, (qk_width + KVDIM // owners * d) // HEAD)
        part = jnp.zeros((owned, HEAD), F32)
        for k, t in enumerate(tiles):
            part = jnp.where(at == k, sums[:, t * HEAD : t * HEAD + HEAD], part)
        plane = d // n
        p5[plane // 2, plane % 2, d % n // 2, d % 2, :, 2 * KVDIM :] = part.astype(BF)
    red[5].stage0()
    red[2].stage2(); red[3].stage2(); red[4].stage2()
    red[5].stage1()
    qk = QDIM + 2 * KVDIM
    gp = gp_v[...]
    def back(j, w):
        weight = qkv_ref[pl.ds(j * 8, 8), :, :qk].reshape(8 * owned, qk)
        cols = pl.ds(pl.multiple_of(j * 8 * owned, 8 * owned), 8 * owned)
        dx_out[:, cols] = contract_cols(gp, weight)
        return w
    lax.fori_loop(0, owners // 8, back, 0)
    red[2].stage3(); red[3].stage3(); red[4].stage3()
    red[5].stage2()
    own_raw.wait()
    def fed(d, w):
        src = lax.rem(c + d, n)
        arrived(raw_v.at[src], grs.at[src], pc)
        return w
    lax.fori_loop(1, n, fed, 0)
    place_back(raw_v, 0, dgate_out)
    dx_out[...] = gm_v[...] + rms_back(x_ref[...].astype(F32), inverse, dx_out[...])
    for i in range(2):
        dout_out[:, i * (width // 2) : (i + 1) * (width // 2)] = red[i].stage4()
    red[5].stage3()
    place_back(raw_v, 1, dup_out)
    gain = gain_ref[...]
    dgain_out[...] = jnp.sum(
        dgate_out[...] * gate_ref[...].astype(F32) + dup_out[...] * up_ref[...].astype(F32), axis=1, keepdims=True
    )
    dgate_out[...] = dgate_out[...] * gain
    dup_out[...] = dup_out[...] * gain
    for i in range(3):
        dqkv_out[:, i * third : (i + 1) * third] = red[2 + i].stage4()
    dqkv_out[:, QDIM:] = red[5].stage4()
    for r in red: r.finish()
    def fed_out(d, w):
        sent(raw_v.at[0], gss.at[lax.rem(c + d, n)], pc)
        return w
    lax.fori_loop(1, n, fed_out, 0)
    for g in range(2):
        lanes = slice(g * 2 * HEAD, g * 2 * HEAD + 2 * HEAD)
        sent(kx.at[:, :, lanes], kxs.at[g], pc)
        for d in range(1, n // 2): sent(kx.at[0, :, lanes], kzs.at[g, d], pc)

def backward_call(n, length, x, og, mid, u, o, att, q, kv, qkv_all, out_all, gate, up, gain, tables, gsum):
    S, V = jax.ShapeDtypeStruct, pltpu.VMEM
    rows, width = x.shape
    owned = qkv_all.shape[1]
    anys = pl.BlockSpec(memory_space=pl.ANY)
    vmem = pl.BlockSpec(memory_space=pltpu.VMEM)
    m = n // 2
    scratch = [V((2, rows, HEAD), F32), V((rows, width), F32), V((rows, width), BF), V((HEADS, rows, HEAD), BF),
               V((rows, QDIM + 2 * KVDIM), BF), V((GROUP * rows, n * rows), BF), V((GROUP * rows, n * rows), BF),
               V((m, 2, rows, 2 * KVDIM), BF), V((m, rows, 2 * KVDIM), BF), V((m, rows, 2 * KVDIM), BF),
               V((n, 2, owned, gsum.shape[2]), BF)]
    for i, w in enumerate((width // 2, width // 2, QDIM // 3, QDIM // 3, QDIM // 3, 2 * KVDIM + HEAD)):
        one = (m, 2, owned, w) if i % 2 == 0 else (2, m, owned, w)
        scratch += [V((2, 2, m, 2, owned, w), BF), V((2, m, 2, owned, w), BF), V(one, BF), V((m, owned, w), BF), V((m, owned, w), BF)]
    scratch += [DMA((2,)), DMA((2,)), DMA((2,)), DMA((2, m)), DMA((2, m)), DMA((n,)), DMA((n,)), DMA((6, 2 + m)), DMA((6, 2 + m))]
    return pl.pallas_call(
        functools.partial(backward_kernel, n),
        out_shape=[S((rows, width), BF), S((rows, width), F32), S((owned, width), F32), S((owned, qkv_all.shape[2]), F32),
                   S(gate.shape, F32), S(gate.shape, F32), S((owned, 1), F32)],
        in_specs=[pl.BlockSpec(memory_space=pltpu.SMEM)] + [vmem] * 13 + [anys] * 2,
        out_specs=[vmem] * 7,
        scratch_shapes=scratch,
        compiler_params=pltpu.CompilerParams(collective_id=2, has_side_effects=True, vmem_limit_bytes=62 * 2**20),
    )(length, x, og, mid, u, o, att, q, kv, qkv_all, out_all, gate, up, gain, tables, gsum)


def kernel_shards(
    tokens,
    lengths,
    attn_gain,
    qkv_weight,
    qkv_bias,
    out_weight,
    mlp_gain,
    gate_weight,
    up_weight,
    down_weight,
    out_grad,
):
    seqs, parts = lax.axis_size("seq"), lax.axis_size("ctx")
    rows, width = tokens.shape[1:]
    owned = gate_weight.shape[0]
    piece = down_weight.shape[0]
    padded = -(-piece // 32) * 32
    owners = seqs * parts
    me = lax.axis_index("seq") * parts + lax.axis_index("ctx")
    gain_one = attn_gain.astype(F32)[:, None]
    gain_two = mlp_gain.astype(F32)[:, None]
    half = HEAD // 2
    frequency = np.float32(ROPE_BASE) ** (-np.arange(half, dtype=np.float32) * np.float32(2.0 / HEAD))
    angles = np.arange(rows * parts, dtype=np.float32)[:, None] * frequency.astype(np.float32)[None, :]
    cosine, sine = np.cos(angles), np.sin(angles)
    tables = jnp.asarray(np.stack([np.concatenate([cosine, cosine], 1), np.concatenate([-sine, sine], 1)]), F32)
    down = jnp.pad(down_weight, ((0, padded - piece), (0, 0)))
    x, og = tokens[0], out_grad[0]
    gu_all, down_all, cot_all, qkv_all, out_all, kv_all, q, att, mid, n2 = forward_call(
        parts, lengths, x, og, qkv_weight, gain_one, qkv_bias[None], gate_weight, up_weight, gain_two,
        out_weight, down, tables,
    )
    u, o, gate_up_sum, grad_down = ffn_call(parts, n2, gu_all, down_all, cot_all)
    joint = qkv_all.shape[-1]
    output, grad_inputs, grad_out, raw_qkv, grad_gate, grad_up, grad_mlp_gain = backward_call(
        parts, lengths, x, og, mid, u, o, att, q, kv_all.reshape(parts, rows, 2 * KVDIM),
        qkv_all.reshape(owners, owned, joint), out_all.reshape(owners, owned, width),
        gate_weight, up_weight, gain_two, tables, gate_up_sum,
    )
    qk = QDIM + 2 * KVDIM
    bias_rows, raw_qkv = raw_qkv[:3, qk:], raw_qkv[:, :qk]
    grad_attn_gain = jnp.sum(raw_qkv * qkv_weight.astype(F32), axis=1)
    per, per_value = (QDIM + KVDIM) // owners, KVDIM // owners
    grad_qk_bias = lax.dynamic_slice_in_dim(bias_rows[:2].reshape(2 * HEAD), lax.rem(per * me, HEAD), per)
    grad_value_bias = lax.dynamic_slice_in_dim(bias_rows[2], lax.rem(per_value * me, HEAD), per_value)
    return (
        output[None],
        grad_inputs.astype(BF)[None],
        grad_attn_gain,
        raw_qkv * gain_one,
        grad_qk_bias,
        grad_out,
        grad_mlp_gain[:, 0],
        grad_gate,
        grad_up,
        grad_down[:piece],
        grad_value_bias,
    )


def solution(mesh):
    seqs, parts = mesh.shape["seq"], mesh.shape["ctx"]
    tiled = seqs == 4 and parts == 8 and 1536 // (seqs * parts) % 16 == 0
    rows, vector = P(BOTH, None), P(BOTH)
    token = P("seq", "ctx", None)
    return jax.shard_map(
        kernel_shards if tiled else plain_shards,
        mesh=mesh,
        in_specs=(token, P("seq"), vector, rows, vector, rows, vector, rows, rows, rows, token),
        out_specs=(token, token, vector, rows, vector, rows, vector, rows, rows, rows, vector),
        check_vma=False,
    )
```

```python
import functools

import jax
import jax.numpy as jnp
import numpy as np
from jax import lax
from jax.experimental import pallas as pl
from jax.experimental.pallas import tpu as pltpu
from jax.sharding import PartitionSpec as P

HEADS = 12
KV_HEADS = 2
HEAD = 128
QDIM = 1536
KVDIM = 256
GROUP = HEADS // KV_HEADS

EPSILON = 1e-06
ROPE_BASE = 1000000.0
MASKED = -1e30
SCALE = HEAD ** (-0.5)
BF = jnp.bfloat16
F32 = jnp.float32
BOTH = ("seq", "ctx")


DMA = pltpu.SemaphoreType.DMA
MESH = pl.DeviceIdType.MESH


def product(left, right):
    return jnp.dot(left, right, preferred_element_type=F32)


def contract_rows(left, right):
    return lax.dot_general(left, right, (((0,), (0,)), ((), ())), preferred_element_type=F32)


def contract_cols(left, right):
    return lax.dot_general(left, right, (((1,), (1,)), ((), ())), preferred_element_type=F32)


def inverse_rms(values):
    return lax.rsqrt(jnp.mean(values * values, axis=-1, keepdims=True) + EPSILON)


def rms_back(values, inverse, scaled_grad):
    inner = jnp.mean(scaled_grad * values, axis=-1, keepdims=True)
    return inverse * scaled_grad - values * (inverse * inverse * inverse) * inner


def rope_tables(positions):
    half = HEAD // 2
    frequency = ROPE_BASE ** (-jnp.arange(half, dtype=F32) * 2.0 / HEAD)
    angles = positions.astype(F32)[:, None] * frequency[None, :]
    return jnp.cos(angles), jnp.sin(angles)


def rotate(values, cosine, sine):
    half = HEAD // 2
    first, second = values[..., :half], values[..., half:]
    cosine, sine = cosine[:, None, :], sine[:, None, :]
    return jnp.concatenate([first * cosine - second * sine, second * cosine + first * sine], -1)


def gather(values, axes):
    return lax.all_gather(values, axes, axis=0, tiled=True)


def scatter(values, axes):
    return lax.psum_scatter(values, axes, scatter_dimension=0, tiled=True)


def plain_shards(
    tokens,
    lengths,
    attn_gain,
    qkv_weight,
    qkv_bias,
    out_weight,
    mlp_gain,
    gate_weight,
    up_weight,
    down_weight,
    out_grad,
):
    seqs, parts = lax.axis_size("seq"), lax.axis_size("ctx")
    inputs = tokens[0].astype(F32)
    rows, width = inputs.shape
    owned, hidden = gate_weight.shape
    piece = down_weight.shape[0]
    chunk = hidden // parts
    length = lengths[0]
    positions = lax.axis_index("ctx") * rows + jnp.arange(rows, dtype=jnp.int32)
    living = (positions < length).astype(F32)[:, None]
    cosine, sine = rope_tables(positions)

    gain_one = attn_gain.astype(F32)[:, None]
    gain_two = mlp_gain.astype(F32)[:, None]
    qkv_all = gather((qkv_weight.astype(F32) * gain_one).astype(BF), BOTH)
    bias_all = gather(qkv_bias, BOTH).astype(F32)
    out_all = gather(out_weight, BOTH)

    def to_chunks(weight):
        scaled = (weight.astype(F32) * gain_two).astype(BF)
        return scaled.reshape(owned, seqs, parts, piece).transpose(2, 0, 1, 3)

    both = jnp.stack([to_chunks(gate_weight), to_chunks(up_weight)], axis=1)
    both = lax.all_to_all(both.reshape(parts, 2, owned, chunk), "ctx", 0, 0)
    both = lax.all_gather(both, "seq", axis=0)
    gate_chunk = both[:, :, 0].reshape(width, chunk)
    up_chunk = both[:, :, 1].reshape(width, chunk)
    down_chunk = gather(down_weight, "seq")
    cotangent = out_grad[0].astype(F32) * living
    cot_all = gather(cotangent.astype(BF), "ctx")

    inverse_one = inverse_rms(inputs)
    normed_one = (inputs * inverse_one).astype(BF)
    project = product(normed_one, qkv_all) + bias_all
    queries = rotate(project[:, :QDIM].reshape(rows, HEADS, HEAD), cosine, sine).astype(BF)
    own_keys = rotate(
        project[:, QDIM : QDIM + KVDIM].reshape(rows, KV_HEADS, HEAD), cosine, sine
    ).astype(BF)
    own_values = project[:, QDIM + KVDIM :].astype(BF).reshape(rows, KV_HEADS, HEAD)
    keys, values = gather(own_keys, "ctx"), gather(own_values, "ctx")
    key_pos = jnp.arange(rows * parts, dtype=jnp.int32)
    allowed = (key_pos[None, :] <= positions[:, None]) & (key_pos[None, :] < length)
    grouped = queries.reshape(rows, KV_HEADS, GROUP, HEAD)
    scores = jnp.einsum("qgha,kga->ghqk", grouped, keys, preferred_element_type=F32) * SCALE
    scores = jnp.where(allowed, scores, MASKED)
    largest = jnp.max(scores, axis=-1, keepdims=True)
    exponent = jnp.exp(scores - largest)
    summed = jnp.sum(exponent, axis=-1, keepdims=True)
    probs = exponent / summed
    probs_low = probs.astype(BF)
    attended = jnp.einsum("ghqk,kga->qgha", probs_low, values, preferred_element_type=F32)
    attended = attended.reshape(rows, QDIM).astype(BF)
    middle = inputs + product(attended, out_all)

    inverse_two = inverse_rms(middle)
    normed_two = gather((middle * inverse_two).astype(BF), "ctx")
    gate_pre = product(normed_two, gate_chunk)
    up_pre = product(normed_two, up_chunk)
    sig = jax.nn.sigmoid(gate_pre)
    activated = (gate_pre * sig * up_pre).astype(BF)
    grad_act = contract_cols(cot_all, down_chunk)
    grad_gate = (grad_act * up_pre * (sig + gate_pre * sig * (1.0 - sig))).astype(BF)
    grad_up = (grad_act * gate_pre * sig).astype(BF)
    scaled_two = contract_cols(grad_gate, gate_chunk) + contract_cols(grad_up, up_chunk)
    scaled_two = scatter(scaled_two.astype(BF), "ctx").astype(F32)
    branch = scatter(product(activated, down_chunk).astype(BF), "ctx").astype(F32)
    output = ((middle + branch) * living).astype(BF)
    grad_down = scatter(contract_rows(activated, cot_all).astype(BF), "seq").astype(F32)
    raw = jnp.stack([contract_rows(normed_two, grad_gate), contract_rows(normed_two, grad_up)], 1)
    raw = scatter(raw.astype(BF), "seq").reshape(parts, owned, 2, chunk)
    raw = lax.all_to_all(raw, "ctx", 0, 0).astype(F32)
    raw = raw.reshape(parts, owned, 2, seqs, piece).transpose(2, 1, 3, 0, 4)
    raw = raw.reshape(2, owned, hidden)
    grad_mlp_gain = jnp.sum(raw[0] * gate_weight.astype(F32) + raw[1] * up_weight.astype(F32), 1)

    grad_middle = cotangent + rms_back(middle, inverse_two, scaled_two)
    grad_branch = grad_middle.astype(BF)
    grad_out = scatter(contract_rows(attended, grad_branch).astype(BF), BOTH).astype(F32)
    grad_mixed = contract_cols(grad_branch, out_all).astype(BF)
    grad_mixed = grad_mixed.reshape(rows, KV_HEADS, GROUP, HEAD)
    grad_probs = jnp.einsum("qgha,kga->ghqk", grad_mixed, values, preferred_element_type=F32)
    inner = jnp.sum(probs * grad_probs, axis=-1, keepdims=True)
    grad_scores = (probs * (grad_probs - inner)).astype(BF)
    grad_q = jnp.einsum("ghqk,kga->qgha", grad_scores, keys, preferred_element_type=F32) * SCALE
    grad_k = jnp.einsum("ghqk,qgha->kga", grad_scores, grouped, preferred_element_type=F32) * SCALE
    grad_v = jnp.einsum("ghqk,qgha->kga", probs_low, grad_mixed, preferred_element_type=F32)
    grad_k = scatter(grad_k.astype(BF), "ctx").astype(F32)
    grad_v = scatter(grad_v.astype(BF), "ctx").astype(F32)
    grad_q = rotate(grad_q.reshape(rows, HEADS, HEAD), cosine, -sine).reshape(rows, QDIM)
    grad_k = rotate(grad_k, cosine, -sine).reshape(rows, KVDIM)
    grad_project = jnp.concatenate([grad_q, grad_k, grad_v.reshape(rows, KVDIM)], axis=1)
    grad_project = grad_project.astype(BF)
    raw_qkv = scatter(contract_rows(normed_one, grad_project).astype(BF), BOTH).astype(F32)
    grad_attn_gain = jnp.sum(raw_qkv * qkv_weight.astype(F32), axis=1)
    grad_bias = jnp.sum(grad_project.astype(F32), axis=0)
    qk_width = QDIM + KVDIM
    grad_qk_bias = scatter(grad_bias[:qk_width], BOTH)
    grad_value_bias = scatter(grad_bias[qk_width:], BOTH)
    scaled_one = contract_cols(grad_project, qkv_all)
    grad_inputs = (grad_middle + rms_back(inputs, inverse_one, scaled_one)).astype(BF)
    return (
        output[None],
        grad_inputs[None],
        grad_attn_gain,
        raw_qkv * gain_one,
        grad_qk_bias,
        grad_out,
        grad_mlp_gain,
        raw[0] * gain_two,
        raw[1] * gain_two,
        grad_down,
        grad_value_bias,
    )


class Place:
    def __init__(self, n):
        self.n = n
        self.s, self.c = lax.axis_index("seq"), lax.axis_index("ctx")
        self.me = self.s * n + self.c
        self.core = lax.rem(self.s, 2)
        self.sib = self.s + 1 - 2 * self.core
        self.far = lax.rem(self.s + 2, 4)
        half = self.c // 2
        self.pos = half + lax.rem(self.c, 2) * (n - 1 - 2 * half)
        self.nxt, self.prv = self.at(1), self.at(-1)
    def at(self, offset):
        p = lax.rem(self.pos + offset + 2 * self.n, self.n)
        return 2 * p + (p // (self.n // 2)) * (2 * self.n - 1 - 4 * p)

def send(src, dst, ssem, rsem, seq, ctx):
    copy = pltpu.make_async_remote_copy(src, dst, ssem, rsem, device_id=(seq, ctx), device_id_type=MESH)
    copy.start()

def arrived(dst, rsem, place):
    pltpu.make_async_remote_copy(dst, dst, rsem, rsem, device_id=(place.s, place.c), device_id_type=MESH).wait_recv()

def sent(src, ssem, place):
    pltpu.make_async_remote_copy(src, src, ssem, ssem, device_id=(place.s, place.c), device_id_type=MESH).wait_send()

def enter(place, whole_group=True):
    barrier = pltpu.get_barrier_semaphore()
    def greet(d, z):
        pl.semaphore_signal(barrier, inc=1, device_id=(place.s, lax.rem(place.c + d, place.n)), device_id_type=MESH)
        return z
    lax.fori_loop(1, place.n, greet, 0)
    pl.semaphore_signal(barrier, inc=1, device_id=(place.sib, place.c), device_id_type=MESH)
    pl.semaphore_signal(barrier, inc=1, device_id=(place.far, place.c), device_id_type=MESH)
    pl.semaphore_wait(barrier, place.n + 1)


def add_low(left, right):
    return (left.astype(F32) + right.astype(F32)).astype(BF)

class RingGather:
    def __init__(self, pc, slots, ssem, rsem, index=None):
        self.pc, self.slots, self.ssem, self.rsem, self.index = pc, slots, ssem, rsem, index
        self.steps, self.half = pc.n // 2, slots.shape[2] // 2
        self.ways = ((0, -1, pc.nxt), (1, 1, pc.prv))
    def slot(self, offset):
        return self.index[offset] if self.index else self.pc.at(offset)
    def part(self, ref, f, t):
        return ref if t < self.steps - 1 else ref.at[:, pl.ds(f * self.half, self.half)]
    def hop(self, t, own=None):
        for f, sign, to in self.ways:
            src = self.slots.at[self.slot(sign * t)] if own is None else own
            there = self.slots.at[self.slot(sign * (t + 1) if self.index else sign * t)]
            send(self.part(src, f, t), self.part(there, f, t), self.ssem.at[f, t], self.rsem.at[f, t], self.pc.s, to)
    def turn(self, t):
        for f, sign, _ in self.ways:
            arrived(self.part(self.slots.at[self.slot(sign * (t + 1))], f, t), self.rsem.at[f, t], self.pc)
        if t + 1 < self.steps: self.hop(t + 1)
    def finish(self):
        for f in range(2):
            for t in range(self.steps): sent(self.part(self.slots.at[0], f, t), self.ssem.at[f, t], self.pc)

class RingSum:
    def __init__(self, pc, term, index, held_half, held, ssem, rsem, out):
        self.pc, self.term, self.index, self.out = pc, term, index, out
        self.held_half, self.held, self.ssem, self.rsem = held_half, held, ssem, rsem
        self.steps, self.half = pc.n // 2, term.shape[2] // 2
    def turn(self, t):
        pc, ahead = self.pc, self.steps - t
        for f, sign, to in ((0, 1, pc.nxt), (1, -1, pc.prv)):
            cols = slice(f * self.half, (f + 1) * self.half)
            i = self.index[sign * ahead]
            if t == 1:
                arrived(self.held_half.at[f], self.rsem.at[f, 0], pc)
                self.term[i, :, cols] = add_low(self.term[i, :, cols], self.held_half[f])
            elif t > 1:
                arrived(self.held.at[f, t - 2], self.rsem.at[f, t - 1], pc)
                if t < self.steps: self.term[i] = add_low(self.term[i], self.held[f, t - 2])
            if t == 0:
                src, dst = self.term.at[i, :, pl.ds(f * self.half, self.half)], self.held_half.at[f]
            elif t < self.steps:
                src, dst = self.term.at[i], self.held.at[f, t - 1]
            if t < self.steps: send(src, dst, self.ssem.at[f, t], self.rsem.at[f, t], pc.s, to)
        if t == self.steps:
            i = self.index[0]
            self.out[...] = self.term[i].astype(F32) + self.held[0, t - 2].astype(F32) + self.held[1, t - 2].astype(F32)
    def finish(self):
        for f in range(2):
            sent(self.held_half.at[f], self.ssem.at[f, 0], self.pc)
            for t in range(1, self.steps): sent(self.held.at[f, 0], self.ssem.at[f, t], self.pc)

class Spread:
    def __init__(self, pc, x_first, w, ss, rs, i):
        self.pc, self.x_first, self.w, self.ss, self.rs, self.i = pc, x_first, w, ss, rs, i
        self.y, self.x, self.z = pc.s // 2, lax.rem(pc.c, 2), pc.c // 2
        self.xp = pc.c + 1 - 2 * self.x
        self.deep = pc.n // 2
    def go(self, k, part, seq, ctx):
        send(part, part, self.ss.at[self.i, k], self.rs.at[self.i, k], seq, ctx)
    def come(self, k, part):
        arrived(part, self.rs.at[self.i, k], self.pc)
    def both(self, k, part, sib_k, seq, ctx, sib_part):
        self.go(k, part, seq, ctx)
        self.go(sib_k, sib_part, self.pc.sib, self.pc.c)
    def begin(self):
        own = self.w.at[self.y, self.pc.core, self.z, self.x]
        for d in range(1, self.deep):
            self.go(d - 1, own, self.pc.s, 2 * lax.rem(self.z + d, self.deep) + self.x)
    def stage1(self):
        pc, w, y, x = self.pc, self.w, self.y, self.x
        for d in range(1, self.deep):
            self.come(d - 1, w.at[y, pc.core, lax.rem(self.z + self.deep - d, self.deep), x])
        column = w.at[y, pc.core, :, x]
        if self.x_first: self.both(self.deep, column, self.deep + 2, pc.s, self.xp, column)
        else: self.both(self.deep, column, self.deep + 2, pc.far, pc.c, column)
    def stage2(self):
        pc, w, y, x = self.pc, self.w, self.y, self.x
        if self.x_first:
            new = w.at[y, pc.core, :, 1 - x]
            self.come(self.deep, new)
            self.both(self.deep + 1, w.at[y, pc.core], self.deep + 3, pc.far, pc.c, new)
        else:
            new = w.at[1 - y, pc.core, :, x]
            self.come(self.deep, new)
            self.both(self.deep + 1, w.at[:, pc.core, :, x], self.deep + 3, pc.s, self.xp, new)
    def stage3(self):
        pc, w, y, x = self.pc, self.w, self.y, self.x
        new = w.at[1 - y, pc.core] if self.x_first else w.at[:, pc.core, :, 1 - x]
        self.come(self.deep + 1, new)
        self.go(self.deep + 4, new, pc.sib, pc.c)
    def stage4(self):
        pc, w, y, x = self.pc, self.w, self.y, self.x
        other = 1 - pc.core
        self.come(self.deep + 2, w.at[y, other, :, x])
        self.come(self.deep + 3, w.at[y, other, :, 1 - x] if self.x_first else w.at[1 - y, other, :, x])
        self.come(self.deep + 4, w.at[1 - y, other] if self.x_first else w.at[:, other, :, 1 - x])
    def finish(self):
        w, four = self.w, self.w.at[0, 0, :, 0]
        eight = w.at[0, 0] if self.x_first else w.at[:, 0, :, 0]
        for d in range(1, self.deep): sent(w.at[0, 0, 0, 0], self.ss.at[self.i, d - 1], self.pc)
        for k, part in enumerate((four, eight, four, four, eight)): sent(part, self.ss.at[self.i, self.deep + k], self.pc)

def windows(n, piece, padded):
    for part in range(n):
        for plane in range(4):
            whole, packed = (plane * n + part) * piece, plane * padded
            first, packed_first = whole // 128 * 128, packed // 128 * 128
            span = -(-(whole + piece) // 128) * 128 - first
            packed_span = -(-(packed + piece) // 128) * 128 - packed_first
            yield part, whole - first, packed - packed_first, first, span, packed_first, packed_span

def shift_lanes(block, span, shift):
    if block.shape[1] < span:
        block = jnp.concatenate([block, jnp.zeros((block.shape[0], span - block.shape[1]), block.dtype)], 1)
    shift = shift % block.shape[1]
    return pltpu.roll(block, shift, 1) if shift else block

def place_back(raw, a, out):
    n, _, owned, chunk = raw.shape
    piece, padded = out.shape[1] // (4 * n), chunk // 4
    for part, at, packed_at, first, span, packed_first, packed_span in windows(n, piece, padded):
        block = raw[part, a, :, packed_first : packed_first + packed_span].astype(F32)
        block = shift_lanes(block, span, at - packed_at)[:, :span]
        lane = lax.broadcasted_iota(jnp.int32, block.shape, 1)
        here = (lane >= at) & (lane < at + piece)
        out[:, first : first + span] = jnp.where(here, block, out[:, first : first + span])

def place_out(weight, gain, a, packs):
    n, _, _, chunk = packs.shape
    owned = weight.shape[0]
    piece, padded = weight.shape[1] // (4 * n), chunk // 4
    for part in range(n): packs[part, a, :owned] = jnp.zeros((owned, chunk), BF)
    for part, at, packed_at, first, span, packed_first, packed_span in windows(n, piece, padded):
        block = weight[:, first : first + span].astype(F32) * gain
        block = shift_lanes(block, packed_span, packed_at - at)[:, :packed_span]
        lane = lax.broadcasted_iota(jnp.int32, block.shape, 1)
        here = (lane >= packed_at) & (lane < packed_at + piece)
        before = packs[part, a, :owned, packed_first : packed_first + packed_span].astype(F32)
        packs[part, a, :owned, packed_first : packed_first + packed_span] = jnp.where(here, block, before).astype(BF)


def rope(values, table_c, table_s):
    return values * table_c + pltpu.roll(values, HEAD // 2, 1) * table_s

def layer_kernel(n, length_ref, x_ref, og_ref, qw_ref, g1_ref, b_ref, gate_ref, up_ref, g2_ref, down, outw, tables,
                 qkv_all, out_all, kv_all, q_out, half_sum, dsum, att_out, mid_out, u_own, o_own,
                 gu_v, down_v, cot_v, n2_v, act_v, gg_v, gp_v, ut, uhh, uh, ot, ohh, oh, dgu_v, dd_v, r0g, r0d, r1d, w_o2,
                 kv_v, q_v, tab_v,
                 local, save, ss, rs, g_recv, g_send, g_own, g_far, g_sib, d_recv, d_far, d_sib, c_recv, c_send,
                 kz_s, kz_r, kx_s, kx_r, n_recv, n_send, u_recv, u_send, o_recv_, o_send_, gs0, gr0, gsave, ds0, dr0, ds1, dr1, dsave):
    pc = Place(n)
    me, s, c = pc.me, pc.s, pc.c
    y, x, z, xp = s // 2, lax.rem(c, 2), c // 2, c + 1 - 2 * lax.rem(c, 2)
    rows, width = x_ref.shape
    owned, piece = qw_ref.shape[0], down.shape[0]
    length = length_ref[0]
    third, owners, deep = QDIM // 3, 4 * n, n // 2

    def g_slot(i): return gu_v.at[:, pl.ds(pl.multiple_of(i * owned, owned), owned), :]
    def pack(i): return act_v.at[i, :, pl.ds(0, owned), :]
    def d_slot(i): return down_v.at[pl.ds(pl.multiple_of(i * piece, piece), piece), :]

    kvw = 2 * KVDIM + HEAD
    def cut(ref, first, w): return ref.at[:, :, :, :, :, pl.ds(first, w)]
    w_kv = cut(dgu_v.at[0], 0, kvw)
    wide = (w_kv, cut(dgu_v.at[0], kvw, third), cut(dgu_v.at[1], 0, third), cut(dgu_v.at[1], third, third),
            cut(r0g, 0, width // 2), cut(r0g, width // 2, width // 4), w_o2)
    spreads = [Spread(pc, i % 2 == 0, w, ss, rs, i) for i, w in enumerate(wide)]
    kvs, q0, q1, q2, o0, o1, o2 = spreads
    outs = ((o0, 0, width // 2), (o1, width // 2, width // 4), (o2, width // 4 * 3, width // 4))
    pairs = n // 2
    offsets = [o for j in range(1, pairs) for o in (-j, j)] + [pairs, 0]
    index = {o: i for i, o in enumerate(offsets)}
    index[-pairs] = index[pairs]
    cring = RingGather(pc, cot_v, c_send, c_recv, index)
    nring = RingGather(pc, n2_v, n_send, n_recv, index)
    uring = RingSum(pc, ut, index, uhh, uh, u_send, u_recv, u_own)
    oring = RingSum(pc, ot, index, ohh, oh, o_send_, o_recv_, o_own)
    lc = [pltpu.make_async_copy(a, b, local.at[i]) for i, (a, b) in enumerate((
        (outw.at[:, pl.ds(0, width // 2)], wide[4].at[y, pc.core, z, x]), (outw.at[:, pl.ds(width // 2, width // 4)], wide[5].at[y, pc.core, z, x]),
        (outw.at[:, pl.ds(width // 4 * 3, width // 4)], w_o2.at[y, pc.core, z, x]), (down, d_slot(s)), (tables.at[:, pl.ds(pl.multiple_of(c * rows, rows), rows), :], tab_v)))]
    for copy in lc: copy.start()
    g1 = g1_ref[...]
    def scaled(first, w): return (qw_ref[:, first : first + w].astype(F32) * g1).astype(BF)
    w_kv[y, pc.core, z, x, :, : 2 * KVDIM] = scaled(QDIM, 2 * KVDIM)
    share = b_ref.shape[1]
    bias = b_ref[...].astype(F32)
    rest = jnp.zeros((1, HEAD - share), F32)
    odd = lax.rem(me, 2) == 1
    row = jnp.where(odd, jnp.concatenate([rest, bias], 1), jnp.concatenate([bias, rest], 1))
    first_row = lax.broadcasted_iota(jnp.int32, (owned, HEAD), 0) == 0
    w_kv[y, pc.core, z, x, :, 2 * KVDIM :] = jnp.where(first_row, row, 0.0).astype(BF)
    for i, w in enumerate(wide[1:4]): w[y, pc.core, z, x] = scaled(i * third, third)
    slot_pos = c * rows + lax.broadcasted_iota(jnp.int32, (rows, width), 0)
    cot_v[index[0]] = jnp.where(slot_pos < length, og_ref[...].astype(F32), 0.0).astype(BF)
    enter(pc)
    def gu_turn(t):
        k = s * n + lax.rem(c + n - t, n)
        arrived(g_slot(k), g_recv.at[k], pc)
        send(g_slot(k), g_slot(k), g_far.at[lax.rem(c + n - t, n)], g_recv.at[k], pc.far, c)
        send(g_slot(k), g_slot(k), g_sib.at[k], g_recv.at[k], pc.sib, c)
    for p in (kvs, q0, q1, q2): p.begin()
    send(down, d_slot(s), d_far.at[0], d_recv.at[s], pc.far, c)
    send(down, d_slot(s), d_sib.at[s], d_recv.at[s], pc.sib, c)
    xf = x_ref[...].astype(F32)
    att_out[...] = (xf * inverse_rms(xf)).astype(BF)
    g2 = g2_ref[...]
    place_out(gate_ref, g2, 0, act_v)
    kvs.stage1()
    q0.stage1()
    place_out(up_ref, g2, 1, act_v)
    q1.stage1()
    kvs.stage2()
    own_gu = pltpu.make_async_copy(pack(c), g_slot(me), local.at[5])
    own_gu.start()
    def feed(d, v):
        to = lax.rem(c + d, n)
        send(pack(to), g_slot(me), g_send.at[to], g_recv.at[me], s, to)
        return v
    q2.stage1()
    lax.fori_loop(1, n, feed, 0)
    q0.stage2()
    kvs.stage3()
    q1.stage2()
    for copy in lc[:3]: copy.wait()
    o0.begin(); o1.begin(); o2.begin()
    q2.stage2()
    q0.stage3()
    q1.stage3()
    q2.stage3()
    send(pack(c), g_slot(me), g_own.at[0], g_recv.at[me], pc.far, c)
    send(pack(c), g_slot(me), g_own.at[1], g_recv.at[me], pc.sib, c)
    kvs.stage4()
    lc[4].wait()
    tc, ts = tab_v[0], tab_v[1]
    xh = att_out[...]
    def bias_of(tile):
        d = 2 * tile
        def part(i):
            plane, place = i // n, i % n
            return w_kv[plane // 2, plane % 2, place // 2, place % 2, 0:1, 2 * KVDIM :].astype(F32)
        return part(d) + part(d + 1)
    kv = product(xh, w_kv[..., : 2 * KVDIM].reshape(owners * owned, 2 * KVDIM))
    for k in range(2 * KV_HEADS):
        lanes = slice(k * HEAD, (k + 1) * HEAD)
        one = kv[:, lanes] + bias_of(QDIM // HEAD + k)
        kv_v[z, x, :, lanes] = (rope(one, tc, ts) if k < KV_HEADS else one).astype(BF)
    own_kv = kv_v.at[z, x]
    for d in range(1, deep):
        send(own_kv, own_kv, kz_s.at[d], kz_r.at[d], s, 2 * lax.rem(z + d, deep) + x)
    send(own_kv, own_kv, kx_s.at[0], kx_r.at[0], s, xp)
    o0.stage1(); o1.stage1(); o2.stage1()
    for i, p in enumerate((q0, q1, q2)):
        p.stage4()
        r = product(xh, p.w[...].reshape(owners * owned, third))
        for k in range(third // HEAD):
            h = i * (third // HEAD) + k
            q_v[h] = rope(r[:, k * HEAD : (k + 1) * HEAD] + bias_of(h), tc, ts).astype(BF)
    for d in range(1, deep):
        block = kv_v.at[lax.rem(z + deep - d, deep), x]
        arrived(block, kz_r.at[d], pc)
        send(block, block, kx_s.at[d], kx_r.at[d], s, xp)
    cring.hop(0)
    o0.stage2(); o1.stage2(); o2.stage2()
    saves = [pltpu.make_async_copy(q_v, q_out, save.at[0])]
    for i, (p, first) in enumerate(((kvs, QDIM), (q0, 0), (q1, third), (q2, 2 * third))):
        saves.append(pltpu.make_async_copy(p.w, qkv_all.at[:, :, :, :, :, pl.ds(first, p.w.shape[5])], save.at[1 + i]))
    for copy in saves: copy.start()
    for d in range(deep):
        arrived(kv_v.at[lax.rem(z + deep - d, deep), 1 - x], kx_r.at[d], pc)

    total = n * rows
    at_row = c * rows + lax.broadcasted_iota(jnp.int32, (rows, total), 0)
    at_col = lax.broadcasted_iota(jnp.int32, (rows, total), 1)
    allowed = (at_col <= at_row) & (at_col < length)
    def heads(first, count):
        def head(h, v):
            col = pl.multiple_of(h // GROUP * HEAD, HEAD)
            key = kv_v[:, :, :, pl.ds(col, HEAD)].reshape(total, HEAD)
            val = kv_v[:, :, :, pl.ds(pl.multiple_of(KVDIM + col, HEAD), HEAD)].reshape(total, HEAD)
            scores = jnp.where(allowed, contract_cols(q_v[h], key) * SCALE, MASKED)
            e = jnp.exp(scores - jnp.max(scores, axis=1, keepdims=True))
            probs = (e / jnp.sum(e, axis=1, keepdims=True)).astype(BF)
            att_out[:, pl.ds(pl.multiple_of(h * HEAD, HEAD), HEAD)] = product(probs, val).astype(BF)
            return v
        lax.fori_loop(first, first + count, head, 0)
    gu_turn(1); gu_turn(2)
    o0.stage3(); o1.stage3(); o2.stage3()
    heads(0, GROUP)
    gu_turn(3); gu_turn(4)
    cring.turn(0)
    heads(GROUP, GROUP)
    gu_turn(5); gu_turn(6)
    own_gu.wait()
    for i in range(2): sent(pack(0), g_own.at[i], pc)
    def fed(d, v):
        sent(pack(0), g_send.at[lax.rem(c + d, n)], pc)
        return v
    lax.fori_loop(1, n, fed, 0)
    gu_turn(7)
    o0.stage4(); o1.stage4(); o2.stage4()
    saves2 = [pltpu.make_async_copy(kv_v, kv_all, save.at[5])]
    for i, (p, first, w) in enumerate(outs):
        saves2.append(pltpu.make_async_copy(p.w, out_all.at[:, :, :, :, :, pl.ds(first, w)], save.at[6 + i]))
    for copy in saves2: copy.start()
    cring.turn(1)
    att = att_out[...]
    for p, first, w in outs:
        lanes = slice(first, first + w)
        mid_out[:, lanes] = x_ref[:, lanes].astype(F32) + product(att, p.w[...].reshape(owners * owned, w))
    mid = mid_out[...]
    n2_v[index[0]] = (mid * inverse_rms(mid)).astype(BF)
    nring.hop(0)
    cring.turn(2)
    arrived(d_slot(pc.far), d_recv.at[pc.far], pc)
    send(d_slot(pc.far), d_slot(pc.far), d_sib.at[pc.far], d_recv.at[pc.far], pc.sib, c)
    def across(t):
        k = pc.far * n + lax.rem(c + n - t, n)
        arrived(g_slot(k), g_recv.at[k], pc)
        send(g_slot(k), g_slot(k), g_sib.at[k], g_recv.at[k], pc.sib, c)
    for t in range(n):
        if t == n - 1:
            for copy in saves + saves2: copy.wait()
            for p in spreads: p.finish()
        across(t)
        if t == 1: nring.turn(0)
        if t == 3: cring.turn(3)
        if t == 4: nring.turn(1)
    for plane in range(2):
        other = 2 * plane + 1 - pc.core
        arrived(d_slot(other), d_recv.at[other], pc)
        def come(t, v):
            i = other * n + t
            arrived(g_slot(i), g_recv.at[i], pc)
            return v
        lax.fori_loop(0, n, come, 0)
    lc[3].wait()
    tall, chunk = 2 * rows, gu_v.shape[2]
    def forward(j):
        pair = slice(2 * j, 2 * j + 2)
        normed = n2_v[pair].reshape(tall, width)
        gate = product(normed, gu_v[0])
        up = product(normed, gu_v[1])
        sig = jax.nn.sigmoid(gate)
        gs = gate * sig
        act = (gs * up).astype(BF)
        act_v[pair] = act.reshape(2, 2, rows // 2, chunk)
        gp_v[pair] = gs.astype(BF).reshape(2, rows, chunk)
        gg_v[pair] = (up * (sig + gs * (1.0 - sig))).astype(BF).reshape(2, rows, chunk)
        ot[pair] = product(act, down_v[...]).astype(BF).reshape(2, rows, width)
    def backward(j):
        pair = slice(2 * j, 2 * j + 2)
        grad = contract_cols(cot_v[pair].reshape(tall, width), down_v[...])
        gg = (grad * gg_v[pair].reshape(tall, chunk).astype(F32)).astype(BF)
        gp = (grad * gp_v[pair].reshape(tall, chunk).astype(F32)).astype(BF)
        gg_v[pair] = gg.reshape(2, rows, chunk)
        gp_v[pair] = gp.reshape(2, rows, chunk)
        ut[pair] = (contract_cols(gg, gu_v[0]) + contract_cols(gp, gu_v[1])).astype(BF).reshape(2, rows, width)

    all_rows = n * rows
    plane = n * owned
    core = pc.core
    tile = 384
    def cols_of(j): return pl.ds(j * tile, tile)
    wide_pieces = [(0, j, a) for j in range(chunk // tile) for a in range(2)]
    down_pieces = [(1, j, 0) for j in range(width // tile)]
    def compute(p):
        kind, j, a = p
        if kind == 0:
            lhs, rhs = n2_v[...].reshape(all_rows, width), (gg_v, gp_v)[a]
            grad = contract_rows(lhs, rhs[:, :, cols_of(j)].reshape(all_rows, tile))
            dgu_v[a, :, :, :, :, :, cols_of(j)] = grad.astype(BF).reshape(2, 2, deep, 2, owned, tile)
            send(dgu_v.at[a, :, 1 - core, :, :, :, cols_of(j)], r0g.at[a, :, :, :, :, cols_of(j)],
                 gs0.at[a, j], gr0.at[a, j], pc.sib, c)
        else:
            grad = contract_rows(act_v[...].reshape(all_rows, chunk), cot_v[:, :, cols_of(j)].reshape(all_rows, tile))
            dd_v[:, :, :, cols_of(j)] = grad.astype(BF).reshape(2, 2, piece, tile)
            send(dd_v.at[:, 1 - core, :, cols_of(j)], r0d.at[:, :, cols_of(j)], ds0.at[j], dr0.at[j], pc.sib, c)
    def add_core(p):
        kind, j, a = p
        cols = cols_of(j)
        if kind == 0:
            arrived(r0g.at[a, :, :, :, :, cols], gr0.at[a, j], pc)
            for k in range(2):
                r0g[a, k, :, :, :, cols] = add_low(r0g[a, k, :, :, :, cols], dgu_v[a, k, core, :, :, :, cols])
            copy = pltpu.make_async_copy(r0g.at[a, :, :, :, :, cols], half_sum.at[a, :, :, :, :, cols], gsave.at[a, j])
            copy.start()
            saves.append(copy)
        else:
            arrived(r0d.at[:, :, cols], dr0.at[j], pc)
            for k in range(2):
                r0d[k, :, cols] = add_low(r0d[k, :, cols], dd_v[k, core, :, cols])
            send(r0d.at[1 - y, :, cols], r1d.at[:, cols], ds1.at[j], dr1.at[j], pc.far, c)
    def add_far(p):
        _, j, _ = p
        cols = cols_of(j)
        arrived(r1d.at[:, cols], dr1.at[j], pc)
        r1d[:, cols] = add_low(r1d[:, cols], r0d[y, :, cols])
        copy = pltpu.make_async_copy(r1d.at[:, cols], dsum.at[:, cols], dsave.at[j])
        copy.start()
        saves.append(copy)
    saves.clear()
    forward(0)
    nring.turn(2)
    forward(1)
    nring.turn(3)
    forward(2)
    forward(3)
    backward(3)
    uring.turn(0)
    oring.turn(0)
    compute(down_pieces[0])
    compute(down_pieces[1])
    add_core(down_pieces[0])
    backward(2)
    uring.turn(1)
    add_core(down_pieces[1])
    compute(down_pieces[2])
    backward(1)
    uring.turn(2)
    add_core(down_pieces[2])
    compute(down_pieces[3])
    backward(0)
    uring.turn(3)
    add_core(down_pieces[3])
    for i, p in enumerate(wide_pieces):
        compute(p)
        if i: add_core(wide_pieces[i - 1])
        if i == 0: oring.turn(1)
        if i == 3: uring.turn(4)
        if i == 4: oring.turn(2)
    add_core(wide_pieces[-1])
    for p in down_pieces: add_far(p)
    oring.turn(3)
    oring.turn(4)
    for kind, j, a in wide_pieces + down_pieces:
        cols = cols_of(j)
        if kind == 0:
            sent(r0g.at[a, :, :, :, :, cols], gs0.at[a, j], pc)
        else:
            sent(r0d.at[:, :, cols], ds0.at[j], pc)
            sent(r1d.at[:, cols], ds1.at[j], pc)
    for copy in saves: copy.wait()
    nring.finish()
    uring.finish()
    oring.finish()
    cring.finish()
    for d in range(1, deep): sent(own_kv, kz_s.at[d], pc)
    for d in range(deep): sent(own_kv, kx_s.at[d], pc)
    sent(down, d_far.at[0], pc)
    def left(t, v):
        sent(g_slot(0), g_sib.at[pc.far * n + t], pc)
        @pl.when(t > 0)
        def _():
            src = lax.rem(c + t, n)
            sent(g_slot(0), g_far.at[src], pc)
            sent(g_slot(0), g_sib.at[s * n + src], pc)
        return v
    lax.fori_loop(0, n, left, 0)
    sent(down, d_sib.at[s], pc)
    sent(down, d_sib.at[pc.far], pc)

def layer_call(n, length, x, og, qkv, gain_one, bias, gate, up, gain_two, down, outw, tables):
    N, m = 4 * n, n // 2
    rows, width = x.shape
    owned, piece = qkv.shape[0], down.shape[0]
    chunk = 4 * piece
    S, V = jax.ShapeDtypeStruct, pltpu.VMEM
    joint = QDIM + 2 * KVDIM + HEAD
    shapes = [S((2, 2, m, 2, owned, joint), BF), S((2, 2, m, 2, owned, width), BF), S((m, 2, rows, 2 * KVDIM), BF),
              S((HEADS, rows, HEAD), BF), S((2, 2, m, 2, owned, chunk), BF), S((piece, width), BF),
              S((rows, QDIM), BF), S((rows, width), F32), S((rows, width), F32), S((rows, width), F32)]
    anys = pl.BlockSpec(memory_space=pl.ANY)
    vmem = pl.BlockSpec(memory_space=pltpu.VMEM)
    all_rows = V((n, rows, width), BF)
    hidden = V((n, rows, chunk), BF)
    scratch = [V((2, N * owned, chunk), BF), V((4 * piece, width), BF), all_rows, all_rows, V((n, 2, rows // 2, chunk), BF), hidden, hidden,
               all_rows, V((2, rows, width // 2), BF), V((2, n // 2 - 1, rows, width), BF),
               all_rows, V((2, rows, width // 2), BF), V((2, n // 2 - 1, rows, width), BF),
               V((2, 2, 2, m, 2, owned, chunk), BF), V((2, 2, piece, width), BF), V((2, 2, m, 2, owned, chunk), BF),
               V((2, piece, width), BF), V((piece, width), BF),
               V((2, 2, m, 2, owned, width // 4), BF),
               V((m, 2, rows, 2 * KVDIM), BF), V((HEADS, rows, HEAD), BF), V((2, rows, HEAD), F32)]
    a, b = chunk // 384, width // 384
    scratch += [DMA((6,)), DMA((9,)), DMA((7, m + 5)), DMA((7, m + 5)), DMA((N,)), DMA((n,)), DMA((2,)), DMA((n,)), DMA((N,)),
                DMA((4,)), DMA((1,)), DMA((4,)), DMA((2, m)), DMA((2, m)), DMA((m,)), DMA((m,)), DMA((m,)), DMA((m,))]
    scratch += [DMA((2, m))] * 6 + [DMA((2, a))] * 3 + [DMA((b,))] * 5
    return pl.pallas_call(
        functools.partial(layer_kernel, n),
        out_shape=shapes,
        in_specs=[pl.BlockSpec(memory_space=pltpu.SMEM)] + [vmem] * 9 + [anys] * 2,
        out_specs=[anys] * 6 + [vmem] * 4,
        scratch_shapes=scratch,
        compiler_params=pltpu.CompilerParams(collective_id=0, has_side_effects=True, vmem_limit_bytes=63 * 2**20),
    )(length, x, og, qkv, gain_one, bias, gate, up, gain_two, down, outw, tables)


class Reduce:
    def __init__(self, pc, far_first, p, r0, r1, r2, r3, ss, rs, i):
        self.pc, self.far_first, self.p = pc, far_first, p
        self.r0, self.r1, self.r2, self.r3, self.ss, self.rs, self.i = r0, r1, r2, r3, ss, rs, i
        self.y, self.x, self.z = pc.s // 2, lax.rem(pc.c, 2), pc.c // 2
        self.xp = pc.c + 1 - 2 * self.x
    def go(self, k, src, dst, seq, ctx):
        send(src, dst, self.ss.at[self.i, k], self.rs.at[self.i, k], seq, ctx)
    def come(self, k, dst):
        arrived(dst, self.rs.at[self.i, k], self.pc)
    def stage0(self):
        pc = self.pc
        self.go(0, self.p.at[:, 1 - pc.core], self.r0, pc.sib, pc.c)
    def stage1(self):
        pc, r0 = self.pc, self.r0
        self.come(0, r0)
        r0[...] = add_low(r0[...], self.p[:, pc.core])
        if self.far_first: self.go(1, r0.at[1 - self.y], self.r1, pc.far, pc.c)
        else: self.go(1, r0.at[:, :, 1 - self.x], self.r1, pc.s, self.xp)
    def stage2(self):
        pc, r0, r1 = self.pc, self.r0, self.r1
        self.come(1, r1)
        if self.far_first:
            r1[...] = add_low(r1[...], r0[self.y])
            self.go(2, r1.at[:, 1 - self.x], self.r2, pc.s, self.xp)
        else:
            r1[...] = add_low(r1[...], r0[:, :, self.x])
            self.go(2, r1.at[1 - self.y], self.r2, pc.far, pc.c)
    def stage3(self):
        pc, r1, r2, n = self.pc, self.r1, self.r2, self.pc.n
        self.come(2, r2)
        r2[...] = add_low(r2[...], r1[:, self.x] if self.far_first else r1[self.y])
        def hand(d, w):
            to = lax.rem(self.z + d, n // 2)
            send(r2.at[to], self.r3.at[self.z], self.ss.at[self.i, 2 + d], self.rs.at[self.i, 2 + d], pc.s, 2 * to + self.x)
            return w
        lax.fori_loop(1, n // 2, hand, 0)
    def stage4(self):
        n = self.pc.n
        total = self.r2[self.z].astype(F32)
        for d in range(1, n // 2):
            src = lax.rem(self.z + n // 2 - d, n // 2)
            arrived(self.r3.at[src], self.rs.at[self.i, 2 + d], self.pc)
            total = total + self.r3[src].astype(F32)
        return total
    def finish(self):
        sent(self.r0, self.ss.at[self.i, 0], self.pc)
        sent(self.r1, self.ss.at[self.i, 1], self.pc)
        sent(self.r2, self.ss.at[self.i, 2], self.pc)
        for d in range(1, self.pc.n // 2):
            sent(self.r2.at[0], self.ss.at[self.i, 2 + d], self.pc)

def backward_kernel(n, length_ref, x_ref, og_ref, mid_ref, u_ref, o_ref, att_ref, q_ref, kv_ref, qkv_ref, out_ref, gate_ref, up_ref, gain_ref, tables, half_sum,
                    y_out, dx_out, dout_out, dqkv_out, dgate_out, dup_out, dgain_out,
                    tab_v, gm_v, gb_v, dm_v, gp_v, p_v, gs_v, dkv_v, kx, kz, raw_v, r1_v, mine_v, *rest):
    pieces = 6
    bufs, (local, kxs, kxr, kzs, kzr, gss, grs, fs, fr, ss, rs) = rest[: 5 * pieces], rest[5 * pieces :]
    pc = Place(n)
    s, c = pc.s, pc.c
    rows, width = x_ref.shape
    total = n * rows
    length = length_ref[0]
    x, z = lax.rem(c, 2), c // 2
    xp = c + 1 - 2 * x
    red = [Reduce(pc, i % 2 == 0, *bufs[5 * i : 5 * i + 5], ss, rs, i) for i in range(pieces)]
    tab = pltpu.make_async_copy(tables.at[:, pl.ds(pl.multiple_of(c * rows, rows), rows), :], tab_v, local.at[0])
    tab.start()
    y = s // 2
    mine = pltpu.make_async_copy(half_sum.at[:, y], mine_v, local.at[1])
    mine.start()
    enter(pc)
    owned = out_ref.shape[1]
    def cross(a):
        send(half_sum.at[a, 1 - y], r1_v.at[a], fs.at[a], fr.at[a], pc.far, c)
    def feed(a):
        arrived(r1_v.at[a], fr.at[a], pc)
        if a == 0:
            cross(1)
            mine.wait()
        r1_v[a] = add_low(r1_v[a], mine_v[a])
        def hand(d, w):
            to = lax.rem(c + d, n)
            send(r1_v.at[a, to // 2, lax.rem(to, 2)], raw_v.at[c, a], gss.at[a, to], grs.at[a, c], s, to)
            return w
        lax.fori_loop(1, n, hand, 0)
        raw_v[c, a] = r1_v[a, c // 2, lax.rem(c, 2)]
    def fed(a):
        def come(d, w):
            src = lax.rem(c + d, n)
            arrived(raw_v.at[src, a], grs.at[a, src], pc)
            return w
        lax.fori_loop(1, n, come, 0)
    cross(0)
    pos = c * rows + lax.broadcasted_iota(jnp.int32, (rows, width), 0)
    live = pos < length
    mid = mid_ref[...]
    gm = jnp.where(live, og_ref[...].astype(F32), 0.0) + rms_back(mid, inverse_rms(mid), u_ref[...])
    gm_v[...] = gm
    gb_v[...] = gm.astype(BF)
    y_out[...] = jnp.where(live, mid + o_ref[...], 0.0).astype(BF)
    owners = 4 * n
    def mix(j, w):
        weight = out_ref[pl.ds(j * 8, 8)].reshape(8 * owned, width)
        r = contract_cols(gb_v[...], weight).astype(BF)
        for k in range(8 * owned // HEAD):
            dm_v[j * (8 * owned // HEAD) + k] = r[:, k * HEAD : (k + 1) * HEAD]
        return w
    lax.fori_loop(0, owners // 8, mix, 0)
    gb = gb_v[...]
    for i in range(2):
        w = width // 2
        grad = contract_rows(att_ref[...], gb[:, i * w : (i + 1) * w])
        red[i].p[...] = grad.astype(BF).reshape(red[i].p.shape)
        red[i].stage0()
    tab.wait()
    tc, ts = tab_v[0], tab_v[1]

    at_row = c * rows + lax.broadcasted_iota(jnp.int32, (rows, total), 0)
    at_col = lax.broadcasted_iota(jnp.int32, (rows, total), 1)
    allowed = (at_col <= at_row) & (at_col < length)
    def group(g):
        key = kv_ref[:, :, g * HEAD : (g + 1) * HEAD].reshape(total, HEAD)
        val = kv_ref[:, :, KVDIM + g * HEAD : KVDIM + (g + 1) * HEAD].reshape(total, HEAD)
        def head(i, w):
            h = g * GROUP + i
            part = pl.ds(pl.multiple_of(i * rows, rows), rows)
            scores = jnp.where(allowed, contract_cols(q_ref[h], key) * SCALE, MASKED)
            e = jnp.exp(scores - jnp.max(scores, axis=1, keepdims=True))
            probs = e / jnp.sum(e, axis=1, keepdims=True)
            gprobs = contract_cols(dm_v[h], val)
            inner = jnp.sum(probs * gprobs, axis=1, keepdims=True)
            gs = (probs * (gprobs - inner)).astype(BF)
            p_v[part, :] = probs.astype(BF)
            gs_v[part, :] = gs
            dq = product(gs, key) * SCALE
            gp_v[:, pl.ds(pl.multiple_of(h * HEAD, HEAD), HEAD)] = (dq * tc - pltpu.roll(dq, HEAD // 2, 1) * ts).astype(BF)
            return w
        lax.fori_loop(0, GROUP, head, 0)
        mine = slice(g * GROUP, (g + 1) * GROUP)
        dk = contract_rows(gs_v[...], q_ref[mine].reshape(GROUP * rows, HEAD)) * SCALE
        dv = contract_rows(p_v[...], dm_v[mine].reshape(GROUP * rows, HEAD))
        lanes = slice(g * 2 * HEAD, g * 2 * HEAD + 2 * HEAD)
        dkv_v[:, :, :, lanes] = jnp.concatenate([dk, dv], 1).astype(BF).reshape(n // 2, 2, rows, 2 * HEAD)
        send(dkv_v.at[:, 1 - x, :, lanes], kx.at[:, :, lanes], kxs.at[g], kxr.at[g], s, xp)
    def kv_x(g):
        lanes = slice(g * 2 * HEAD, g * 2 * HEAD + 2 * HEAD)
        arrived(kx.at[:, :, lanes], kxr.at[g], pc)
        kx[:, :, lanes] = add_low(kx[:, :, lanes], dkv_v[:, x, :, lanes])
        for d in range(1, n // 2):
            to = lax.rem(z + d, n // 2)
            send(kx.at[to, :, lanes], kz.at[z, :, lanes], kzs.at[g, d], kzr.at[g, d], s, 2 * to + x)
    def kv_z(g):
        lanes = slice(g * 2 * HEAD, g * 2 * HEAD + 2 * HEAD)
        sumkv = kx[z, :, lanes].astype(F32)
        for d in range(1, n // 2):
            src = lax.rem(z + n // 2 - d, n // 2)
            arrived(kz.at[src, :, lanes], kzr.at[g, d], pc)
            sumkv = sumkv + kz[src, :, lanes].astype(F32)
        dk, dv = sumkv[:, :HEAD], sumkv[:, HEAD:]
        k0, v0 = QDIM + g * HEAD, QDIM + KVDIM + g * HEAD
        gp_v[:, k0 : k0 + HEAD] = (dk * tc - pltpu.roll(dk, HEAD // 2, 1) * ts).astype(BF)
        gp_v[:, v0 : v0 + HEAD] = dv.astype(BF)
    xin = x_ref[...].astype(F32)
    inverse = inverse_rms(xin)
    def joint(i, first, w):
        xh = (x_ref[...].astype(F32) * inverse).astype(BF)
        grad = contract_rows(xh, gp_v[:, first : first + w]).astype(BF)
        shape = red[i].p.shape[:-1] + (w,)
        red[i].p[..., :w] = grad.reshape(shape)
    group(0)
    red[0].stage1(); red[1].stage1()
    feed(0)
    group(1)
    kv_x(0)
    red[0].stage2(); red[1].stage2()
    third = QDIM // 3
    for i in range(3):
        joint(2 + i, i * third, third)
        red[2 + i].stage0()
        if i == 0: kv_x(1)
    red[0].stage3(); red[1].stage3()
    red[2].stage1(); red[3].stage1(); red[4].stage1()
    feed(1)
    kv_z(0); kv_z(1)
    joint(5, QDIM, 2 * KVDIM)
    sums = jnp.sum(gp_v[...].astype(F32), axis=0, keepdims=True)
    p5 = red[5].p
    qk_width = QDIM + KVDIM
    at = lax.broadcasted_iota(jnp.int32, (owned, HEAD), 0)
    for d in range(owners):
        tiles = (qk_width // owners * d // HEAD, qk_width // owners * d // HEAD + 1, (qk_width + KVDIM // owners * d) // HEAD)
        part = jnp.zeros((owned, HEAD), F32)
        for k, t in enumerate(tiles):
            part = jnp.where(at == k, sums[:, t * HEAD : t * HEAD + HEAD], part)
        plane = d // n
        p5[plane // 2, plane % 2, d % n // 2, d % 2, :, 2 * KVDIM :] = part.astype(BF)
    red[5].stage0()
    red[2].stage2(); red[3].stage2(); red[4].stage2()
    red[5].stage1()
    qk = QDIM + 2 * KVDIM
    gp = gp_v[...]
    def back(j, w):
        weight = qkv_ref[pl.ds(j * 8, 8), :, :qk].reshape(8 * owned, qk)
        cols = pl.ds(pl.multiple_of(j * 8 * owned, 8 * owned), 8 * owned)
        dx_out[:, cols] = contract_cols(gp, weight)
        return w
    lax.fori_loop(0, owners // 8, back, 0)
    red[2].stage3(); red[3].stage3(); red[4].stage3()
    red[5].stage2()
    fed(0)
    place_back(raw_v, 0, dgate_out)
    dx_out[...] = gm_v[...] + rms_back(x_ref[...].astype(F32), inverse, dx_out[...])
    for i in range(2):
        dout_out[:, i * (width // 2) : (i + 1) * (width // 2)] = red[i].stage4()
    red[5].stage3()
    fed(1)
    place_back(raw_v, 1, dup_out)
    gain = gain_ref[...]
    dgain_out[...] = jnp.sum(
        dgate_out[...] * gate_ref[...].astype(F32) + dup_out[...] * up_ref[...].astype(F32), axis=1, keepdims=True
    )
    dgate_out[...] = dgate_out[...] * gain
    dup_out[...] = dup_out[...] * gain
    for i in range(3):
        dqkv_out[:, i * third : (i + 1) * third] = red[2 + i].stage4()
    dqkv_out[:, QDIM:] = red[5].stage4()
    for r in red: r.finish()
    for a in range(2):
        sent(r1_v.at[a], fs.at[a], pc)
        def left(d, w):
            sent(raw_v.at[0, a], gss.at[a, lax.rem(c + d, n)], pc)
            return w
        lax.fori_loop(1, n, left, 0)
    for g in range(2):
        lanes = slice(g * 2 * HEAD, g * 2 * HEAD + 2 * HEAD)
        sent(kx.at[:, :, lanes], kxs.at[g], pc)
        for d in range(1, n // 2): sent(kx.at[0, :, lanes], kzs.at[g, d], pc)

def backward_call(n, length, x, og, mid, u, o, att, q, kv, qkv_all, out_all, gate, up, gain, tables, half_sum):
    S, V = jax.ShapeDtypeStruct, pltpu.VMEM
    rows, width = x.shape
    owned = qkv_all.shape[1]
    anys = pl.BlockSpec(memory_space=pl.ANY)
    vmem = pl.BlockSpec(memory_space=pltpu.VMEM)
    m = n // 2
    scratch = [V((2, rows, HEAD), F32), V((rows, width), F32), V((rows, width), BF), V((HEADS, rows, HEAD), BF),
               V((rows, QDIM + 2 * KVDIM), BF), V((GROUP * rows, n * rows), BF), V((GROUP * rows, n * rows), BF),
               V((m, 2, rows, 2 * KVDIM), BF), V((m, rows, 2 * KVDIM), BF), V((m, rows, 2 * KVDIM), BF),
               V((n, 2, owned, half_sum.shape[-1]), BF), V((2,) + half_sum.shape[2:], BF), V((2,) + half_sum.shape[2:], BF)]
    for i, w in enumerate((width // 2, width // 2, QDIM // 3, QDIM // 3, QDIM // 3, 2 * KVDIM + HEAD)):
        one = (m, 2, owned, w) if i % 2 == 0 else (2, m, owned, w)
        scratch += [V((2, 2, m, 2, owned, w), BF), V((2, m, 2, owned, w), BF), V(one, BF), V((m, owned, w), BF), V((m, owned, w), BF)]
    scratch += [DMA((2,)), DMA((2,)), DMA((2,)), DMA((2, m)), DMA((2, m)), DMA((2, n)), DMA((2, n)), DMA((2,)), DMA((2,)), DMA((6, 2 + m)), DMA((6, 2 + m))]
    return pl.pallas_call(
        functools.partial(backward_kernel, n),
        out_shape=[S((rows, width), BF), S((rows, width), F32), S((owned, width), F32), S((owned, qkv_all.shape[2]), F32),
                   S(gate.shape, F32), S(gate.shape, F32), S((owned, 1), F32)],
        in_specs=[pl.BlockSpec(memory_space=pltpu.SMEM)] + [vmem] * 13 + [anys] * 2,
        out_specs=[vmem] * 7,
        scratch_shapes=scratch,
        compiler_params=pltpu.CompilerParams(collective_id=2, has_side_effects=True, vmem_limit_bytes=62 * 2**20),
    )(length, x, og, mid, u, o, att, q, kv, qkv_all, out_all, gate, up, gain, tables, half_sum)


def kernel_shards(
    tokens,
    lengths,
    attn_gain,
    qkv_weight,
    qkv_bias,
    out_weight,
    mlp_gain,
    gate_weight,
    up_weight,
    down_weight,
    out_grad,
):
    seqs, parts = lax.axis_size("seq"), lax.axis_size("ctx")
    rows, width = tokens.shape[1:]
    owned = gate_weight.shape[0]
    piece = down_weight.shape[0]
    padded = -(-piece // 32) * 32
    owners = seqs * parts
    me = lax.axis_index("seq") * parts + lax.axis_index("ctx")
    gain_one = attn_gain.astype(F32)[:, None]
    gain_two = mlp_gain.astype(F32)[:, None]
    half = HEAD // 2
    frequency = np.float32(ROPE_BASE) ** (-np.arange(half, dtype=np.float32) * np.float32(2.0 / HEAD))
    angles = np.arange(rows * parts, dtype=np.float32)[:, None] * frequency.astype(np.float32)[None, :]
    cosine, sine = np.cos(angles), np.sin(angles)
    tables = jnp.asarray(np.stack([np.concatenate([cosine, cosine], 1), np.concatenate([-sine, sine], 1)]), F32)
    down = jnp.pad(down_weight, ((0, padded - piece), (0, 0)))
    x, og = tokens[0], out_grad[0]
    qkv_all, out_all, kv_all, q, half_sum, grad_down, att, mid, u, o = layer_call(
        parts, lengths, x, og, qkv_weight, gain_one, qkv_bias[None], gate_weight, up_weight, gain_two,
        down, out_weight, tables,
    )
    joint = qkv_all.shape[-1]
    output, grad_inputs, grad_out, raw_qkv, grad_gate, grad_up, grad_mlp_gain = backward_call(
        parts, lengths, x, og, mid, u, o, att, q, kv_all.reshape(parts, rows, 2 * KVDIM),
        qkv_all.reshape(owners, owned, joint), out_all.reshape(owners, owned, width),
        gate_weight, up_weight, gain_two, tables, half_sum,
    )
    qk = QDIM + 2 * KVDIM
    bias_rows, raw_qkv = raw_qkv[:3, qk:], raw_qkv[:, :qk]
    grad_attn_gain = jnp.sum(raw_qkv * qkv_weight.astype(F32), axis=1)
    per, per_value = (QDIM + KVDIM) // owners, KVDIM // owners
    grad_qk_bias = lax.dynamic_slice_in_dim(bias_rows[:2].reshape(2 * HEAD), lax.rem(per * me, HEAD), per)
    grad_value_bias = lax.dynamic_slice_in_dim(bias_rows[2], lax.rem(per_value * me, HEAD), per_value)
    return (
        output[None],
        grad_inputs.astype(BF)[None],
        grad_attn_gain,
        raw_qkv * gain_one,
        grad_qk_bias,
        grad_out,
        grad_mlp_gain[:, 0],
        grad_gate,
        grad_up,
        grad_down[:piece].astype(F32),
        grad_value_bias,
    )


def solution(mesh):
    seqs, parts = mesh.shape["seq"], mesh.shape["ctx"]
    tiled = seqs == 4 and parts == 8 and 1536 // (seqs * parts) % 16 == 0
    rows, vector = P(BOTH, None), P(BOTH)
    token = P("seq", "ctx", None)
    return jax.shard_map(
        kernel_shards if tiled else plain_shards,
        mesh=mesh,
        in_specs=(token, P("seq"), vector, rows, vector, rows, vector, rows, rows, rows, token),
        out_specs=(token, token, vector, rows, vector, rows, vector, rows, rows, rows, vector),
        check_vma=False,
    )
```

```python
import functools

import jax
import jax.numpy as jnp
import numpy as np
from jax import lax
from jax.experimental import pallas as pl
from jax.experimental.pallas import tpu as pltpu
from jax.sharding import PartitionSpec as P

HEADS = 12
KV_HEADS = 2
HEAD = 128
QDIM = 1536
KVDIM = 256
GROUP = HEADS // KV_HEADS

EPSILON = 1e-06
ROPE_BASE = 1000000.0
MASKED = -1e30
SCALE = HEAD ** (-0.5)
BF = jnp.bfloat16
F32 = jnp.float32
BOTH = ("seq", "ctx")


DMA = pltpu.SemaphoreType.DMA
MESH = pl.DeviceIdType.MESH


def product(left, right):
    return jnp.dot(left, right, preferred_element_type=F32)


def contract_rows(left, right):
    return lax.dot_general(left, right, (((0,), (0,)), ((), ())), preferred_element_type=F32)


def contract_cols(left, right):
    return lax.dot_general(left, right, (((1,), (1,)), ((), ())), preferred_element_type=F32)


def inverse_rms(values):
    return lax.rsqrt(jnp.mean(values * values, axis=-1, keepdims=True) + EPSILON)


def rms_back(values, inverse, scaled_grad):
    inner = jnp.mean(scaled_grad * values, axis=-1, keepdims=True)
    return inverse * scaled_grad - values * (inverse * inverse * inverse) * inner


def rope_tables(positions):
    half = HEAD // 2
    frequency = ROPE_BASE ** (-jnp.arange(half, dtype=F32) * 2.0 / HEAD)
    angles = positions.astype(F32)[:, None] * frequency[None, :]
    return jnp.cos(angles), jnp.sin(angles)


def rotate(values, cosine, sine):
    half = HEAD // 2
    first, second = values[..., :half], values[..., half:]
    cosine, sine = cosine[:, None, :], sine[:, None, :]
    return jnp.concatenate([first * cosine - second * sine, second * cosine + first * sine], -1)


def gather(values, axes):
    return lax.all_gather(values, axes, axis=0, tiled=True)


def scatter(values, axes):
    return lax.psum_scatter(values, axes, scatter_dimension=0, tiled=True)


def plain_shards(
    tokens,
    lengths,
    attn_gain,
    qkv_weight,
    qkv_bias,
    out_weight,
    mlp_gain,
    gate_weight,
    up_weight,
    down_weight,
    out_grad,
):
    seqs, parts = lax.axis_size("seq"), lax.axis_size("ctx")
    inputs = tokens[0].astype(F32)
    rows, width = inputs.shape
    owned, hidden = gate_weight.shape
    piece = down_weight.shape[0]
    chunk = hidden // parts
    length = lengths[0]
    positions = lax.axis_index("ctx") * rows + jnp.arange(rows, dtype=jnp.int32)
    living = (positions < length).astype(F32)[:, None]
    cosine, sine = rope_tables(positions)

    gain_one = attn_gain.astype(F32)[:, None]
    gain_two = mlp_gain.astype(F32)[:, None]
    qkv_all = gather((qkv_weight.astype(F32) * gain_one).astype(BF), BOTH)
    bias_all = gather(qkv_bias, BOTH).astype(F32)
    out_all = gather(out_weight, BOTH)

    def to_chunks(weight):
        scaled = (weight.astype(F32) * gain_two).astype(BF)
        return scaled.reshape(owned, seqs, parts, piece).transpose(2, 0, 1, 3)

    both = jnp.stack([to_chunks(gate_weight), to_chunks(up_weight)], axis=1)
    both = lax.all_to_all(both.reshape(parts, 2, owned, chunk), "ctx", 0, 0)
    both = lax.all_gather(both, "seq", axis=0)
    gate_chunk = both[:, :, 0].reshape(width, chunk)
    up_chunk = both[:, :, 1].reshape(width, chunk)
    down_chunk = gather(down_weight, "seq")
    cotangent = out_grad[0].astype(F32) * living
    cot_all = gather(cotangent.astype(BF), "ctx")

    inverse_one = inverse_rms(inputs)
    normed_one = (inputs * inverse_one).astype(BF)
    project = product(normed_one, qkv_all) + bias_all
    queries = rotate(project[:, :QDIM].reshape(rows, HEADS, HEAD), cosine, sine).astype(BF)
    own_keys = rotate(
        project[:, QDIM : QDIM + KVDIM].reshape(rows, KV_HEADS, HEAD), cosine, sine
    ).astype(BF)
    own_values = project[:, QDIM + KVDIM :].astype(BF).reshape(rows, KV_HEADS, HEAD)
    keys, values = gather(own_keys, "ctx"), gather(own_values, "ctx")
    key_pos = jnp.arange(rows * parts, dtype=jnp.int32)
    allowed = (key_pos[None, :] <= positions[:, None]) & (key_pos[None, :] < length)
    grouped = queries.reshape(rows, KV_HEADS, GROUP, HEAD)
    scores = jnp.einsum("qgha,kga->ghqk", grouped, keys, preferred_element_type=F32) * SCALE
    scores = jnp.where(allowed, scores, MASKED)
    largest = jnp.max(scores, axis=-1, keepdims=True)
    exponent = jnp.exp(scores - largest)
    summed = jnp.sum(exponent, axis=-1, keepdims=True)
    probs = exponent / summed
    probs_low = probs.astype(BF)
    attended = jnp.einsum("ghqk,kga->qgha", probs_low, values, preferred_element_type=F32)
    attended = attended.reshape(rows, QDIM).astype(BF)
    middle = inputs + product(attended, out_all)

    inverse_two = inverse_rms(middle)
    normed_two = gather((middle * inverse_two).astype(BF), "ctx")
    gate_pre = product(normed_two, gate_chunk)
    up_pre = product(normed_two, up_chunk)
    sig = jax.nn.sigmoid(gate_pre)
    activated = (gate_pre * sig * up_pre).astype(BF)
    grad_act = contract_cols(cot_all, down_chunk)
    grad_gate = (grad_act * up_pre * (sig + gate_pre * sig * (1.0 - sig))).astype(BF)
    grad_up = (grad_act * gate_pre * sig).astype(BF)
    scaled_two = contract_cols(grad_gate, gate_chunk) + contract_cols(grad_up, up_chunk)
    scaled_two = scatter(scaled_two.astype(BF), "ctx").astype(F32)
    branch = scatter(product(activated, down_chunk).astype(BF), "ctx").astype(F32)
    output = ((middle + branch) * living).astype(BF)
    grad_down = scatter(contract_rows(activated, cot_all).astype(BF), "seq").astype(F32)
    raw = jnp.stack([contract_rows(normed_two, grad_gate), contract_rows(normed_two, grad_up)], 1)
    raw = scatter(raw.astype(BF), "seq").reshape(parts, owned, 2, chunk)
    raw = lax.all_to_all(raw, "ctx", 0, 0).astype(F32)
    raw = raw.reshape(parts, owned, 2, seqs, piece).transpose(2, 1, 3, 0, 4)
    raw = raw.reshape(2, owned, hidden)
    grad_mlp_gain = jnp.sum(raw[0] * gate_weight.astype(F32) + raw[1] * up_weight.astype(F32), 1)

    grad_middle = cotangent + rms_back(middle, inverse_two, scaled_two)
    grad_branch = grad_middle.astype(BF)
    grad_out = scatter(contract_rows(attended, grad_branch).astype(BF), BOTH).astype(F32)
    grad_mixed = contract_cols(grad_branch, out_all).astype(BF)
    grad_mixed = grad_mixed.reshape(rows, KV_HEADS, GROUP, HEAD)
    grad_probs = jnp.einsum("qgha,kga->ghqk", grad_mixed, values, preferred_element_type=F32)
    inner = jnp.sum(probs * grad_probs, axis=-1, keepdims=True)
    grad_scores = (probs * (grad_probs - inner)).astype(BF)
    grad_q = jnp.einsum("ghqk,kga->qgha", grad_scores, keys, preferred_element_type=F32) * SCALE
    grad_k = jnp.einsum("ghqk,qgha->kga", grad_scores, grouped, preferred_element_type=F32) * SCALE
    grad_v = jnp.einsum("ghqk,qgha->kga", probs_low, grad_mixed, preferred_element_type=F32)
    grad_k = scatter(grad_k.astype(BF), "ctx").astype(F32)
    grad_v = scatter(grad_v.astype(BF), "ctx").astype(F32)
    grad_q = rotate(grad_q.reshape(rows, HEADS, HEAD), cosine, -sine).reshape(rows, QDIM)
    grad_k = rotate(grad_k, cosine, -sine).reshape(rows, KVDIM)
    grad_project = jnp.concatenate([grad_q, grad_k, grad_v.reshape(rows, KVDIM)], axis=1)
    grad_project = grad_project.astype(BF)
    raw_qkv = scatter(contract_rows(normed_one, grad_project).astype(BF), BOTH).astype(F32)
    grad_attn_gain = jnp.sum(raw_qkv * qkv_weight.astype(F32), axis=1)
    grad_bias = jnp.sum(grad_project.astype(F32), axis=0)
    qk_width = QDIM + KVDIM
    grad_qk_bias = scatter(grad_bias[:qk_width], BOTH)
    grad_value_bias = scatter(grad_bias[qk_width:], BOTH)
    scaled_one = contract_cols(grad_project, qkv_all)
    grad_inputs = (grad_middle + rms_back(inputs, inverse_one, scaled_one)).astype(BF)
    return (
        output[None],
        grad_inputs[None],
        grad_attn_gain,
        raw_qkv * gain_one,
        grad_qk_bias,
        grad_out,
        grad_mlp_gain,
        raw[0] * gain_two,
        raw[1] * gain_two,
        grad_down,
        grad_value_bias,
    )


class Place:
    def __init__(self, n):
        self.n = n
        self.s, self.c = lax.axis_index("seq"), lax.axis_index("ctx")
        self.me = self.s * n + self.c
        self.core = lax.rem(self.s, 2)
        self.sib = self.s + 1 - 2 * self.core
        self.far = lax.rem(self.s + 2, 4)
        half = self.c // 2
        self.pos = half + lax.rem(self.c, 2) * (n - 1 - 2 * half)
        self.nxt, self.prv = self.at(1), self.at(-1)
    def at(self, offset):
        p = lax.rem(self.pos + offset + 2 * self.n, self.n)
        return 2 * p + (p // (self.n // 2)) * (2 * self.n - 1 - 4 * p)

def send(src, dst, ssem, rsem, seq, ctx):
    copy = pltpu.make_async_remote_copy(src, dst, ssem, rsem, device_id=(seq, ctx), device_id_type=MESH)
    copy.start()

def arrived(dst, rsem, place):
    pltpu.make_async_remote_copy(dst, dst, rsem, rsem, device_id=(place.s, place.c), device_id_type=MESH).wait_recv()

def sent(src, ssem, place):
    pltpu.make_async_remote_copy(src, src, ssem, ssem, device_id=(place.s, place.c), device_id_type=MESH).wait_send()

def enter(place, whole_group=True):
    barrier = pltpu.get_barrier_semaphore()
    def greet(d, z):
        pl.semaphore_signal(barrier, inc=1, device_id=(place.s, lax.rem(place.c + d, place.n)), device_id_type=MESH)
        return z
    lax.fori_loop(1, place.n, greet, 0)
    pl.semaphore_signal(barrier, inc=1, device_id=(place.sib, place.c), device_id_type=MESH)
    pl.semaphore_signal(barrier, inc=1, device_id=(place.far, place.c), device_id_type=MESH)
    pl.semaphore_wait(barrier, place.n + 1)


def add_low(left, right):
    return (left.astype(F32) + right.astype(F32)).astype(BF)

def diagonal(n):
    return lax.broadcasted_iota(jnp.int32, (n, n), 0) == lax.broadcasted_iota(jnp.int32, (n, n), 1)

def column(row):
    return jnp.sum(jnp.where(diagonal(row.shape[1]), row.astype(F32), 0.0), axis=1, keepdims=True)

def as_row(values):
    return jnp.sum(jnp.where(diagonal(values.shape[0]), values, 0.0), axis=0, keepdims=True)

class RingGather:
    def __init__(self, pc, slots, ssem, rsem, index=None):
        self.pc, self.slots, self.ssem, self.rsem, self.index = pc, slots, ssem, rsem, index
        self.steps, self.half = pc.n // 2, slots.shape[2] // 2
        self.ways = ((0, -1, pc.nxt), (1, 1, pc.prv))
    def slot(self, offset):
        return self.index[offset] if self.index else self.pc.at(offset)
    def part(self, ref, f, t):
        return ref if t < self.steps - 1 else ref.at[:, pl.ds(f * self.half, self.half)]
    def hop(self, t, own=None):
        for f, sign, to in self.ways:
            src = self.slots.at[self.slot(sign * t)] if own is None else own
            there = self.slots.at[self.slot(sign * (t + 1) if self.index else sign * t)]
            send(self.part(src, f, t), self.part(there, f, t), self.ssem.at[f, t], self.rsem.at[f, t], self.pc.s, to)
    def turn(self, t):
        for f, sign, _ in self.ways:
            arrived(self.part(self.slots.at[self.slot(sign * (t + 1))], f, t), self.rsem.at[f, t], self.pc)
        if t + 1 < self.steps: self.hop(t + 1)
    def finish(self):
        for f in range(2):
            for t in range(self.steps): sent(self.part(self.slots.at[0], f, t), self.ssem.at[f, t], self.pc)

class RingSum:
    def __init__(self, pc, term, index, held_half, held, ssem, rsem, out):
        self.pc, self.term, self.index, self.out = pc, term, index, out
        self.held_half, self.held, self.ssem, self.rsem = held_half, held, ssem, rsem
        self.steps, self.half = pc.n // 2, term.shape[2] // 2
    def turn(self, t):
        pc, ahead = self.pc, self.steps - t
        for f, sign, to in ((0, 1, pc.nxt), (1, -1, pc.prv)):
            cols = slice(f * self.half, (f + 1) * self.half)
            i = self.index[sign * ahead]
            if t == 1:
                arrived(self.held_half.at[f], self.rsem.at[f, 0], pc)
                self.term[i, :, cols] = add_low(self.term[i, :, cols], self.held_half[f])
            elif t > 1:
                arrived(self.held.at[f, t - 2], self.rsem.at[f, t - 1], pc)
                if t < self.steps: self.term[i] = add_low(self.term[i], self.held[f, t - 2])
            if t == 0:
                src, dst = self.term.at[i, :, pl.ds(f * self.half, self.half)], self.held_half.at[f]
            elif t < self.steps:
                src, dst = self.term.at[i], self.held.at[f, t - 1]
            if t < self.steps: send(src, dst, self.ssem.at[f, t], self.rsem.at[f, t], pc.s, to)
        if t == self.steps:
            i = self.index[0]
            self.out[...] = self.term[i].astype(F32) + self.held[0, t - 2].astype(F32) + self.held[1, t - 2].astype(F32)
    def finish(self):
        for f in range(2):
            sent(self.held_half.at[f], self.ssem.at[f, 0], self.pc)
            for t in range(1, self.steps): sent(self.held.at[f, 0], self.ssem.at[f, t], self.pc)

class Spread:
    def __init__(self, pc, x_first, w, ss, rs, i):
        self.pc, self.x_first, self.w, self.ss, self.rs, self.i = pc, x_first, w, ss, rs, i
        self.y, self.x, self.z = pc.s // 2, lax.rem(pc.c, 2), pc.c // 2
        self.xp = pc.c + 1 - 2 * self.x
        self.deep = pc.n // 2
    def go(self, k, part, seq, ctx):
        send(part, part, self.ss.at[self.i, k], self.rs.at[self.i, k], seq, ctx)
    def come(self, k, part):
        arrived(part, self.rs.at[self.i, k], self.pc)
    def both(self, k, part, sib_k, seq, ctx, sib_part):
        self.go(k, part, seq, ctx)
        self.go(sib_k, sib_part, self.pc.sib, self.pc.c)
    def begin(self):
        own = self.w.at[self.y, self.pc.core, self.z, self.x]
        for d in range(1, self.deep):
            self.go(d - 1, own, self.pc.s, 2 * lax.rem(self.z + d, self.deep) + self.x)
    def stage1(self):
        pc, w, y, x = self.pc, self.w, self.y, self.x
        for d in range(1, self.deep):
            self.come(d - 1, w.at[y, pc.core, lax.rem(self.z + self.deep - d, self.deep), x])
        column = w.at[y, pc.core, :, x]
        if self.x_first: self.both(self.deep, column, self.deep + 2, pc.s, self.xp, column)
        else: self.both(self.deep, column, self.deep + 2, pc.far, pc.c, column)
    def stage2(self):
        pc, w, y, x = self.pc, self.w, self.y, self.x
        if self.x_first:
            new = w.at[y, pc.core, :, 1 - x]
            self.come(self.deep, new)
            self.both(self.deep + 1, w.at[y, pc.core], self.deep + 3, pc.far, pc.c, new)
        else:
            new = w.at[1 - y, pc.core, :, x]
            self.come(self.deep, new)
            self.both(self.deep + 1, w.at[:, pc.core, :, x], self.deep + 3, pc.s, self.xp, new)
    def stage3(self):
        pc, w, y, x = self.pc, self.w, self.y, self.x
        new = w.at[1 - y, pc.core] if self.x_first else w.at[:, pc.core, :, 1 - x]
        self.come(self.deep + 1, new)
        self.go(self.deep + 4, new, pc.sib, pc.c)
    def stage4(self):
        pc, w, y, x = self.pc, self.w, self.y, self.x
        other = 1 - pc.core
        self.come(self.deep + 2, w.at[y, other, :, x])
        self.come(self.deep + 3, w.at[y, other, :, 1 - x] if self.x_first else w.at[1 - y, other, :, x])
        self.come(self.deep + 4, w.at[1 - y, other] if self.x_first else w.at[:, other, :, 1 - x])
    def finish(self):
        w, four = self.w, self.w.at[0, 0, :, 0]
        eight = w.at[0, 0] if self.x_first else w.at[:, 0, :, 0]
        for d in range(1, self.deep): sent(w.at[0, 0, 0, 0], self.ss.at[self.i, d - 1], self.pc)
        for k, part in enumerate((four, eight, four, four, eight)): sent(part, self.ss.at[self.i, self.deep + k], self.pc)

def windows(n, piece, padded):
    for part in range(n):
        for plane in range(4):
            whole, packed = (plane * n + part) * piece, plane * padded
            first, packed_first = whole // 128 * 128, packed // 128 * 128
            span = -(-(whole + piece) // 128) * 128 - first
            packed_span = -(-(packed + piece) // 128) * 128 - packed_first
            yield part, whole - first, packed - packed_first, first, span, packed_first, packed_span

def shift_lanes(block, span, shift):
    if block.shape[1] < span:
        block = jnp.concatenate([block, jnp.zeros((block.shape[0], span - block.shape[1]), block.dtype)], 1)
    shift = shift % block.shape[1]
    return pltpu.roll(block, shift, 1) if shift else block

def place_back(raw, a, out):
    n, _, owned, chunk = raw.shape
    piece, padded = out.shape[1] // (4 * n), chunk // 4
    for part, at, packed_at, first, span, packed_first, packed_span in windows(n, piece, padded):
        block = raw[part, a, :, packed_first : packed_first + packed_span].astype(F32)
        block = shift_lanes(block, span, at - packed_at)[:, :span]
        lane = lax.broadcasted_iota(jnp.int32, block.shape, 1)
        here = (lane >= at) & (lane < at + piece)
        out[:, first : first + span] = jnp.where(here, block, out[:, first : first + span])

def place_out(weight, gain, a, packs):
    n, _, _, chunk = packs.shape
    owned = weight.shape[0]
    piece, padded = weight.shape[1] // (4 * n), chunk // 4
    for part in range(n): packs[part, a, :owned] = jnp.zeros((owned, chunk), BF)
    for part, at, packed_at, first, span, packed_first, packed_span in windows(n, piece, padded):
        block = weight[:, first : first + span].astype(F32) * gain
        block = shift_lanes(block, packed_span, packed_at - at)[:, :packed_span]
        lane = lax.broadcasted_iota(jnp.int32, block.shape, 1)
        here = (lane >= packed_at) & (lane < packed_at + piece)
        before = packs[part, a, :owned, packed_first : packed_first + packed_span].astype(F32)
        packs[part, a, :owned, packed_first : packed_first + packed_span] = jnp.where(here, block, before).astype(BF)


def rope(values, table_c, table_s):
    return values * table_c + pltpu.roll(values, HEAD // 2, 1) * table_s

def layer_kernel(n, length_ref, x_ref, og_ref, qw_ref, g1_ref, b_ref, gate_ref, up_ref, g2_ref, down, outw, tables,
                 qkv_all, out_all, kv_all, q_out, half_sum, dsum, att_out, mid_out, u_own, o_own,
                 gu_v, down_v, cot_v, n2_v, act_v, gg_v, gp_v, ut, uhh, uh, ot, ohh, oh, dgu_v, dd_v, r0g, r0d, r1d, w_o2,
                 kv_v, q_v, tab_v,
                 local, save, ss, rs, g_recv, g_send, g_own, g_far, g_sib, d_recv, d_far, d_sib, c_recv, c_send,
                 kz_s, kz_r, kx_s, kx_r, n_recv, n_send, u_recv, u_send, o_recv_, o_send_, gs0, gr0, gsave, ds0, dr0, ds1, dr1, dsave):
    pc = Place(n)
    me, s, c = pc.me, pc.s, pc.c
    y, x, z, xp = s // 2, lax.rem(c, 2), c // 2, c + 1 - 2 * lax.rem(c, 2)
    rows, width = x_ref.shape
    owned, piece = qw_ref.shape[0], down_v.shape[0] // 4
    length = length_ref[0]
    third, owners, deep = QDIM // 3, 4 * n, n // 2

    def g_slot(i): return gu_v.at[:, pl.ds(pl.multiple_of(i * owned, owned), owned), :]
    def pack(i): return act_v.at[i, :, pl.ds(0, owned), :]
    def d_slot(i): return down_v.at[pl.ds(pl.multiple_of(i * piece, piece), piece), :]

    kvw = 2 * KVDIM + HEAD
    def cut(ref, first, w): return ref.at[:, :, :, :, :, pl.ds(first, w)]
    w_kv = cut(dgu_v.at[0], 0, kvw)
    wide = (w_kv, cut(dgu_v.at[0], kvw, third), cut(dgu_v.at[1], 0, third), cut(dgu_v.at[1], third, third),
            cut(r0g, 0, width // 2), cut(r0g, width // 2, width // 4), w_o2)
    spreads = [Spread(pc, i % 2 == 0, w, ss, rs, i) for i, w in enumerate(wide)]
    kvs, q0, q1, q2, o0, o1, o2 = spreads
    outs = ((o0, 0, width // 2), (o1, width // 2, width // 4), (o2, width // 4 * 3, width // 4))
    pairs = n // 2
    offsets = [o for j in range(1, pairs) for o in (-j, j)] + [pairs, 0]
    index = {o: i for i, o in enumerate(offsets)}
    index[-pairs] = index[pairs]
    cring = RingGather(pc, cot_v, c_send, c_recv, index)
    nring = RingGather(pc, n2_v, n_send, n_recv, index)
    uring = RingSum(pc, ut, index, uhh, uh, u_send, u_recv, u_own)
    oring = RingSum(pc, ot, index, ohh, oh, o_send_, o_recv_, o_own)
    lc = [pltpu.make_async_copy(a, b, local.at[i]) for i, (a, b) in enumerate((
        (outw.at[:, pl.ds(0, width // 2)], wide[4].at[y, pc.core, z, x]), (outw.at[:, pl.ds(width // 2, width // 4)], wide[5].at[y, pc.core, z, x]),
        (outw.at[:, pl.ds(width // 4 * 3, width // 4)], w_o2.at[y, pc.core, z, x]), (tables.at[:, pl.ds(pl.multiple_of(c * rows, rows), rows), :], tab_v)))]
    for copy in lc: copy.start()
    g1 = column(g1_ref[...])
    def scaled(first, w): return (qw_ref[:, first : first + w].astype(F32) * g1).astype(BF)
    w_kv[y, pc.core, z, x, :, : 2 * KVDIM] = scaled(QDIM, 2 * KVDIM)
    share = b_ref.shape[1]
    bias = b_ref[...].astype(F32)
    rest = jnp.zeros((1, HEAD - share), F32)
    odd = lax.rem(me, 2) == 1
    row = jnp.where(odd, jnp.concatenate([rest, bias], 1), jnp.concatenate([bias, rest], 1))
    first_row = lax.broadcasted_iota(jnp.int32, (owned, HEAD), 0) == 0
    w_kv[y, pc.core, z, x, :, 2 * KVDIM :] = jnp.where(first_row, row, 0.0).astype(BF)
    for i, w in enumerate(wide[1:4]): w[y, pc.core, z, x] = scaled(i * third, third)
    slot_pos = c * rows + lax.broadcasted_iota(jnp.int32, (rows, width), 0)
    cot_v[index[0]] = jnp.where(slot_pos < length, og_ref[...].astype(F32), 0.0).astype(BF)
    g2 = column(g2_ref[...])
    place_out(gate_ref, g2, 0, act_v)
    place_out(up_ref, g2, 1, act_v)
    short = down[...].astype(F32)
    padding = jnp.zeros((piece - short.shape[0], width), F32)
    down_v[pl.ds(pl.multiple_of(s * piece, piece), piece), :] = jnp.concatenate([short, padding], 0).astype(BF)
    enter(pc)
    def gu_turn(t):
        k = s * n + lax.rem(c + n - t, n)
        arrived(g_slot(k), g_recv.at[k], pc)
        send(g_slot(k), g_slot(k), g_far.at[lax.rem(c + n - t, n)], g_recv.at[k], pc.far, c)
        send(g_slot(k), g_slot(k), g_sib.at[k], g_recv.at[k], pc.sib, c)
    for p in (kvs, q0, q1, q2): p.begin()
    own_gu = pltpu.make_async_copy(pack(c), g_slot(me), local.at[5])
    own_gu.start()
    def feed(d, v):
        to = lax.rem(c + d, n)
        send(pack(to), g_slot(me), g_send.at[to], g_recv.at[me], s, to)
        return v
    lax.fori_loop(1, n, feed, 0)
    send(d_slot(s), d_slot(s), d_far.at[0], d_recv.at[s], pc.far, c)
    send(d_slot(s), d_slot(s), d_sib.at[s], d_recv.at[s], pc.sib, c)
    xf = x_ref[...].astype(F32)
    att_out[...] = (xf * inverse_rms(xf)).astype(BF)
    kvs.stage1()
    q0.stage1()
    q1.stage1()
    kvs.stage2()
    q2.stage1()
    q0.stage2()
    kvs.stage3()
    q1.stage2()
    for copy in lc[:3]: copy.wait()
    o0.begin(); o1.begin(); o2.begin()
    q2.stage2()
    q0.stage3()
    q1.stage3()
    q2.stage3()
    send(pack(c), g_slot(me), g_own.at[0], g_recv.at[me], pc.far, c)
    send(pack(c), g_slot(me), g_own.at[1], g_recv.at[me], pc.sib, c)
    kvs.stage4()
    lc[3].wait()
    tc, ts = tab_v[0], tab_v[1]
    xh = att_out[...]
    def bias_of(tile):
        d = 2 * tile
        def part(i):
            plane, place = i // n, i % n
            return w_kv[plane // 2, plane % 2, place // 2, place % 2, 0:1, 2 * KVDIM :].astype(F32)
        return part(d) + part(d + 1)
    kv = product(xh, w_kv[..., : 2 * KVDIM].reshape(owners * owned, 2 * KVDIM))
    for k in range(2 * KV_HEADS):
        lanes = slice(k * HEAD, (k + 1) * HEAD)
        one = kv[:, lanes] + bias_of(QDIM // HEAD + k)
        kv_v[z, x, :, lanes] = (rope(one, tc, ts) if k < KV_HEADS else one).astype(BF)
    own_kv = kv_v.at[z, x]
    for d in range(1, deep):
        send(own_kv, own_kv, kz_s.at[d], kz_r.at[d], s, 2 * lax.rem(z + d, deep) + x)
    send(own_kv, own_kv, kx_s.at[0], kx_r.at[0], s, xp)
    o0.stage1(); o1.stage1(); o2.stage1()
    for i, p in enumerate((q0, q1, q2)):
        p.stage4()
        r = product(xh, p.w[...].reshape(owners * owned, third))
        for k in range(third // HEAD):
            h = i * (third // HEAD) + k
            q_v[h] = rope(r[:, k * HEAD : (k + 1) * HEAD] + bias_of(h), tc, ts).astype(BF)
    for d in range(1, deep):
        block = kv_v.at[lax.rem(z + deep - d, deep), x]
        arrived(block, kz_r.at[d], pc)
        send(block, block, kx_s.at[d], kx_r.at[d], s, xp)
    cring.hop(0)
    o0.stage2(); o1.stage2(); o2.stage2()
    saves = [pltpu.make_async_copy(q_v, q_out, save.at[0])]
    for i, (p, first) in enumerate(((kvs, QDIM), (q0, 0), (q1, third), (q2, 2 * third))):
        saves.append(pltpu.make_async_copy(p.w, qkv_all.at[:, :, :, :, :, pl.ds(first, p.w.shape[5])], save.at[1 + i]))
    for copy in saves: copy.start()
    for d in range(deep):
        arrived(kv_v.at[lax.rem(z + deep - d, deep), 1 - x], kx_r.at[d], pc)

    total = n * rows
    at_row = c * rows + lax.broadcasted_iota(jnp.int32, (rows, total), 0)
    at_col = lax.broadcasted_iota(jnp.int32, (rows, total), 1)
    allowed = (at_col <= at_row) & (at_col < length)
    def heads(first, count):
        def head(h, v):
            col = pl.multiple_of(h // GROUP * HEAD, HEAD)
            key = kv_v[:, :, :, pl.ds(col, HEAD)].reshape(total, HEAD)
            val = kv_v[:, :, :, pl.ds(pl.multiple_of(KVDIM + col, HEAD), HEAD)].reshape(total, HEAD)
            scores = jnp.where(allowed, contract_cols(q_v[h], key) * SCALE, MASKED)
            e = jnp.exp(scores - jnp.max(scores, axis=1, keepdims=True))
            probs = (e / jnp.sum(e, axis=1, keepdims=True)).astype(BF)
            att_out[:, pl.ds(pl.multiple_of(h * HEAD, HEAD), HEAD)] = product(probs, val).astype(BF)
            return v
        lax.fori_loop(first, first + count, head, 0)
    gu_turn(1); gu_turn(2)
    o0.stage3(); o1.stage3(); o2.stage3()
    heads(0, GROUP)
    gu_turn(3); gu_turn(4)
    cring.turn(0)
    heads(GROUP, GROUP)
    gu_turn(5); gu_turn(6)
    own_gu.wait()
    for i in range(2): sent(pack(0), g_own.at[i], pc)
    def fed(d, v):
        sent(pack(0), g_send.at[lax.rem(c + d, n)], pc)
        return v
    lax.fori_loop(1, n, fed, 0)
    gu_turn(7)
    o0.stage4(); o1.stage4(); o2.stage4()
    saves2 = [pltpu.make_async_copy(kv_v, kv_all, save.at[5])]
    for i, (p, first, w) in enumerate(outs):
        saves2.append(pltpu.make_async_copy(p.w, out_all.at[:, :, :, :, :, pl.ds(first, w)], save.at[6 + i]))
    for copy in saves2: copy.start()
    cring.turn(1)
    att = att_out[...]
    for p, first, w in outs:
        lanes = slice(first, first + w)
        mid_out[:, lanes] = x_ref[:, lanes].astype(F32) + product(att, p.w[...].reshape(owners * owned, w))
    mid = mid_out[...]
    n2_v[index[0]] = (mid * inverse_rms(mid)).astype(BF)
    nring.hop(0)
    cring.turn(2)
    arrived(d_slot(pc.far), d_recv.at[pc.far], pc)
    send(d_slot(pc.far), d_slot(pc.far), d_sib.at[pc.far], d_recv.at[pc.far], pc.sib, c)
    def across(t):
        k = pc.far * n + lax.rem(c + n - t, n)
        arrived(g_slot(k), g_recv.at[k], pc)
        send(g_slot(k), g_slot(k), g_sib.at[k], g_recv.at[k], pc.sib, c)
    for t in range(n):
        if t == n - 1:
            for copy in saves + saves2: copy.wait()
            for p in spreads: p.finish()
        across(t)
        if t == 1: nring.turn(0)
        if t == 3: cring.turn(3)
        if t == 4: nring.turn(1)
    for plane in range(2):
        other = 2 * plane + 1 - pc.core
        arrived(d_slot(other), d_recv.at[other], pc)
        def come(t, v):
            i = other * n + t
            arrived(g_slot(i), g_recv.at[i], pc)
            return v
        lax.fori_loop(0, n, come, 0)
    tall, chunk = 2 * rows, gu_v.shape[2]
    def forward(j):
        pair = slice(2 * j, 2 * j + 2)
        normed = n2_v[pair].reshape(tall, width)
        gate = product(normed, gu_v[0])
        up = product(normed, gu_v[1])
        sig = jax.nn.sigmoid(gate)
        gs = gate * sig
        act = (gs * up).astype(BF)
        act_v[pair] = act.reshape(2, 2, rows // 2, chunk)
        gp_v[pair] = gs.astype(BF).reshape(2, rows, chunk)
        gg_v[pair] = (up * (sig + gs * (1.0 - sig))).astype(BF).reshape(2, rows, chunk)
        ot[pair] = product(act, down_v[...]).astype(BF).reshape(2, rows, width)
    def backward(j):
        pair = slice(2 * j, 2 * j + 2)
        grad = contract_cols(cot_v[pair].reshape(tall, width), down_v[...])
        gg = (grad * gg_v[pair].reshape(tall, chunk).astype(F32)).astype(BF)
        gp = (grad * gp_v[pair].reshape(tall, chunk).astype(F32)).astype(BF)
        gg_v[pair] = gg.reshape(2, rows, chunk)
        gp_v[pair] = gp.reshape(2, rows, chunk)
        ut[pair] = (contract_cols(gg, gu_v[0]) + contract_cols(gp, gu_v[1])).astype(BF).reshape(2, rows, width)

    all_rows = n * rows
    plane = n * owned
    core = pc.core
    tile = 384
    def cols_of(j): return pl.ds(j * tile, tile)
    wide_pieces = [(0, j, a) for j in range(chunk // tile) for a in range(2)]
    down_pieces = [(1, j, 0) for j in range(width // tile)]
    def compute(p):
        kind, j, a = p
        if kind == 0:
            lhs, rhs = n2_v[...].reshape(all_rows, width), (gg_v, gp_v)[a]
            grad = contract_rows(lhs, rhs[:, :, cols_of(j)].reshape(all_rows, tile))
            dgu_v[a, :, :, :, :, :, cols_of(j)] = grad.astype(BF).reshape(2, 2, deep, 2, owned, tile)
            send(dgu_v.at[a, :, 1 - core, :, :, :, cols_of(j)], r0g.at[a, :, :, :, :, cols_of(j)],
                 gs0.at[a, j], gr0.at[a, j], pc.sib, c)
        else:
            grad = contract_rows(act_v[...].reshape(all_rows, chunk), cot_v[:, :, cols_of(j)].reshape(all_rows, tile))
            dd_v[:, :, :, cols_of(j)] = grad.astype(BF).reshape(2, 2, piece, tile)
            send(dd_v.at[:, 1 - core, :, cols_of(j)], r0d.at[:, :, cols_of(j)], ds0.at[j], dr0.at[j], pc.sib, c)
    def add_core(p):
        kind, j, a = p
        cols = cols_of(j)
        if kind == 0:
            arrived(r0g.at[a, :, :, :, :, cols], gr0.at[a, j], pc)
            for k in range(2):
                r0g[a, k, :, :, :, cols] = add_low(r0g[a, k, :, :, :, cols], dgu_v[a, k, core, :, :, :, cols])
            copy = pltpu.make_async_copy(r0g.at[a, :, :, :, :, cols], half_sum.at[a, :, :, :, :, cols], gsave.at[a, j])
            copy.start()
            saves.append(copy)
        else:
            arrived(r0d.at[:, :, cols], dr0.at[j], pc)
            for k in range(2):
                r0d[k, :, cols] = add_low(r0d[k, :, cols], dd_v[k, core, :, cols])
            send(r0d.at[1 - y, :, cols], r1d.at[:, cols], ds1.at[j], dr1.at[j], pc.far, c)
    def add_far(p):
        _, j, _ = p
        cols = cols_of(j)
        arrived(r1d.at[:, cols], dr1.at[j], pc)
        r1d[:, cols] = add_low(r1d[:, cols], r0d[y, :, cols])
        copy = pltpu.make_async_copy(r1d.at[:, cols], dsum.at[:, cols], dsave.at[j])
        copy.start()
        saves.append(copy)
    saves.clear()
    forward(0)
    nring.turn(2)
    forward(1)
    nring.turn(3)
    forward(2)
    forward(3)
    backward(3)
    uring.turn(0)
    oring.turn(0)
    compute(down_pieces[0])
    compute(down_pieces[1])
    add_core(down_pieces[0])
    backward(2)
    uring.turn(1)
    add_core(down_pieces[1])
    compute(down_pieces[2])
    backward(1)
    uring.turn(2)
    add_core(down_pieces[2])
    compute(down_pieces[3])
    backward(0)
    uring.turn(3)
    add_core(down_pieces[3])
    for i, p in enumerate(wide_pieces):
        compute(p)
        if i: add_core(wide_pieces[i - 1])
        if i == 0: oring.turn(1)
        if i == 3: uring.turn(4)
        if i == 4: oring.turn(2)
    add_core(wide_pieces[-1])
    for p in down_pieces: add_far(p)
    oring.turn(3)
    oring.turn(4)
    for kind, j, a in wide_pieces + down_pieces:
        cols = cols_of(j)
        if kind == 0:
            sent(r0g.at[a, :, :, :, :, cols], gs0.at[a, j], pc)
        else:
            sent(r0d.at[:, :, cols], ds0.at[j], pc)
            sent(r1d.at[:, cols], ds1.at[j], pc)
    for copy in saves: copy.wait()
    nring.finish()
    uring.finish()
    oring.finish()
    cring.finish()
    for d in range(1, deep): sent(own_kv, kz_s.at[d], pc)
    for d in range(deep): sent(own_kv, kx_s.at[d], pc)
    sent(d_slot(0), d_far.at[0], pc)
    def left(t, v):
        sent(g_slot(0), g_sib.at[pc.far * n + t], pc)
        @pl.when(t > 0)
        def _():
            src = lax.rem(c + t, n)
            sent(g_slot(0), g_far.at[src], pc)
            sent(g_slot(0), g_sib.at[s * n + src], pc)
        return v
    lax.fori_loop(0, n, left, 0)
    sent(d_slot(0), d_sib.at[s], pc)
    sent(d_slot(0), d_sib.at[pc.far], pc)

def layer_call(n, length, x, og, qkv, gain_one, bias, gate, up, gain_two, down, outw, tables):
    N, m = 4 * n, n // 2
    rows, width = x.shape
    owned, piece = qkv.shape[0], -(-down.shape[0] // 32) * 32
    chunk = 4 * piece
    S, V = jax.ShapeDtypeStruct, pltpu.VMEM
    joint = QDIM + 2 * KVDIM + HEAD
    shapes = [S((2, 2, m, 2, owned, joint), BF), S((2, 2, m, 2, owned, width), BF), S((m, 2, rows, 2 * KVDIM), BF),
              S((HEADS, rows, HEAD), BF), S((2, 2, m, 2, owned, chunk), BF), S((piece, width), BF),
              S((rows, QDIM), BF), S((rows, width), F32), S((rows, width), F32), S((rows, width), F32)]
    anys = pl.BlockSpec(memory_space=pl.ANY)
    vmem = pl.BlockSpec(memory_space=pltpu.VMEM)
    all_rows = V((n, rows, width), BF)
    hidden = V((n, rows, chunk), BF)
    scratch = [V((2, N * owned, chunk), BF), V((4 * piece, width), BF), all_rows, all_rows, V((n, 2, rows // 2, chunk), BF), hidden, hidden,
               all_rows, V((2, rows, width // 2), BF), V((2, n // 2 - 1, rows, width), BF),
               all_rows, V((2, rows, width // 2), BF), V((2, n // 2 - 1, rows, width), BF),
               V((2, 2, 2, m, 2, owned, chunk), BF), V((2, 2, piece, width), BF), V((2, 2, m, 2, owned, chunk), BF),
               V((2, piece, width), BF), V((piece, width), BF),
               V((2, 2, m, 2, owned, width // 4), BF),
               V((m, 2, rows, 2 * KVDIM), BF), V((HEADS, rows, HEAD), BF), V((2, rows, HEAD), F32)]
    a, b = chunk // 384, width // 384
    scratch += [DMA((6,)), DMA((9,)), DMA((7, m + 5)), DMA((7, m + 5)), DMA((N,)), DMA((n,)), DMA((2,)), DMA((n,)), DMA((N,)),
                DMA((4,)), DMA((1,)), DMA((4,)), DMA((2, m)), DMA((2, m)), DMA((m,)), DMA((m,)), DMA((m,)), DMA((m,))]
    scratch += [DMA((2, m))] * 6 + [DMA((2, a))] * 3 + [DMA((b,))] * 5
    return pl.pallas_call(
        functools.partial(layer_kernel, n),
        out_shape=shapes,
        in_specs=[pl.BlockSpec(memory_space=pltpu.SMEM)] + [vmem] * 9 + [anys] * 2,
        out_specs=[anys] * 6 + [vmem] * 4,
        scratch_shapes=scratch,
        compiler_params=pltpu.CompilerParams(collective_id=0, has_side_effects=True, vmem_limit_bytes=63 * 2**20),
    )(length, x, og, qkv, gain_one, bias, gate, up, gain_two, down, outw, tables)


class Reduce:
    def __init__(self, pc, far_first, p, r0, r1, r2, r3, ss, rs, i):
        self.pc, self.far_first, self.p = pc, far_first, p
        self.r0, self.r1, self.r2, self.r3, self.ss, self.rs, self.i = r0, r1, r2, r3, ss, rs, i
        self.y, self.x, self.z = pc.s // 2, lax.rem(pc.c, 2), pc.c // 2
        self.xp = pc.c + 1 - 2 * self.x
    def go(self, k, src, dst, seq, ctx):
        send(src, dst, self.ss.at[self.i, k], self.rs.at[self.i, k], seq, ctx)
    def come(self, k, dst):
        arrived(dst, self.rs.at[self.i, k], self.pc)
    def stage0(self):
        pc = self.pc
        self.go(0, self.p.at[:, 1 - pc.core], self.r0, pc.sib, pc.c)
    def stage1(self):
        pc, r0 = self.pc, self.r0
        self.come(0, r0)
        r0[...] = add_low(r0[...], self.p[:, pc.core])
        if self.far_first: self.go(1, r0.at[1 - self.y], self.r1, pc.far, pc.c)
        else: self.go(1, r0.at[:, :, 1 - self.x], self.r1, pc.s, self.xp)
    def stage2(self):
        pc, r0, r1 = self.pc, self.r0, self.r1
        self.come(1, r1)
        if self.far_first:
            r1[...] = add_low(r1[...], r0[self.y])
            self.go(2, r1.at[:, 1 - self.x], self.r2, pc.s, self.xp)
        else:
            r1[...] = add_low(r1[...], r0[:, :, self.x])
            self.go(2, r1.at[1 - self.y], self.r2, pc.far, pc.c)
    def stage3(self):
        pc, r1, r2, n = self.pc, self.r1, self.r2, self.pc.n
        self.come(2, r2)
        r2[...] = add_low(r2[...], r1[:, self.x] if self.far_first else r1[self.y])
        def hand(d, w):
            to = lax.rem(self.z + d, n // 2)
            send(r2.at[to], self.r3.at[self.z], self.ss.at[self.i, 2 + d], self.rs.at[self.i, 2 + d], pc.s, 2 * to + self.x)
            return w
        lax.fori_loop(1, n // 2, hand, 0)
    def stage4(self):
        n = self.pc.n
        total = self.r2[self.z].astype(F32)
        for d in range(1, n // 2):
            src = lax.rem(self.z + n // 2 - d, n // 2)
            arrived(self.r3.at[src], self.rs.at[self.i, 2 + d], self.pc)
            total = total + self.r3[src].astype(F32)
        return total
    def finish(self):
        sent(self.r0, self.ss.at[self.i, 0], self.pc)
        sent(self.r1, self.ss.at[self.i, 1], self.pc)
        sent(self.r2, self.ss.at[self.i, 2], self.pc)
        for d in range(1, self.pc.n // 2):
            sent(self.r2.at[0], self.ss.at[self.i, 2 + d], self.pc)

def backward_kernel(n, length_ref, x_ref, og_ref, mid_ref, u_ref, o_ref, att_ref, q_ref, kv_ref, out_ref, gate_ref, up_ref, qw_ref, gain_ref, gain_one_ref, qkv_all, tables, half_sum,
                    y_out, dx_out, dout_out, dqkv_out, dbias_out, dgate_out, dup_out, dgain_out, dgain_one_out,
                    tab_v, gm_v, gb_v, dm_v, gp_v, p_v, gs_v, dkv_v, kx, kz, raw_v, r1_v, mine_v, dx_v, qkv_v, *rest):
    pieces = 6
    bufs, (local, kxs, kxr, kzs, kzr, gss, grs, fs, fr, ss, rs) = rest[: 5 * pieces], rest[5 * pieces :]
    pc = Place(n)
    s, c = pc.s, pc.c
    rows, width = x_ref.shape
    total = n * rows
    length = length_ref[0]
    x, z = lax.rem(c, 2), c // 2
    xp = c + 1 - 2 * x
    red = [Reduce(pc, i % 2 == 0, *bufs[5 * i : 5 * i + 5], ss, rs, i) for i in range(pieces)]
    tab = pltpu.make_async_copy(tables.at[:, pl.ds(pl.multiple_of(c * rows, rows), rows), :], tab_v, local.at[0])
    tab.start()
    y = s // 2
    mine = pltpu.make_async_copy(half_sum.at[:, y], mine_v, local.at[1])
    mine.start()
    weights = pltpu.make_async_copy(qkv_all, qkv_v, local.at[2])
    weights.start()
    enter(pc)
    owned = out_ref.shape[1]
    def cross(a):
        send(half_sum.at[a, 1 - y], r1_v.at[a], fs.at[a], fr.at[a], pc.far, c)
    def feed(a):
        arrived(r1_v.at[a], fr.at[a], pc)
        if a == 0:
            cross(1)
            mine.wait()
        r1_v[a] = add_low(r1_v[a], mine_v[a])
        def hand(d, w):
            to = lax.rem(c + d, n)
            send(r1_v.at[a, to // 2, lax.rem(to, 2)], raw_v.at[c, a], gss.at[a, to], grs.at[a, c], s, to)
            return w
        lax.fori_loop(1, n, hand, 0)
        raw_v[c, a] = r1_v[a, c // 2, lax.rem(c, 2)]
    def fed(a):
        def come(d, w):
            src = lax.rem(c + d, n)
            arrived(raw_v.at[src, a], grs.at[a, src], pc)
            return w
        lax.fori_loop(1, n, come, 0)
    cross(0)
    pos = c * rows + lax.broadcasted_iota(jnp.int32, (rows, width), 0)
    live = pos < length
    mid = mid_ref[...]
    gm = jnp.where(live, og_ref[...].astype(F32), 0.0) + rms_back(mid, inverse_rms(mid), u_ref[...])
    gm_v[...] = gm
    gb_v[...] = gm.astype(BF)
    y_out[...] = jnp.where(live, mid + o_ref[...], 0.0).astype(BF)
    owners = 4 * n
    def mix(j, w):
        weight = out_ref[pl.ds(j * 8, 8)].reshape(8 * owned, width)
        r = contract_cols(gb_v[...], weight).astype(BF)
        for k in range(8 * owned // HEAD):
            dm_v[j * (8 * owned // HEAD) + k] = r[:, k * HEAD : (k + 1) * HEAD]
        return w
    lax.fori_loop(0, owners // 8, mix, 0)
    gb = gb_v[...]
    for i in range(2):
        w = width // 2
        grad = contract_rows(att_ref[...], gb[:, i * w : (i + 1) * w])
        red[i].p[...] = grad.astype(BF).reshape(red[i].p.shape)
        red[i].stage0()
    tab.wait()
    tc, ts = tab_v[0], tab_v[1]

    at_row = c * rows + lax.broadcasted_iota(jnp.int32, (rows, total), 0)
    at_col = lax.broadcasted_iota(jnp.int32, (rows, total), 1)
    allowed = (at_col <= at_row) & (at_col < length)
    def group(g):
        key = kv_ref[:, :, g * HEAD : (g + 1) * HEAD].reshape(total, HEAD)
        val = kv_ref[:, :, KVDIM + g * HEAD : KVDIM + (g + 1) * HEAD].reshape(total, HEAD)
        def head(i, w):
            h = g * GROUP + i
            part = pl.ds(pl.multiple_of(i * rows, rows), rows)
            scores = jnp.where(allowed, contract_cols(q_ref[h], key) * SCALE, MASKED)
            e = jnp.exp(scores - jnp.max(scores, axis=1, keepdims=True))
            probs = e / jnp.sum(e, axis=1, keepdims=True)
            gprobs = contract_cols(dm_v[h], val)
            inner = jnp.sum(probs * gprobs, axis=1, keepdims=True)
            gs = (probs * (gprobs - inner)).astype(BF)
            p_v[part, :] = probs.astype(BF)
            gs_v[part, :] = gs
            dq = product(gs, key) * SCALE
            gp_v[:, pl.ds(pl.multiple_of(h * HEAD, HEAD), HEAD)] = (dq * tc - pltpu.roll(dq, HEAD // 2, 1) * ts).astype(BF)
            return w
        lax.fori_loop(0, GROUP, head, 0)
        mine = slice(g * GROUP, (g + 1) * GROUP)
        dk = contract_rows(gs_v[...], q_ref[mine].reshape(GROUP * rows, HEAD)) * SCALE
        dv = contract_rows(p_v[...], dm_v[mine].reshape(GROUP * rows, HEAD))
        lanes = slice(g * 2 * HEAD, g * 2 * HEAD + 2 * HEAD)
        dkv_v[:, :, :, lanes] = jnp.concatenate([dk, dv], 1).astype(BF).reshape(n // 2, 2, rows, 2 * HEAD)
        send(dkv_v.at[:, 1 - x, :, lanes], kx.at[:, :, lanes], kxs.at[g], kxr.at[g], s, xp)
    def kv_x(g):
        lanes = slice(g * 2 * HEAD, g * 2 * HEAD + 2 * HEAD)
        arrived(kx.at[:, :, lanes], kxr.at[g], pc)
        kx[:, :, lanes] = add_low(kx[:, :, lanes], dkv_v[:, x, :, lanes])
        for d in range(1, n // 2):
            to = lax.rem(z + d, n // 2)
            send(kx.at[to, :, lanes], kz.at[z, :, lanes], kzs.at[g, d], kzr.at[g, d], s, 2 * to + x)
    def kv_z(g):
        lanes = slice(g * 2 * HEAD, g * 2 * HEAD + 2 * HEAD)
        sumkv = kx[z, :, lanes].astype(F32)
        for d in range(1, n // 2):
            src = lax.rem(z + n // 2 - d, n // 2)
            arrived(kz.at[src, :, lanes], kzr.at[g, d], pc)
            sumkv = sumkv + kz[src, :, lanes].astype(F32)
        dk, dv = sumkv[:, :HEAD], sumkv[:, HEAD:]
        k0, v0 = QDIM + g * HEAD, QDIM + KVDIM + g * HEAD
        gp_v[:, k0 : k0 + HEAD] = (dk * tc - pltpu.roll(dk, HEAD // 2, 1) * ts).astype(BF)
        gp_v[:, v0 : v0 + HEAD] = dv.astype(BF)
    xin = x_ref[...].astype(F32)
    inverse = inverse_rms(xin)
    def joint(i, first, w):
        xh = (x_ref[...].astype(F32) * inverse).astype(BF)
        grad = contract_rows(xh, gp_v[:, first : first + w]).astype(BF)
        shape = red[i].p.shape[:-1] + (w,)
        red[i].p[..., :w] = grad.reshape(shape)
    group(0)
    red[0].stage1(); red[1].stage1()
    feed(0)
    group(1)
    kv_x(0)
    red[0].stage2(); red[1].stage2()
    third = QDIM // 3
    for i in range(3):
        joint(2 + i, i * third, third)
        red[2 + i].stage0()
        if i == 0: kv_x(1)
    red[0].stage3(); red[1].stage3()
    red[2].stage1(); red[3].stage1(); red[4].stage1()
    feed(1)
    kv_z(0); kv_z(1)
    joint(5, QDIM, 2 * KVDIM)
    sums = jnp.sum(gp_v[...].astype(F32), axis=0, keepdims=True)
    p5 = red[5].p
    qk_width = QDIM + KVDIM
    at = lax.broadcasted_iota(jnp.int32, (owned, HEAD), 0)
    for d in range(owners):
        tiles = (qk_width // owners * d // HEAD, qk_width // owners * d // HEAD + 1, (qk_width + KVDIM // owners * d) // HEAD)
        part = jnp.zeros((owned, HEAD), F32)
        for k, t in enumerate(tiles):
            part = jnp.where(at == k, sums[:, t * HEAD : t * HEAD + HEAD], part)
        plane = d // n
        p5[plane // 2, plane % 2, d % n // 2, d % 2, :, 2 * KVDIM :] = part.astype(BF)
    red[5].stage0()
    red[2].stage2(); red[3].stage2(); red[4].stage2()
    red[5].stage1()
    qk = QDIM + 2 * KVDIM
    gp = gp_v[...]
    weights.wait()
    def back(j, w):
        weight = qkv_v[pl.ds(j * 8, 8), :, :qk].reshape(8 * owned, qk)
        cols = pl.ds(pl.multiple_of(j * 8 * owned, 8 * owned), 8 * owned)
        dx_v[:, cols] = contract_cols(gp, weight)
        return w
    lax.fori_loop(0, owners // 8, back, 0)
    red[2].stage3(); red[3].stage3(); red[4].stage3()
    red[5].stage2()
    fed(0)
    place_back(raw_v, 0, dgate_out)
    dx_out[...] = (gm_v[...] + rms_back(x_ref[...].astype(F32), inverse, dx_v[...])).astype(BF)
    for i in range(2):
        dout_out[:, i * (width // 2) : (i + 1) * (width // 2)] = red[i].stage4()
    red[5].stage3()
    fed(1)
    place_back(raw_v, 1, dup_out)
    gain = column(gain_ref[...])
    dgain_out[...] = as_row(jnp.sum(
        dgate_out[...] * gate_ref[...].astype(F32) + dup_out[...] * up_ref[...].astype(F32), axis=1, keepdims=True
    ))
    dgate_out[...] = dgate_out[...] * gain
    dup_out[...] = dup_out[...] * gain
    gain_one = column(gain_one_ref[...])
    rows_sum = jnp.zeros((owned, 1), F32)
    for i in range(3):
        cols = slice(i * third, (i + 1) * third)
        raw = red[2 + i].stage4()
        rows_sum = rows_sum + jnp.sum(raw * qw_ref[:, cols].astype(F32), axis=1, keepdims=True)
        dqkv_out[:, cols] = raw * gain_one
    raw = red[5].stage4()
    dbias_out[...] = raw[:8, 2 * KVDIM :]
    raw = raw[:, : 2 * KVDIM]
    rows_sum = rows_sum + jnp.sum(raw * qw_ref[:, QDIM:].astype(F32), axis=1, keepdims=True)
    dqkv_out[:, QDIM:] = raw * gain_one
    dgain_one_out[...] = as_row(rows_sum)
    for r in red: r.finish()
    for a in range(2):
        sent(r1_v.at[a], fs.at[a], pc)
        def left(d, w):
            sent(raw_v.at[0, a], gss.at[a, lax.rem(c + d, n)], pc)
            return w
        lax.fori_loop(1, n, left, 0)
    for g in range(2):
        lanes = slice(g * 2 * HEAD, g * 2 * HEAD + 2 * HEAD)
        sent(kx.at[:, :, lanes], kxs.at[g], pc)
        for d in range(1, n // 2): sent(kx.at[0, :, lanes], kzs.at[g, d], pc)

def backward_call(n, length, x, og, mid, u, o, att, q, kv, out_all, gate, up, qkv, gain, gain_one, qkv_all, tables, half_sum):
    S, V = jax.ShapeDtypeStruct, pltpu.VMEM
    rows, width = x.shape
    owned = qkv_all.shape[1]
    anys = pl.BlockSpec(memory_space=pl.ANY)
    vmem = pl.BlockSpec(memory_space=pltpu.VMEM)
    m = n // 2
    scratch = [V((2, rows, HEAD), F32), V((rows, width), F32), V((rows, width), BF), V((HEADS, rows, HEAD), BF),
               V((rows, QDIM + 2 * KVDIM), BF), V((GROUP * rows, n * rows), BF), V((GROUP * rows, n * rows), BF),
               V((m, 2, rows, 2 * KVDIM), BF), V((m, rows, 2 * KVDIM), BF), V((m, rows, 2 * KVDIM), BF),
               V((n, 2, owned, half_sum.shape[-1]), BF), V((2,) + half_sum.shape[2:], BF), V((2,) + half_sum.shape[2:], BF),
               V((rows, width), F32), V(qkv_all.shape, BF)]
    for i, w in enumerate((width // 2, width // 2, QDIM // 3, QDIM // 3, QDIM // 3, 2 * KVDIM + HEAD)):
        one = (m, 2, owned, w) if i % 2 == 0 else (2, m, owned, w)
        scratch += [V((2, 2, m, 2, owned, w), BF), V((2, m, 2, owned, w), BF), V(one, BF), V((m, owned, w), BF), V((m, owned, w), BF)]
    scratch += [DMA((3,)), DMA((2,)), DMA((2,)), DMA((2, m)), DMA((2, m)), DMA((2, n)), DMA((2, n)), DMA((2,)), DMA((2,)), DMA((6, 2 + m)), DMA((6, 2 + m))]
    return pl.pallas_call(
        functools.partial(backward_kernel, n),
        out_shape=[S((rows, width), BF), S((rows, width), BF), S((owned, width), F32), S(qkv.shape, F32), S((8, HEAD), F32),
                   S(gate.shape, F32), S(gate.shape, F32), S((1, owned), F32), S((1, owned), F32)],
        in_specs=[pl.BlockSpec(memory_space=pltpu.SMEM)] + [vmem] * 14 + [anys] * 3,
        out_specs=[vmem] * 9,
        scratch_shapes=scratch,
        compiler_params=pltpu.CompilerParams(collective_id=2, has_side_effects=True, vmem_limit_bytes=62 * 2**20),
    )(length, x, og, mid, u, o, att, q, kv, out_all, gate, up, qkv, gain, gain_one, qkv_all, tables, half_sum)


def kernel_shards(
    tokens,
    lengths,
    attn_gain,
    qkv_weight,
    qkv_bias,
    out_weight,
    mlp_gain,
    gate_weight,
    up_weight,
    down_weight,
    out_grad,
):
    seqs, parts = lax.axis_size("seq"), lax.axis_size("ctx")
    rows, width = tokens.shape[1:]
    owned = gate_weight.shape[0]
    piece = down_weight.shape[0]
    owners = seqs * parts
    me = lax.axis_index("seq") * parts + lax.axis_index("ctx")
    gain_one, gain_two = attn_gain[None], mlp_gain[None]
    half = HEAD // 2
    frequency = np.float32(ROPE_BASE) ** (-np.arange(half, dtype=np.float32) * np.float32(2.0 / HEAD))
    angles = np.arange(rows * parts, dtype=np.float32)[:, None] * frequency.astype(np.float32)[None, :]
    cosine, sine = np.cos(angles), np.sin(angles)
    tables = jnp.asarray(np.stack([np.concatenate([cosine, cosine], 1), np.concatenate([-sine, sine], 1)]), F32)
    x, og = tokens[0], out_grad[0]
    qkv_all, out_all, kv_all, q, half_sum, grad_down, att, mid, u, o = layer_call(
        parts, lengths, x, og, qkv_weight, gain_one, qkv_bias[None], gate_weight, up_weight, gain_two,
        down_weight, out_weight, tables,
    )
    joint = qkv_all.shape[-1]
    output, grad_inputs, grad_out, grad_qkv, bias_rows, grad_gate, grad_up, grad_mlp_gain, grad_attn_gain = backward_call(
        parts, lengths, x, og, mid, u, o, att, q, kv_all.reshape(parts, rows, 2 * KVDIM),
        out_all.reshape(owners, owned, width), gate_weight, up_weight, qkv_weight, gain_two, gain_one,
        qkv_all.reshape(owners, owned, joint), tables, half_sum,
    )
    per, per_value = (QDIM + KVDIM) // owners, KVDIM // owners
    grad_qk_bias = lax.dynamic_slice_in_dim(bias_rows[:2].reshape(2 * HEAD), lax.rem(per * me, HEAD), per)
    grad_value_bias = lax.dynamic_slice_in_dim(bias_rows[2], lax.rem(per_value * me, HEAD), per_value)
    return (
        output[None],
        grad_inputs[None],
        grad_attn_gain[0],
        grad_qkv,
        grad_qk_bias,
        grad_out,
        grad_mlp_gain[0],
        grad_gate,
        grad_up,
        grad_down[:piece].astype(F32),
        grad_value_bias,
    )


def solution(mesh):
    seqs, parts = mesh.shape["seq"], mesh.shape["ctx"]
    tiled = seqs == 4 and parts == 8 and 1536 // (seqs * parts) % 16 == 0
    rows, vector = P(BOTH, None), P(BOTH)
    token = P("seq", "ctx", None)
    return jax.shard_map(
        kernel_shards if tiled else plain_shards,
        mesh=mesh,
        in_specs=(token, P("seq"), vector, rows, vector, rows, vector, rows, rows, rows, token),
        out_specs=(token, token, vector, rows, vector, rows, vector, rows, rows, rows, vector),
        check_vma=False,
    )
```

```python
import functools

import jax
import jax.numpy as jnp
import numpy as np
from jax import lax
from jax.experimental import pallas as pl
from jax.experimental.pallas import tpu as pltpu
from jax.sharding import PartitionSpec as P

HEADS = 12
KV_HEADS = 2
HEAD = 128
QDIM = 1536
KVDIM = 256
GROUP = HEADS // KV_HEADS

EPSILON = 1e-06
ROPE_BASE = 1000000.0
MASKED = -1e30
SCALE = HEAD ** (-0.5)
BF = jnp.bfloat16
F32 = jnp.float32
BOTH = ("seq", "ctx")


DMA = pltpu.SemaphoreType.DMA
MESH = pl.DeviceIdType.MESH


def product(left, right):
    return jnp.dot(left, right, preferred_element_type=F32)


def contract_rows(left, right):
    return lax.dot_general(left, right, (((0,), (0,)), ((), ())), preferred_element_type=F32)


def contract_cols(left, right):
    return lax.dot_general(left, right, (((1,), (1,)), ((), ())), preferred_element_type=F32)


def inverse_rms(values):
    return lax.rsqrt(jnp.mean(values * values, axis=-1, keepdims=True) + EPSILON)


def rms_back(values, inverse, scaled_grad):
    inner = jnp.mean(scaled_grad * values, axis=-1, keepdims=True)
    return inverse * scaled_grad - values * (inverse * inverse * inverse) * inner


def rope_tables(positions):
    half = HEAD // 2
    frequency = ROPE_BASE ** (-jnp.arange(half, dtype=F32) * 2.0 / HEAD)
    angles = positions.astype(F32)[:, None] * frequency[None, :]
    return jnp.cos(angles), jnp.sin(angles)


def rotate(values, cosine, sine):
    half = HEAD // 2
    first, second = values[..., :half], values[..., half:]
    cosine, sine = cosine[:, None, :], sine[:, None, :]
    return jnp.concatenate([first * cosine - second * sine, second * cosine + first * sine], -1)


def gather(values, axes):
    return lax.all_gather(values, axes, axis=0, tiled=True)


def scatter(values, axes):
    return lax.psum_scatter(values, axes, scatter_dimension=0, tiled=True)


def plain_shards(
    tokens,
    lengths,
    attn_gain,
    qkv_weight,
    qkv_bias,
    out_weight,
    mlp_gain,
    gate_weight,
    up_weight,
    down_weight,
    out_grad,
):
    seqs, parts = lax.axis_size("seq"), lax.axis_size("ctx")
    inputs = tokens[0].astype(F32)
    rows, width = inputs.shape
    owned, hidden = gate_weight.shape
    piece = down_weight.shape[0]
    chunk = hidden // parts
    length = lengths[0]
    positions = lax.axis_index("ctx") * rows + jnp.arange(rows, dtype=jnp.int32)
    living = (positions < length).astype(F32)[:, None]
    cosine, sine = rope_tables(positions)

    gain_one = attn_gain.astype(F32)[:, None]
    gain_two = mlp_gain.astype(F32)[:, None]
    qkv_all = gather((qkv_weight.astype(F32) * gain_one).astype(BF), BOTH)
    bias_all = gather(qkv_bias, BOTH).astype(F32)
    out_all = gather(out_weight, BOTH)

    def to_chunks(weight):
        scaled = (weight.astype(F32) * gain_two).astype(BF)
        return scaled.reshape(owned, seqs, parts, piece).transpose(2, 0, 1, 3)

    both = jnp.stack([to_chunks(gate_weight), to_chunks(up_weight)], axis=1)
    both = lax.all_to_all(both.reshape(parts, 2, owned, chunk), "ctx", 0, 0)
    both = lax.all_gather(both, "seq", axis=0)
    gate_chunk = both[:, :, 0].reshape(width, chunk)
    up_chunk = both[:, :, 1].reshape(width, chunk)
    down_chunk = gather(down_weight, "seq")
    cotangent = out_grad[0].astype(F32) * living
    cot_all = gather(cotangent.astype(BF), "ctx")

    inverse_one = inverse_rms(inputs)
    normed_one = (inputs * inverse_one).astype(BF)
    project = product(normed_one, qkv_all) + bias_all
    queries = rotate(project[:, :QDIM].reshape(rows, HEADS, HEAD), cosine, sine).astype(BF)
    own_keys = rotate(
        project[:, QDIM : QDIM + KVDIM].reshape(rows, KV_HEADS, HEAD), cosine, sine
    ).astype(BF)
    own_values = project[:, QDIM + KVDIM :].astype(BF).reshape(rows, KV_HEADS, HEAD)
    keys, values = gather(own_keys, "ctx"), gather(own_values, "ctx")
    key_pos = jnp.arange(rows * parts, dtype=jnp.int32)
    allowed = (key_pos[None, :] <= positions[:, None]) & (key_pos[None, :] < length)
    grouped = queries.reshape(rows, KV_HEADS, GROUP, HEAD)
    scores = jnp.einsum("qgha,kga->ghqk", grouped, keys, preferred_element_type=F32) * SCALE
    scores = jnp.where(allowed, scores, MASKED)
    largest = jnp.max(scores, axis=-1, keepdims=True)
    exponent = jnp.exp(scores - largest)
    summed = jnp.sum(exponent, axis=-1, keepdims=True)
    probs = exponent / summed
    probs_low = probs.astype(BF)
    attended = jnp.einsum("ghqk,kga->qgha", probs_low, values, preferred_element_type=F32)
    attended = attended.reshape(rows, QDIM).astype(BF)
    middle = inputs + product(attended, out_all)

    inverse_two = inverse_rms(middle)
    normed_two = gather((middle * inverse_two).astype(BF), "ctx")
    gate_pre = product(normed_two, gate_chunk)
    up_pre = product(normed_two, up_chunk)
    sig = jax.nn.sigmoid(gate_pre)
    activated = (gate_pre * sig * up_pre).astype(BF)
    grad_act = contract_cols(cot_all, down_chunk)
    grad_gate = (grad_act * up_pre * (sig + gate_pre * sig * (1.0 - sig))).astype(BF)
    grad_up = (grad_act * gate_pre * sig).astype(BF)
    scaled_two = contract_cols(grad_gate, gate_chunk) + contract_cols(grad_up, up_chunk)
    scaled_two = scatter(scaled_two.astype(BF), "ctx").astype(F32)
    branch = scatter(product(activated, down_chunk).astype(BF), "ctx").astype(F32)
    output = ((middle + branch) * living).astype(BF)
    grad_down = scatter(contract_rows(activated, cot_all).astype(BF), "seq").astype(F32)
    raw = jnp.stack([contract_rows(normed_two, grad_gate), contract_rows(normed_two, grad_up)], 1)
    raw = scatter(raw.astype(BF), "seq").reshape(parts, owned, 2, chunk)
    raw = lax.all_to_all(raw, "ctx", 0, 0).astype(F32)
    raw = raw.reshape(parts, owned, 2, seqs, piece).transpose(2, 1, 3, 0, 4)
    raw = raw.reshape(2, owned, hidden)
    grad_mlp_gain = jnp.sum(raw[0] * gate_weight.astype(F32) + raw[1] * up_weight.astype(F32), 1)

    grad_middle = cotangent + rms_back(middle, inverse_two, scaled_two)
    grad_branch = grad_middle.astype(BF)
    grad_out = scatter(contract_rows(attended, grad_branch).astype(BF), BOTH).astype(F32)
    grad_mixed = contract_cols(grad_branch, out_all).astype(BF)
    grad_mixed = grad_mixed.reshape(rows, KV_HEADS, GROUP, HEAD)
    grad_probs = jnp.einsum("qgha,kga->ghqk", grad_mixed, values, preferred_element_type=F32)
    inner = jnp.sum(probs * grad_probs, axis=-1, keepdims=True)
    grad_scores = (probs * (grad_probs - inner)).astype(BF)
    grad_q = jnp.einsum("ghqk,kga->qgha", grad_scores, keys, preferred_element_type=F32) * SCALE
    grad_k = jnp.einsum("ghqk,qgha->kga", grad_scores, grouped, preferred_element_type=F32) * SCALE
    grad_v = jnp.einsum("ghqk,qgha->kga", probs_low, grad_mixed, preferred_element_type=F32)
    grad_k = scatter(grad_k.astype(BF), "ctx").astype(F32)
    grad_v = scatter(grad_v.astype(BF), "ctx").astype(F32)
    grad_q = rotate(grad_q.reshape(rows, HEADS, HEAD), cosine, -sine).reshape(rows, QDIM)
    grad_k = rotate(grad_k, cosine, -sine).reshape(rows, KVDIM)
    grad_project = jnp.concatenate([grad_q, grad_k, grad_v.reshape(rows, KVDIM)], axis=1)
    grad_project = grad_project.astype(BF)
    raw_qkv = scatter(contract_rows(normed_one, grad_project).astype(BF), BOTH).astype(F32)
    grad_attn_gain = jnp.sum(raw_qkv * qkv_weight.astype(F32), axis=1)
    grad_bias = jnp.sum(grad_project.astype(F32), axis=0)
    qk_width = QDIM + KVDIM
    grad_qk_bias = scatter(grad_bias[:qk_width], BOTH)
    grad_value_bias = scatter(grad_bias[qk_width:], BOTH)
    scaled_one = contract_cols(grad_project, qkv_all)
    grad_inputs = (grad_middle + rms_back(inputs, inverse_one, scaled_one)).astype(BF)
    return (
        output[None],
        grad_inputs[None],
        grad_attn_gain,
        raw_qkv * gain_one,
        grad_qk_bias,
        grad_out,
        grad_mlp_gain,
        raw[0] * gain_two,
        raw[1] * gain_two,
        grad_down,
        grad_value_bias,
    )


class Place:
    def __init__(self, n):
        self.n = n
        self.s, self.c = lax.axis_index("seq"), lax.axis_index("ctx")
        self.me = self.s * n + self.c
        self.core = lax.rem(self.s, 2)
        self.sib = self.s + 1 - 2 * self.core
        self.far = lax.rem(self.s + 2, 4)
        half = self.c // 2
        self.pos = half + lax.rem(self.c, 2) * (n - 1 - 2 * half)
        self.nxt, self.prv = self.at(1), self.at(-1)
    def at(self, offset):
        p = lax.rem(self.pos + offset + 2 * self.n, self.n)
        return 2 * p + (p // (self.n // 2)) * (2 * self.n - 1 - 4 * p)

def send(src, dst, ssem, rsem, seq, ctx):
    copy = pltpu.make_async_remote_copy(src, dst, ssem, rsem, device_id=(seq, ctx), device_id_type=MESH)
    copy.start()

def arrived(dst, rsem, place):
    pltpu.make_async_remote_copy(dst, dst, rsem, rsem, device_id=(place.s, place.c), device_id_type=MESH).wait_recv()

def sent(src, ssem, place):
    pltpu.make_async_remote_copy(src, src, ssem, ssem, device_id=(place.s, place.c), device_id_type=MESH).wait_send()

def enter(place, whole_group=True):
    barrier = pltpu.get_barrier_semaphore()
    def greet(d, z):
        pl.semaphore_signal(barrier, inc=1, device_id=(place.s, lax.rem(place.c + d, place.n)), device_id_type=MESH)
        return z
    lax.fori_loop(1, place.n, greet, 0)
    pl.semaphore_signal(barrier, inc=1, device_id=(place.sib, place.c), device_id_type=MESH)
    pl.semaphore_signal(barrier, inc=1, device_id=(place.far, place.c), device_id_type=MESH)
    pl.semaphore_wait(barrier, place.n + 1)


def add_low(left, right):
    return (left.astype(F32) + right.astype(F32)).astype(BF)

def diagonal(n):
    return lax.broadcasted_iota(jnp.int32, (n, n), 0) == lax.broadcasted_iota(jnp.int32, (n, n), 1)

def column(row):
    return jnp.sum(jnp.where(diagonal(row.shape[1]), row.astype(F32), 0.0), axis=1, keepdims=True)

def as_row(values):
    return jnp.sum(jnp.where(diagonal(values.shape[0]), values, 0.0), axis=0, keepdims=True)

class RingGather:
    def __init__(self, pc, slots, ssem, rsem, index=None):
        self.pc, self.slots, self.ssem, self.rsem, self.index = pc, slots, ssem, rsem, index
        self.steps, self.half = pc.n // 2, slots.shape[2] // 2
        self.ways = ((0, -1, pc.nxt), (1, 1, pc.prv))
    def slot(self, offset):
        return self.index[offset] if self.index else self.pc.at(offset)
    def part(self, ref, f, t):
        return ref if t < self.steps - 1 else ref.at[:, pl.ds(f * self.half, self.half)]
    def hop(self, t, own=None):
        for f, sign, to in self.ways:
            src = self.slots.at[self.slot(sign * t)] if own is None else own
            there = self.slots.at[self.slot(sign * (t + 1) if self.index else sign * t)]
            send(self.part(src, f, t), self.part(there, f, t), self.ssem.at[f, t], self.rsem.at[f, t], self.pc.s, to)
    def turn(self, t):
        for f, sign, _ in self.ways:
            arrived(self.part(self.slots.at[self.slot(sign * (t + 1))], f, t), self.rsem.at[f, t], self.pc)
        if t + 1 < self.steps: self.hop(t + 1)
    def finish(self):
        for f in range(2):
            for t in range(self.steps): sent(self.part(self.slots.at[0], f, t), self.ssem.at[f, t], self.pc)

class RingSum:
    def __init__(self, pc, term, index, held_half, held, ssem, rsem, out):
        self.pc, self.term, self.index, self.out = pc, term, index, out
        self.held_half, self.held, self.ssem, self.rsem = held_half, held, ssem, rsem
        self.steps, self.half = pc.n // 2, term.shape[2] // 2
    def turn(self, t):
        pc, ahead = self.pc, self.steps - t
        for f, sign, to in ((0, 1, pc.nxt), (1, -1, pc.prv)):
            cols = slice(f * self.half, (f + 1) * self.half)
            i = self.index[sign * ahead]
            if t == 1:
                arrived(self.held_half.at[f], self.rsem.at[f, 0], pc)
                self.term[i, :, cols] = add_low(self.term[i, :, cols], self.held_half[f])
            elif t > 1:
                arrived(self.held.at[f, t - 2], self.rsem.at[f, t - 1], pc)
                if t < self.steps: self.term[i] = add_low(self.term[i], self.held[f, t - 2])
            if t == 0:
                src, dst = self.term.at[i, :, pl.ds(f * self.half, self.half)], self.held_half.at[f]
            elif t < self.steps:
                src, dst = self.term.at[i], self.held.at[f, t - 1]
            if t < self.steps: send(src, dst, self.ssem.at[f, t], self.rsem.at[f, t], pc.s, to)
        if t == self.steps:
            i = self.index[0]
            self.out[...] = self.term[i].astype(F32) + self.held[0, t - 2].astype(F32) + self.held[1, t - 2].astype(F32)
    def finish(self):
        for f in range(2):
            sent(self.held_half.at[f], self.ssem.at[f, 0], self.pc)
            for t in range(1, self.steps): sent(self.held.at[f, 0], self.ssem.at[f, t], self.pc)

class Spread:
    def __init__(self, pc, x_first, w, ss, rs, i):
        self.pc, self.x_first, self.w, self.ss, self.rs, self.i = pc, x_first, w, ss, rs, i
        self.y, self.x, self.z = pc.s // 2, lax.rem(pc.c, 2), pc.c // 2
        self.xp = pc.c + 1 - 2 * self.x
        self.deep = pc.n // 2
    def go(self, k, part, seq, ctx):
        send(part, part, self.ss.at[self.i, k], self.rs.at[self.i, k], seq, ctx)
    def come(self, k, part):
        arrived(part, self.rs.at[self.i, k], self.pc)
    def both(self, k, part, sib_k, seq, ctx, sib_part):
        self.go(k, part, seq, ctx)
        self.go(sib_k, sib_part, self.pc.sib, self.pc.c)
    def begin(self):
        own = self.w.at[self.y, self.pc.core, self.z, self.x]
        for d in range(1, self.deep):
            self.go(d - 1, own, self.pc.s, 2 * lax.rem(self.z + d, self.deep) + self.x)
    def stage1(self):
        pc, w, y, x = self.pc, self.w, self.y, self.x
        for d in range(1, self.deep):
            self.come(d - 1, w.at[y, pc.core, lax.rem(self.z + self.deep - d, self.deep), x])
        column = w.at[y, pc.core, :, x]
        if self.x_first: self.both(self.deep, column, self.deep + 2, pc.s, self.xp, column)
        else: self.both(self.deep, column, self.deep + 2, pc.far, pc.c, column)
    def stage2(self):
        pc, w, y, x = self.pc, self.w, self.y, self.x
        if self.x_first:
            new = w.at[y, pc.core, :, 1 - x]
            self.come(self.deep, new)
            self.both(self.deep + 1, w.at[y, pc.core], self.deep + 3, pc.far, pc.c, new)
        else:
            new = w.at[1 - y, pc.core, :, x]
            self.come(self.deep, new)
            self.both(self.deep + 1, w.at[:, pc.core, :, x], self.deep + 3, pc.s, self.xp, new)
    def stage3(self):
        pc, w, y, x = self.pc, self.w, self.y, self.x
        new = w.at[1 - y, pc.core] if self.x_first else w.at[:, pc.core, :, 1 - x]
        self.come(self.deep + 1, new)
        self.go(self.deep + 4, new, pc.sib, pc.c)
    def stage4(self):
        pc, w, y, x = self.pc, self.w, self.y, self.x
        other = 1 - pc.core
        self.come(self.deep + 2, w.at[y, other, :, x])
        self.come(self.deep + 3, w.at[y, other, :, 1 - x] if self.x_first else w.at[1 - y, other, :, x])
        self.come(self.deep + 4, w.at[1 - y, other] if self.x_first else w.at[:, other, :, 1 - x])
    def finish(self):
        w, four = self.w, self.w.at[0, 0, :, 0]
        eight = w.at[0, 0] if self.x_first else w.at[:, 0, :, 0]
        for d in range(1, self.deep): sent(w.at[0, 0, 0, 0], self.ss.at[self.i, d - 1], self.pc)
        for k, part in enumerate((four, eight, four, four, eight)): sent(part, self.ss.at[self.i, self.deep + k], self.pc)

def windows(n, piece, padded):
    for part in range(n):
        for plane in range(4):
            whole, packed = (plane * n + part) * piece, plane * padded
            first, packed_first = whole // 128 * 128, packed // 128 * 128
            span = -(-(whole + piece) // 128) * 128 - first
            packed_span = -(-(packed + piece) // 128) * 128 - packed_first
            yield part, whole - first, packed - packed_first, first, span, packed_first, packed_span

def shift_lanes(block, span, shift):
    if block.shape[1] < span:
        block = jnp.concatenate([block, jnp.zeros((block.shape[0], span - block.shape[1]), block.dtype)], 1)
    shift = shift % block.shape[1]
    return pltpu.roll(block, shift, 1) if shift else block

def place_back(raw, a, out):
    n, _, owned, chunk = raw.shape
    piece, padded = out.shape[1] // (4 * n), chunk // 4
    for part, at, packed_at, first, span, packed_first, packed_span in windows(n, piece, padded):
        block = raw[part, a, :, packed_first : packed_first + packed_span].astype(F32)
        block = shift_lanes(block, span, at - packed_at)[:, :span]
        lane = lax.broadcasted_iota(jnp.int32, block.shape, 1)
        here = (lane >= at) & (lane < at + piece)
        out[:, first : first + span] = jnp.where(here, block, out[:, first : first + span])

def place_out(weight, gain, a, packs):
    n, _, _, chunk = packs.shape
    owned = weight.shape[0]
    piece, padded = weight.shape[1] // (4 * n), chunk // 4
    for part in range(n): packs[part, a, :owned] = jnp.zeros((owned, chunk), BF)
    for part, at, packed_at, first, span, packed_first, packed_span in windows(n, piece, padded):
        block = weight[:, first : first + span].astype(F32) * gain
        block = shift_lanes(block, packed_span, packed_at - at)[:, :packed_span]
        lane = lax.broadcasted_iota(jnp.int32, block.shape, 1)
        here = (lane >= packed_at) & (lane < packed_at + piece)
        before = packs[part, a, :owned, packed_first : packed_first + packed_span].astype(F32)
        packs[part, a, :owned, packed_first : packed_first + packed_span] = jnp.where(here, block, before).astype(BF)


def rope(values, table_c, table_s):
    return values * table_c + pltpu.roll(values, HEAD // 2, 1) * table_s

def layer_kernel(n, length_ref, x_ref, og_ref, qw_ref, g1_ref, b_ref, gate_ref, up_ref, g2_ref, down, outw, tables,
                 qkv_all, out_all, kv_all, q_out, half_sum, dsum, att_out, mid_out, u_own, o_own,
                 gu_v, down_v, cot_v, n2_v, act_v, gg_v, gp_v, ut, uhh, uh, ot, ohh, oh, dgu_v, dd_v, r0g, r0d, r1d, w_o2,
                 kv_v, q_v, tab_v,
                 local, save, ss, rs, g_recv, g_send, g_own, g_far, g_sib, d_recv, d_far, d_sib, c_recv, c_send,
                 kz_s, kz_r, kx_s, kx_r, n_recv, n_send, u_recv, u_send, o_recv_, o_send_, gs0, gr0, gsave, ds0, dr0, ds1, dr1, dsave):
    pc = Place(n)
    me, s, c = pc.me, pc.s, pc.c
    y, x, z, xp = s // 2, lax.rem(c, 2), c // 2, c + 1 - 2 * lax.rem(c, 2)
    rows, width = x_ref.shape
    owned, piece = qw_ref.shape[0], down_v.shape[0] // 4
    length = length_ref[0]
    third, owners, deep = QDIM // 3, 4 * n, n // 2

    def g_slot(i): return gu_v.at[:, pl.ds(pl.multiple_of(i * owned, owned), owned), :]
    def pack(i): return act_v.at[i, :, pl.ds(0, owned), :]
    def d_slot(i): return down_v.at[pl.ds(pl.multiple_of(i * piece, piece), piece), :]

    kvw = 2 * KVDIM + HEAD
    def cut(ref, first, w): return ref.at[:, :, :, :, :, pl.ds(first, w)]
    w_kv = cut(dgu_v.at[0], 0, kvw)
    wide = (w_kv, cut(dgu_v.at[0], kvw, third), cut(dgu_v.at[1], 0, third), cut(dgu_v.at[1], third, third),
            cut(r0g, 0, width // 2), cut(r0g, width // 2, width // 4), w_o2)
    spreads = [Spread(pc, i % 2 == 0, w, ss, rs, i) for i, w in enumerate(wide)]
    kvs, q0, q1, q2, o0, o1, o2 = spreads
    outs = ((o0, 0, width // 2), (o1, width // 2, width // 4), (o2, width // 4 * 3, width // 4))
    pairs = n // 2
    offsets = [o for j in range(1, pairs) for o in (-j, j)] + [pairs, 0]
    index = {o: i for i, o in enumerate(offsets)}
    index[-pairs] = index[pairs]
    cring = RingGather(pc, cot_v, c_send, c_recv, index)
    nring = RingGather(pc, n2_v, n_send, n_recv, index)
    uring = RingSum(pc, ut, index, uhh, uh, u_send, u_recv, u_own)
    oring = RingSum(pc, ot, index, ohh, oh, o_send_, o_recv_, o_own)
    lc = [pltpu.make_async_copy(a, b, local.at[i]) for i, (a, b) in enumerate((
        (outw.at[:, pl.ds(0, width // 2)], wide[4].at[y, pc.core, z, x]), (outw.at[:, pl.ds(width // 2, width // 4)], wide[5].at[y, pc.core, z, x]),
        (outw.at[:, pl.ds(width // 4 * 3, width // 4)], w_o2.at[y, pc.core, z, x]), (tables.at[:, pl.ds(pl.multiple_of(c * rows, rows), rows), :], tab_v)))]
    for copy in lc: copy.start()
    g1 = column(g1_ref[...])
    def scaled(first, w): return (qw_ref[:, first : first + w].astype(F32) * g1).astype(BF)
    w_kv[y, pc.core, z, x, :, : 2 * KVDIM] = scaled(QDIM, 2 * KVDIM)
    share = b_ref.shape[1]
    bias = b_ref[...].astype(F32)
    rest = jnp.zeros((1, HEAD - share), F32)
    odd = lax.rem(me, 2) == 1
    row = jnp.where(odd, jnp.concatenate([rest, bias], 1), jnp.concatenate([bias, rest], 1))
    first_row = lax.broadcasted_iota(jnp.int32, (owned, HEAD), 0) == 0
    w_kv[y, pc.core, z, x, :, 2 * KVDIM :] = jnp.where(first_row, row, 0.0).astype(BF)
    for i, w in enumerate(wide[1:4]): w[y, pc.core, z, x] = scaled(i * third, third)
    slot_pos = c * rows + lax.broadcasted_iota(jnp.int32, (rows, width), 0)
    cot_v[index[0]] = jnp.where(slot_pos < length, og_ref[...].astype(F32), 0.0).astype(BF)
    g2 = column(g2_ref[...])
    place_out(gate_ref, g2, 0, act_v)
    place_out(up_ref, g2, 1, act_v)
    short = down[...].astype(F32)
    padding = jnp.zeros((piece - short.shape[0], width), F32)
    down_v[pl.ds(pl.multiple_of(s * piece, piece), piece), :] = jnp.concatenate([short, padding], 0).astype(BF)
    enter(pc)
    def gu_turn(t):
        k = s * n + lax.rem(c + n - t, n)
        arrived(g_slot(k), g_recv.at[k], pc)
        send(g_slot(k), g_slot(k), g_far.at[lax.rem(c + n - t, n)], g_recv.at[k], pc.far, c)
        send(g_slot(k), g_slot(k), g_sib.at[k], g_recv.at[k], pc.sib, c)
    for p in (kvs, q0, q1, q2): p.begin()
    own_gu = pltpu.make_async_copy(pack(c), g_slot(me), local.at[5])
    own_gu.start()
    def feed(d, v):
        to = lax.rem(c + d, n)
        send(pack(to), g_slot(me), g_send.at[to], g_recv.at[me], s, to)
        return v
    lax.fori_loop(1, n, feed, 0)
    send(pack(c), g_slot(me), g_own.at[0], g_recv.at[me], pc.far, c)
    send(pack(c), g_slot(me), g_own.at[1], g_recv.at[me], pc.sib, c)
    send(d_slot(s), d_slot(s), d_far.at[0], d_recv.at[s], pc.far, c)
    send(d_slot(s), d_slot(s), d_sib.at[s], d_recv.at[s], pc.sib, c)
    xf = x_ref[...].astype(F32)
    att_out[...] = (xf * inverse_rms(xf)).astype(BF)
    kvs.stage1()
    q0.stage1()
    q1.stage1()
    kvs.stage2()
    q2.stage1()
    q0.stage2()
    kvs.stage3()
    q1.stage2()
    for copy in lc[:3]: copy.wait()
    o0.begin(); o1.begin(); o2.begin()
    q2.stage2()
    q0.stage3()
    q1.stage3()
    q2.stage3()
    gu_turn(1); gu_turn(2)
    kvs.stage4()
    lc[3].wait()
    tc, ts = tab_v[0], tab_v[1]
    xh = att_out[...]
    def bias_of(tile):
        d = 2 * tile
        def part(i):
            plane, place = i // n, i % n
            return w_kv[plane // 2, plane % 2, place // 2, place % 2, 0:1, 2 * KVDIM :].astype(F32)
        return part(d) + part(d + 1)
    kv = product(xh, w_kv[..., : 2 * KVDIM].reshape(owners * owned, 2 * KVDIM))
    for k in range(2 * KV_HEADS):
        lanes = slice(k * HEAD, (k + 1) * HEAD)
        one = kv[:, lanes] + bias_of(QDIM // HEAD + k)
        kv_v[z, x, :, lanes] = (rope(one, tc, ts) if k < KV_HEADS else one).astype(BF)
    own_kv = kv_v.at[z, x]
    for d in range(1, deep):
        send(own_kv, own_kv, kz_s.at[d], kz_r.at[d], s, 2 * lax.rem(z + d, deep) + x)
    send(own_kv, own_kv, kx_s.at[0], kx_r.at[0], s, xp)
    o0.stage1(); o1.stage1(); o2.stage1()
    for i, p in enumerate((q0, q1, q2)):
        p.stage4()
        r = product(xh, p.w[...].reshape(owners * owned, third))
        for k in range(third // HEAD):
            h = i * (third // HEAD) + k
            q_v[h] = rope(r[:, k * HEAD : (k + 1) * HEAD] + bias_of(h), tc, ts).astype(BF)
    for d in range(1, deep):
        block = kv_v.at[lax.rem(z + deep - d, deep), x]
        arrived(block, kz_r.at[d], pc)
        send(block, block, kx_s.at[d], kx_r.at[d], s, xp)
    cring.hop(0)
    o0.stage2(); o1.stage2(); o2.stage2()
    saves = [pltpu.make_async_copy(q_v, q_out, save.at[0])]
    for i, (p, first) in enumerate(((kvs, QDIM), (q0, 0), (q1, third), (q2, 2 * third))):
        saves.append(pltpu.make_async_copy(p.w, qkv_all.at[:, :, :, :, :, pl.ds(first, p.w.shape[5])], save.at[1 + i]))
    for copy in saves: copy.start()
    for d in range(deep):
        arrived(kv_v.at[lax.rem(z + deep - d, deep), 1 - x], kx_r.at[d], pc)

    total = n * rows
    at_row = c * rows + lax.broadcasted_iota(jnp.int32, (rows, total), 0)
    at_col = lax.broadcasted_iota(jnp.int32, (rows, total), 1)
    allowed = (at_col <= at_row) & (at_col < length)
    def heads(first, count):
        def head(h, v):
            col = pl.multiple_of(h // GROUP * HEAD, HEAD)
            key = kv_v[:, :, :, pl.ds(col, HEAD)].reshape(total, HEAD)
            val = kv_v[:, :, :, pl.ds(pl.multiple_of(KVDIM + col, HEAD), HEAD)].reshape(total, HEAD)
            scores = jnp.where(allowed, contract_cols(q_v[h], key) * SCALE, MASKED)
            e = jnp.exp(scores - jnp.max(scores, axis=1, keepdims=True))
            probs = (e * (1.0 / jnp.sum(e, axis=1, keepdims=True))).astype(BF)
            att_out[:, pl.ds(pl.multiple_of(h * HEAD, HEAD), HEAD)] = product(probs, val).astype(BF)
            return v
        lax.fori_loop(first, first + count, head, 0)
    o0.stage3(); o1.stage3(); o2.stage3()
    heads(0, GROUP)
    gu_turn(3); gu_turn(4)
    cring.turn(0)
    heads(GROUP, GROUP)
    gu_turn(5); gu_turn(6)
    own_gu.wait()
    for i in range(2): sent(pack(0), g_own.at[i], pc)
    def fed(d, v):
        sent(pack(0), g_send.at[lax.rem(c + d, n)], pc)
        return v
    lax.fori_loop(1, n, fed, 0)
    gu_turn(7)
    o0.stage4(); o1.stage4(); o2.stage4()
    saves2 = [pltpu.make_async_copy(kv_v, kv_all, save.at[5])]
    for i, (p, first, w) in enumerate(outs):
        saves2.append(pltpu.make_async_copy(p.w, out_all.at[:, :, :, :, :, pl.ds(first, w)], save.at[6 + i]))
    for copy in saves2: copy.start()
    cring.turn(1)
    att = att_out[...]
    for p, first, w in outs:
        lanes = slice(first, first + w)
        mid_out[:, lanes] = x_ref[:, lanes].astype(F32) + product(att, p.w[...].reshape(owners * owned, w))
    mid = mid_out[...]
    n2_v[index[0]] = (mid * inverse_rms(mid)).astype(BF)
    nring.hop(0)
    cring.turn(2)
    arrived(d_slot(pc.far), d_recv.at[pc.far], pc)
    send(d_slot(pc.far), d_slot(pc.far), d_sib.at[pc.far], d_recv.at[pc.far], pc.sib, c)
    def across(t):
        k = pc.far * n + lax.rem(c + n - t, n)
        arrived(g_slot(k), g_recv.at[k], pc)
        send(g_slot(k), g_slot(k), g_sib.at[k], g_recv.at[k], pc.sib, c)
    for t in range(n):
        if t == n - 1:
            for copy in saves + saves2: copy.wait()
            for p in spreads: p.finish()
        across(t)
        if t == 1: nring.turn(0)
        if t == 3: cring.turn(3)
        if t == 4: nring.turn(1)
    for plane in range(2):
        other = 2 * plane + 1 - pc.core
        arrived(d_slot(other), d_recv.at[other], pc)
        def come(t, v):
            i = other * n + t
            arrived(g_slot(i), g_recv.at[i], pc)
            return v
        lax.fori_loop(0, n, come, 0)
    tall, chunk = 2 * rows, gu_v.shape[2]
    def forward(j):
        pair = slice(2 * j, 2 * j + 2)
        normed = n2_v[pair].reshape(tall, width)
        gate = product(normed, gu_v[0])
        up = product(normed, gu_v[1])
        sig = jax.nn.sigmoid(gate)
        gs = gate * sig
        act = (gs * up).astype(BF)
        act_v[pair] = act.reshape(2, 2, rows // 2, chunk)
        gp_v[pair] = gs.astype(BF).reshape(2, rows, chunk)
        gg_v[pair] = (up * (sig + gs * (1.0 - sig))).astype(BF).reshape(2, rows, chunk)
        ot[pair] = product(act, down_v[...]).astype(BF).reshape(2, rows, width)
    def backward(j):
        pair = slice(2 * j, 2 * j + 2)
        grad = contract_cols(cot_v[pair].reshape(tall, width), down_v[...])
        gg = (grad * gg_v[pair].reshape(tall, chunk).astype(F32)).astype(BF)
        gp = (grad * gp_v[pair].reshape(tall, chunk).astype(F32)).astype(BF)
        gg_v[pair] = gg.reshape(2, rows, chunk)
        gp_v[pair] = gp.reshape(2, rows, chunk)
        ut[pair] = (contract_cols(gg, gu_v[0]) + contract_cols(gp, gu_v[1])).astype(BF).reshape(2, rows, width)

    all_rows = n * rows
    plane = n * owned
    core = pc.core
    tile = 384
    def cols_of(j): return pl.ds(j * tile, tile)
    wide_pieces = [(0, j, a) for j in range(chunk // tile) for a in range(2)]
    down_pieces = [(1, j, 0) for j in range(width // tile)]
    def compute(p):
        kind, j, a = p
        if kind == 0:
            lhs, rhs = n2_v[...].reshape(all_rows, width), (gg_v, gp_v)[a]
            grad = contract_rows(lhs, rhs[:, :, cols_of(j)].reshape(all_rows, tile))
            dgu_v[a, :, :, :, :, :, cols_of(j)] = grad.astype(BF).reshape(2, 2, deep, 2, owned, tile)
            send(dgu_v.at[a, :, 1 - core, :, :, :, cols_of(j)], r0g.at[a, :, :, :, :, cols_of(j)],
                 gs0.at[a, j], gr0.at[a, j], pc.sib, c)
        else:
            grad = contract_rows(act_v[...].reshape(all_rows, chunk), cot_v[:, :, cols_of(j)].reshape(all_rows, tile))
            dd_v[:, :, :, cols_of(j)] = grad.astype(BF).reshape(2, 2, piece, tile)
            send(dd_v.at[:, 1 - core, :, cols_of(j)], r0d.at[:, :, cols_of(j)], ds0.at[j], dr0.at[j], pc.sib, c)
    def add_core(p):
        kind, j, a = p
        cols = cols_of(j)
        if kind == 0:
            arrived(r0g.at[a, :, :, :, :, cols], gr0.at[a, j], pc)
            for k in range(2):
                r0g[a, k, :, :, :, cols] = add_low(r0g[a, k, :, :, :, cols], dgu_v[a, k, core, :, :, :, cols])
            copy = pltpu.make_async_copy(r0g.at[a, :, :, :, :, cols], half_sum.at[a, :, :, :, :, cols], gsave.at[a, j])
            copy.start()
            saves.append(copy)
        else:
            arrived(r0d.at[:, :, cols], dr0.at[j], pc)
            for k in range(2):
                r0d[k, :, cols] = add_low(r0d[k, :, cols], dd_v[k, core, :, cols])
            send(r0d.at[1 - y, :, cols], r1d.at[:, cols], ds1.at[j], dr1.at[j], pc.far, c)
    def add_far(p):
        _, j, _ = p
        cols = cols_of(j)
        arrived(r1d.at[:, cols], dr1.at[j], pc)
        r1d[:, cols] = add_low(r1d[:, cols], r0d[y, :, cols])
        copy = pltpu.make_async_copy(r1d.at[:, cols], dsum.at[:, cols], dsave.at[j])
        copy.start()
        saves.append(copy)
    saves.clear()
    forward(0)
    nring.turn(2)
    forward(1)
    nring.turn(3)
    forward(2)
    forward(3)
    backward(3)
    uring.turn(0)
    oring.turn(0)
    compute(down_pieces[0])
    compute(down_pieces[1])
    add_core(down_pieces[0])
    backward(2)
    uring.turn(1)
    add_core(down_pieces[1])
    compute(down_pieces[2])
    backward(1)
    uring.turn(2)
    oring.turn(1)
    add_core(down_pieces[2])
    compute(down_pieces[3])
    backward(0)
    uring.turn(3)
    add_core(down_pieces[3])
    for i, p in enumerate(wide_pieces):
        compute(p)
        if i: add_core(wide_pieces[i - 1])
        if i == 3: uring.turn(4)
        if i == 1: oring.turn(2)
        if i == 5: oring.turn(3)
    add_core(wide_pieces[-1])
    for p in down_pieces: add_far(p)
    oring.turn(4)
    for kind, j, a in wide_pieces + down_pieces:
        cols = cols_of(j)
        if kind == 0:
            sent(r0g.at[a, :, :, :, :, cols], gs0.at[a, j], pc)
        else:
            sent(r0d.at[:, :, cols], ds0.at[j], pc)
            sent(r1d.at[:, cols], ds1.at[j], pc)
    for copy in saves: copy.wait()
    nring.finish()
    uring.finish()
    oring.finish()
    cring.finish()
    for d in range(1, deep): sent(own_kv, kz_s.at[d], pc)
    for d in range(deep): sent(own_kv, kx_s.at[d], pc)
    sent(d_slot(0), d_far.at[0], pc)
    def left(t, v):
        sent(g_slot(0), g_sib.at[pc.far * n + t], pc)
        @pl.when(t > 0)
        def _():
            src = lax.rem(c + t, n)
            sent(g_slot(0), g_far.at[src], pc)
            sent(g_slot(0), g_sib.at[s * n + src], pc)
        return v
    lax.fori_loop(0, n, left, 0)
    sent(d_slot(0), d_sib.at[s], pc)
    sent(d_slot(0), d_sib.at[pc.far], pc)

def layer_call(n, length, x, og, qkv, gain_one, bias, gate, up, gain_two, down, outw, tables):
    N, m = 4 * n, n // 2
    rows, width = x.shape
    owned, piece = qkv.shape[0], -(-down.shape[0] // 32) * 32
    chunk = 4 * piece
    S, V = jax.ShapeDtypeStruct, pltpu.VMEM
    joint = QDIM + 2 * KVDIM + HEAD
    shapes = [S((2, 2, m, 2, owned, joint), BF), S((2, 2, m, 2, owned, width), BF), S((m, 2, rows, 2 * KVDIM), BF),
              S((HEADS, rows, HEAD), BF), S((2, 2, m, 2, owned, chunk), BF), S((piece, width), BF),
              S((rows, QDIM), BF), S((rows, width), F32), S((rows, width), F32), S((rows, width), F32)]
    anys = pl.BlockSpec(memory_space=pl.ANY)
    vmem = pl.BlockSpec(memory_space=pltpu.VMEM)
    all_rows = V((n, rows, width), BF)
    hidden = V((n, rows, chunk), BF)
    scratch = [V((2, N * owned, chunk), BF), V((4 * piece, width), BF), all_rows, all_rows, V((n, 2, rows // 2, chunk), BF), hidden, hidden,
               all_rows, V((2, rows, width // 2), BF), V((2, n // 2 - 1, rows, width), BF),
               all_rows, V((2, rows, width // 2), BF), V((2, n // 2 - 1, rows, width), BF),
               V((2, 2, 2, m, 2, owned, chunk), BF), V((2, 2, piece, width), BF), V((2, 2, m, 2, owned, chunk), BF),
               V((2, piece, width), BF), V((piece, width), BF),
               V((2, 2, m, 2, owned, width // 4), BF),
               V((m, 2, rows, 2 * KVDIM), BF), V((HEADS, rows, HEAD), BF), V((2, rows, HEAD), F32)]
    a, b = chunk // 384, width // 384
    scratch += [DMA((6,)), DMA((9,)), DMA((7, m + 5)), DMA((7, m + 5)), DMA((N,)), DMA((n,)), DMA((2,)), DMA((n,)), DMA((N,)),
                DMA((4,)), DMA((1,)), DMA((4,)), DMA((2, m)), DMA((2, m)), DMA((m,)), DMA((m,)), DMA((m,)), DMA((m,))]
    scratch += [DMA((2, m))] * 6 + [DMA((2, a))] * 3 + [DMA((b,))] * 5
    return pl.pallas_call(
        functools.partial(layer_kernel, n),
        out_shape=shapes,
        in_specs=[pl.BlockSpec(memory_space=pltpu.SMEM)] + [vmem] * 9 + [anys] * 2,
        out_specs=[anys] * 6 + [vmem] * 4,
        scratch_shapes=scratch,
        compiler_params=pltpu.CompilerParams(collective_id=0, has_side_effects=True, vmem_limit_bytes=63 * 2**20),
    )(length, x, og, qkv, gain_one, bias, gate, up, gain_two, down, outw, tables)


class Reduce:
    def __init__(self, pc, far_first, p, r0, r1, r2, r3, ss, rs, i):
        self.pc, self.far_first, self.p = pc, far_first, p
        self.r0, self.r1, self.r2, self.r3, self.ss, self.rs, self.i = r0, r1, r2, r3, ss, rs, i
        self.y, self.x, self.z = pc.s // 2, lax.rem(pc.c, 2), pc.c // 2
        self.xp = pc.c + 1 - 2 * self.x
    def go(self, k, src, dst, seq, ctx):
        send(src, dst, self.ss.at[self.i, k], self.rs.at[self.i, k], seq, ctx)
    def come(self, k, dst):
        arrived(dst, self.rs.at[self.i, k], self.pc)
    def stage0(self):
        pc = self.pc
        self.go(0, self.p.at[:, 1 - pc.core], self.r0, pc.sib, pc.c)
    def stage1(self):
        pc, r0 = self.pc, self.r0
        self.come(0, r0)
        r0[...] = add_low(r0[...], self.p[:, pc.core])
        if self.far_first: self.go(1, r0.at[1 - self.y], self.r1, pc.far, pc.c)
        else: self.go(1, r0.at[:, :, 1 - self.x], self.r1, pc.s, self.xp)
    def stage2(self):
        pc, r0, r1 = self.pc, self.r0, self.r1
        self.come(1, r1)
        if self.far_first:
            r1[...] = add_low(r1[...], r0[self.y])
            self.go(2, r1.at[:, 1 - self.x], self.r2, pc.s, self.xp)
        else:
            r1[...] = add_low(r1[...], r0[:, :, self.x])
            self.go(2, r1.at[1 - self.y], self.r2, pc.far, pc.c)
    def stage3(self):
        pc, r1, r2, n = self.pc, self.r1, self.r2, self.pc.n
        self.come(2, r2)
        r2[...] = add_low(r2[...], r1[:, self.x] if self.far_first else r1[self.y])
        def hand(d, w):
            to = lax.rem(self.z + d, n // 2)
            send(r2.at[to], self.r3.at[self.z], self.ss.at[self.i, 2 + d], self.rs.at[self.i, 2 + d], pc.s, 2 * to + self.x)
            return w
        lax.fori_loop(1, n // 2, hand, 0)
    def stage4(self):
        n = self.pc.n
        total = self.r2[self.z].astype(F32)
        for d in range(1, n // 2):
            src = lax.rem(self.z + n // 2 - d, n // 2)
            arrived(self.r3.at[src], self.rs.at[self.i, 2 + d], self.pc)
            total = total + self.r3[src].astype(F32)
        return total
    def finish(self):
        sent(self.r0, self.ss.at[self.i, 0], self.pc)
        sent(self.r1, self.ss.at[self.i, 1], self.pc)
        sent(self.r2, self.ss.at[self.i, 2], self.pc)
        for d in range(1, self.pc.n // 2):
            sent(self.r2.at[0], self.ss.at[self.i, 2 + d], self.pc)

def backward_kernel(n, length_ref, x_ref, og_ref, mid_ref, u_ref, o_ref, att_ref, q_ref, kv_ref, out_ref, gate_ref, up_ref, qw_ref, gain_ref, gain_one_ref, qkv_all, tables, half_sum,
                    y_out, dx_out, dout_out, dqkv_out, dbias_out, dgate_out, dup_out, dgain_out, dgain_one_out,
                    tab_v, gm_v, gb_v, dm_v, gp_v, p_v, gs_v, dkv_v, kx, kz, raw_v, r1_v, mine_v, dx_v, qkv_v, *rest):
    pieces = 7
    bufs, (local, kxs, kxr, kzs, kzr, gss, grs, fs, fr, ss, rs) = rest[: 5 * pieces], rest[5 * pieces :]
    pc = Place(n)
    s, c = pc.s, pc.c
    rows, width = x_ref.shape
    total = n * rows
    length = length_ref[0]
    x, z = lax.rem(c, 2), c // 2
    xp = c + 1 - 2 * x
    red = [Reduce(pc, i % 2 == 0, *bufs[5 * i : 5 * i + 5], ss, rs, i) for i in range(pieces)]
    tab = pltpu.make_async_copy(tables.at[:, pl.ds(pl.multiple_of(c * rows, rows), rows), :], tab_v, local.at[0])
    tab.start()
    y = s // 2
    mine = pltpu.make_async_copy(half_sum.at[:, y], mine_v, local.at[1])
    mine.start()
    weights = pltpu.make_async_copy(qkv_all, qkv_v, local.at[2])
    weights.start()
    enter(pc)
    owned = out_ref.shape[1]
    def cross(a):
        send(half_sum.at[a, 1 - y], r1_v.at[a], fs.at[a], fr.at[a], pc.far, c)
    def feed(a):
        arrived(r1_v.at[a], fr.at[a], pc)
        if a == 0:
            cross(1)
            mine.wait()
        r1_v[a] = add_low(r1_v[a], mine_v[a])
        def hand(d, w):
            to = lax.rem(c + d, n)
            send(r1_v.at[a, to // 2, lax.rem(to, 2)], raw_v.at[c, a], gss.at[a, to], grs.at[a, c], s, to)
            return w
        lax.fori_loop(1, n, hand, 0)
        raw_v[c, a] = r1_v[a, c // 2, lax.rem(c, 2)]
    def fed(a):
        def come(d, w):
            src = lax.rem(c + d, n)
            arrived(raw_v.at[src, a], grs.at[a, src], pc)
            return w
        lax.fori_loop(1, n, come, 0)
    cross(0)
    pos = c * rows + lax.broadcasted_iota(jnp.int32, (rows, width), 0)
    live = pos < length
    mid = mid_ref[...]
    gm = jnp.where(live, og_ref[...].astype(F32), 0.0) + rms_back(mid, inverse_rms(mid), u_ref[...])
    gm_v[...] = gm
    gb_v[...] = gm.astype(BF)
    y_out[...] = jnp.where(live, mid + o_ref[...], 0.0).astype(BF)
    owners = 4 * n
    def mix(j, w):
        weight = out_ref[pl.ds(j * 8, 8)].reshape(8 * owned, width)
        r = contract_cols(gb_v[...], weight).astype(BF)
        for k in range(8 * owned // HEAD):
            dm_v[j * (8 * owned // HEAD) + k] = r[:, k * HEAD : (k + 1) * HEAD]
        return w
    lax.fori_loop(0, owners // 8, mix, 0)
    gb = gb_v[...]
    for i in range(2):
        w = width // 2
        grad = contract_rows(att_ref[...], gb[:, i * w : (i + 1) * w])
        red[i].p[...] = grad.astype(BF).reshape(red[i].p.shape)
        red[i].stage0()
    tab.wait()
    tc, ts = tab_v[0], tab_v[1]

    at_row = c * rows + lax.broadcasted_iota(jnp.int32, (rows, total), 0)
    at_col = lax.broadcasted_iota(jnp.int32, (rows, total), 1)
    allowed = (at_col <= at_row) & (at_col < length)
    def group(g):
        key = kv_ref[:, :, g * HEAD : (g + 1) * HEAD].reshape(total, HEAD)
        val = kv_ref[:, :, KVDIM + g * HEAD : KVDIM + (g + 1) * HEAD].reshape(total, HEAD)
        def head(i, w):
            h = g * GROUP + i
            part = pl.ds(pl.multiple_of(i * rows, rows), rows)
            scores = jnp.where(allowed, contract_cols(q_ref[h], key) * SCALE, MASKED)
            e = jnp.exp(scores - jnp.max(scores, axis=1, keepdims=True))
            probs = e * (1.0 / jnp.sum(e, axis=1, keepdims=True))
            gprobs = contract_cols(dm_v[h], val)
            inner = jnp.sum(probs * gprobs, axis=1, keepdims=True)
            gs = (probs * (gprobs - inner)).astype(BF)
            p_v[part, :] = probs.astype(BF)
            gs_v[part, :] = gs
            dq = product(gs, key) * SCALE
            gp_v[:, pl.ds(pl.multiple_of(h * HEAD, HEAD), HEAD)] = (dq * tc - pltpu.roll(dq, HEAD // 2, 1) * ts).astype(BF)
            return w
        lax.fori_loop(0, GROUP, head, 0)
        mine = slice(g * GROUP, (g + 1) * GROUP)
        dk = contract_rows(gs_v[...], q_ref[mine].reshape(GROUP * rows, HEAD)) * SCALE
        dv = contract_rows(p_v[...], dm_v[mine].reshape(GROUP * rows, HEAD))
        lanes = slice(g * 2 * HEAD, g * 2 * HEAD + 2 * HEAD)
        dkv_v[:, :, :, lanes] = jnp.concatenate([dk, dv], 1).astype(BF).reshape(n // 2, 2, rows, 2 * HEAD)
        send(dkv_v.at[:, 1 - x, :, lanes], kx.at[:, :, lanes], kxs.at[g], kxr.at[g], s, xp)
    def kv_x(g):
        lanes = slice(g * 2 * HEAD, g * 2 * HEAD + 2 * HEAD)
        arrived(kx.at[:, :, lanes], kxr.at[g], pc)
        kx[:, :, lanes] = add_low(kx[:, :, lanes], dkv_v[:, x, :, lanes])
        for d in range(1, n // 2):
            to = lax.rem(z + d, n // 2)
            send(kx.at[to, :, lanes], kz.at[z, :, lanes], kzs.at[g, d], kzr.at[g, d], s, 2 * to + x)
    def kv_z(g):
        lanes = slice(g * 2 * HEAD, g * 2 * HEAD + 2 * HEAD)
        sumkv = kx[z, :, lanes].astype(F32)
        for d in range(1, n // 2):
            src = lax.rem(z + n // 2 - d, n // 2)
            arrived(kz.at[src, :, lanes], kzr.at[g, d], pc)
            sumkv = sumkv + kz[src, :, lanes].astype(F32)
        dk, dv = sumkv[:, :HEAD], sumkv[:, HEAD:]
        k0, v0 = QDIM + g * HEAD, QDIM + KVDIM + g * HEAD
        gp_v[:, k0 : k0 + HEAD] = (dk * tc - pltpu.roll(dk, HEAD // 2, 1) * ts).astype(BF)
        gp_v[:, v0 : v0 + HEAD] = dv.astype(BF)
    xin = x_ref[...].astype(F32)
    inverse = inverse_rms(xin)
    def joint(i, first, w):
        xh = (x_ref[...].astype(F32) * inverse).astype(BF)
        grad = contract_rows(xh, gp_v[:, first : first + w]).astype(BF)
        shape = red[i].p.shape[:-1] + (w,)
        red[i].p[..., :w] = grad.reshape(shape)
    group(0)
    red[0].stage1(); red[1].stage1()
    feed(0)
    group(1)
    kv_x(0)
    red[0].stage2(); red[1].stage2()
    third = QDIM // 3
    for i in range(3):
        joint(2 + i, i * third, third)
        red[2 + i].stage0()
        if i == 0: kv_x(1)
    red[0].stage3(); red[1].stage3()
    red[2].stage1(); red[3].stage1(); red[4].stage1()
    feed(1)
    kv_z(0); kv_z(1)
    joint(5, QDIM, KVDIM)
    joint(6, QDIM + KVDIM, KVDIM)
    red[6].stage0()
    sums = jnp.sum(gp_v[...].astype(F32), axis=0, keepdims=True)
    p5 = red[5].p
    qk_width = QDIM + KVDIM
    at = lax.broadcasted_iota(jnp.int32, (owned, HEAD), 0)
    for d in range(owners):
        tiles = (qk_width // owners * d // HEAD, qk_width // owners * d // HEAD + 1, (qk_width + KVDIM // owners * d) // HEAD)
        part = jnp.zeros((owned, HEAD), F32)
        for k, t in enumerate(tiles):
            part = jnp.where(at == k, sums[:, t * HEAD : t * HEAD + HEAD], part)
        plane = d // n
        p5[plane // 2, plane % 2, d % n // 2, d % 2, :, KVDIM:] = part.astype(BF)
    red[5].stage0()
    red[2].stage2(); red[3].stage2(); red[4].stage2()
    red[6].stage1(); red[5].stage1()
    qk = QDIM + 2 * KVDIM
    gp = gp_v[...]
    weights.wait()
    def back(j, w):
        weight = qkv_v[pl.ds(j * 8, 8), :, :qk].reshape(8 * owned, qk)
        cols = pl.ds(pl.multiple_of(j * 8 * owned, 8 * owned), 8 * owned)
        dx_v[:, cols] = contract_cols(gp, weight)
        return w
    lax.fori_loop(0, owners // 8, back, 0)
    red[2].stage3(); red[3].stage3(); red[4].stage3()
    red[6].stage2(); red[5].stage2()
    fed(0)
    place_back(raw_v, 0, dgate_out)
    dx_out[...] = (gm_v[...] + rms_back(x_ref[...].astype(F32), inverse, dx_v[...])).astype(BF)
    for i in range(2):
        dout_out[:, i * (width // 2) : (i + 1) * (width // 2)] = red[i].stage4()
    red[6].stage3(); red[5].stage3()
    fed(1)
    place_back(raw_v, 1, dup_out)
    gain = column(gain_ref[...])
    dgain_out[...] = as_row(jnp.sum(
        dgate_out[...] * gate_ref[...].astype(F32) + dup_out[...] * up_ref[...].astype(F32), axis=1, keepdims=True
    ))
    dgate_out[...] = dgate_out[...] * gain
    dup_out[...] = dup_out[...] * gain
    gain_one = column(gain_one_ref[...])
    rows_sum = jnp.zeros((owned, 1), F32)
    for i in range(3):
        cols = slice(i * third, (i + 1) * third)
        raw = red[2 + i].stage4()
        rows_sum = rows_sum + jnp.sum(raw * qw_ref[:, cols].astype(F32), axis=1, keepdims=True)
        dqkv_out[:, cols] = raw * gain_one
    for i, first in ((6, QDIM + KVDIM), (5, QDIM)):
        cols = slice(first, first + KVDIM)
        whole = red[i].stage4()
        raw = whole[:, :KVDIM]
        rows_sum = rows_sum + jnp.sum(raw * qw_ref[:, cols].astype(F32), axis=1, keepdims=True)
        dqkv_out[:, cols] = raw * gain_one
    dbias_out[...] = whole[:8, KVDIM:]
    dgain_one_out[...] = as_row(rows_sum)
    for r in red: r.finish()
    for a in range(2):
        sent(r1_v.at[a], fs.at[a], pc)
        def left(d, w):
            sent(raw_v.at[0, a], gss.at[a, lax.rem(c + d, n)], pc)
            return w
        lax.fori_loop(1, n, left, 0)
    for g in range(2):
        lanes = slice(g * 2 * HEAD, g * 2 * HEAD + 2 * HEAD)
        sent(kx.at[:, :, lanes], kxs.at[g], pc)
        for d in range(1, n // 2): sent(kx.at[0, :, lanes], kzs.at[g, d], pc)

def backward_call(n, length, x, og, mid, u, o, att, q, kv, out_all, gate, up, qkv, gain, gain_one, qkv_all, tables, half_sum):
    S, V = jax.ShapeDtypeStruct, pltpu.VMEM
    rows, width = x.shape
    owned = qkv_all.shape[1]
    anys = pl.BlockSpec(memory_space=pl.ANY)
    vmem = pl.BlockSpec(memory_space=pltpu.VMEM)
    m = n // 2
    scratch = [V((2, rows, HEAD), F32), V((rows, width), F32), V((rows, width), BF), V((HEADS, rows, HEAD), BF),
               V((rows, QDIM + 2 * KVDIM), BF), V((GROUP * rows, n * rows), BF), V((GROUP * rows, n * rows), BF),
               V((m, 2, rows, 2 * KVDIM), BF), V((m, rows, 2 * KVDIM), BF), V((m, rows, 2 * KVDIM), BF),
               V((n, 2, owned, half_sum.shape[-1]), BF), V((2,) + half_sum.shape[2:], BF), V((2,) + half_sum.shape[2:], BF),
               V((rows, width), F32), V(qkv_all.shape, BF)]
    for i, w in enumerate((width // 2, width // 2, QDIM // 3, QDIM // 3, QDIM // 3, KVDIM + HEAD, KVDIM)):
        one = (m, 2, owned, w) if i % 2 == 0 else (2, m, owned, w)
        scratch += [V((2, 2, m, 2, owned, w), BF), V((2, m, 2, owned, w), BF), V(one, BF), V((m, owned, w), BF), V((m, owned, w), BF)]
    scratch += [DMA((3,)), DMA((2,)), DMA((2,)), DMA((2, m)), DMA((2, m)), DMA((2, n)), DMA((2, n)), DMA((2,)), DMA((2,)), DMA((7, 2 + m)), DMA((7, 2 + m))]
    return pl.pallas_call(
        functools.partial(backward_kernel, n),
        out_shape=[S((rows, width), BF), S((rows, width), BF), S((owned, width), F32), S(qkv.shape, F32), S((8, HEAD), F32),
                   S(gate.shape, F32), S(gate.shape, F32), S((1, owned), F32), S((1, owned), F32)],
        in_specs=[pl.BlockSpec(memory_space=pltpu.SMEM)] + [vmem] * 14 + [anys] * 3,
        out_specs=[vmem] * 9,
        scratch_shapes=scratch,
        compiler_params=pltpu.CompilerParams(collective_id=2, has_side_effects=True, vmem_limit_bytes=62 * 2**20),
    )(length, x, og, mid, u, o, att, q, kv, out_all, gate, up, qkv, gain, gain_one, qkv_all, tables, half_sum)


def kernel_shards(
    tokens,
    lengths,
    attn_gain,
    qkv_weight,
    qkv_bias,
    out_weight,
    mlp_gain,
    gate_weight,
    up_weight,
    down_weight,
    out_grad,
):
    seqs, parts = lax.axis_size("seq"), lax.axis_size("ctx")
    rows, width = tokens.shape[1:]
    owned = gate_weight.shape[0]
    piece = down_weight.shape[0]
    owners = seqs * parts
    me = lax.axis_index("seq") * parts + lax.axis_index("ctx")
    gain_one, gain_two = attn_gain[None], mlp_gain[None]
    half = HEAD // 2
    frequency = np.float32(ROPE_BASE) ** (-np.arange(half, dtype=np.float32) * np.float32(2.0 / HEAD))
    angles = np.arange(rows * parts, dtype=np.float32)[:, None] * frequency.astype(np.float32)[None, :]
    cosine, sine = np.cos(angles), np.sin(angles)
    tables = jnp.asarray(np.stack([np.concatenate([cosine, cosine], 1), np.concatenate([-sine, sine], 1)]), F32)
    x, og = tokens[0], out_grad[0]
    qkv_all, out_all, kv_all, q, half_sum, grad_down, att, mid, u, o = layer_call(
        parts, lengths, x, og, qkv_weight, gain_one, qkv_bias[None], gate_weight, up_weight, gain_two,
        down_weight, out_weight, tables,
    )
    joint = qkv_all.shape[-1]
    output, grad_inputs, grad_out, grad_qkv, bias_rows, grad_gate, grad_up, grad_mlp_gain, grad_attn_gain = backward_call(
        parts, lengths, x, og, mid, u, o, att, q, kv_all.reshape(parts, rows, 2 * KVDIM),
        out_all.reshape(owners, owned, width), gate_weight, up_weight, qkv_weight, gain_two, gain_one,
        qkv_all.reshape(owners, owned, joint), tables, half_sum,
    )
    per, per_value = (QDIM + KVDIM) // owners, KVDIM // owners
    grad_qk_bias = lax.dynamic_slice_in_dim(bias_rows[:2].reshape(2 * HEAD), lax.rem(per * me, HEAD), per)
    grad_value_bias = lax.dynamic_slice_in_dim(bias_rows[2], lax.rem(per_value * me, HEAD), per_value)
    return (
        output[None],
        grad_inputs[None],
        grad_attn_gain[0],
        grad_qkv,
        grad_qk_bias,
        grad_out,
        grad_mlp_gain[0],
        grad_gate,
        grad_up,
        grad_down[:piece].astype(F32),
        grad_value_bias,
    )


def solution(mesh):
    seqs, parts = mesh.shape["seq"], mesh.shape["ctx"]
    tiled = seqs == 4 and parts == 8 and 1536 // (seqs * parts) % 16 == 0
    rows, vector = P(BOTH, None), P(BOTH)
    token = P("seq", "ctx", None)
    return jax.shard_map(
        kernel_shards if tiled else plain_shards,
        mesh=mesh,
        in_specs=(token, P("seq"), vector, rows, vector, rows, vector, rows, rows, rows, token),
        out_specs=(token, token, vector, rows, vector, rows, vector, rows, rows, rows, vector),
        check_vma=False,
    )
```

```python
import functools

import jax
import jax.numpy as jnp
import numpy as np
from jax import lax
from jax.experimental import pallas as pl
from jax.experimental.pallas import tpu as pltpu
from jax.sharding import PartitionSpec as P

HEADS = 12
KV_HEADS = 2
HEAD = 128
QDIM = 1536
KVDIM = 256
GROUP = HEADS // KV_HEADS

EPSILON = 1e-06
ROPE_BASE = 1000000.0
MASKED = -1e30
SCALE = HEAD ** (-0.5)
BF = jnp.bfloat16
F32 = jnp.float32
BOTH = ("seq", "ctx")


DMA = pltpu.SemaphoreType.DMA
MESH = pl.DeviceIdType.MESH


def product(left, right):
    return jnp.dot(left, right, preferred_element_type=F32)


def contract_rows(left, right):
    return lax.dot_general(left, right, (((0,), (0,)), ((), ())), preferred_element_type=F32)


def contract_cols(left, right):
    return lax.dot_general(left, right, (((1,), (1,)), ((), ())), preferred_element_type=F32)


def inverse_rms(values):
    return lax.rsqrt(jnp.mean(values * values, axis=-1, keepdims=True) + EPSILON)


def rms_back(values, inverse, scaled_grad):
    inner = jnp.mean(scaled_grad * values, axis=-1, keepdims=True)
    return inverse * scaled_grad - values * (inverse * inverse * inverse) * inner


def rope_tables(positions):
    half = HEAD // 2
    frequency = ROPE_BASE ** (-jnp.arange(half, dtype=F32) * 2.0 / HEAD)
    angles = positions.astype(F32)[:, None] * frequency[None, :]
    return jnp.cos(angles), jnp.sin(angles)


def rotate(values, cosine, sine):
    half = HEAD // 2
    first, second = values[..., :half], values[..., half:]
    cosine, sine = cosine[:, None, :], sine[:, None, :]
    return jnp.concatenate([first * cosine - second * sine, second * cosine + first * sine], -1)


def gather(values, axes):
    return lax.all_gather(values, axes, axis=0, tiled=True)


def scatter(values, axes):
    return lax.psum_scatter(values, axes, scatter_dimension=0, tiled=True)


def plain_shards(
    tokens,
    lengths,
    attn_gain,
    qkv_weight,
    qkv_bias,
    out_weight,
    mlp_gain,
    gate_weight,
    up_weight,
    down_weight,
    out_grad,
):
    seqs, parts = lax.axis_size("seq"), lax.axis_size("ctx")
    inputs = tokens[0].astype(F32)
    rows, width = inputs.shape
    owned, hidden = gate_weight.shape
    piece = down_weight.shape[0]
    chunk = hidden // parts
    length = lengths[0]
    positions = lax.axis_index("ctx") * rows + jnp.arange(rows, dtype=jnp.int32)
    living = (positions < length).astype(F32)[:, None]
    cosine, sine = rope_tables(positions)

    gain_one = attn_gain.astype(F32)[:, None]
    gain_two = mlp_gain.astype(F32)[:, None]
    qkv_all = gather((qkv_weight.astype(F32) * gain_one).astype(BF), BOTH)
    bias_all = gather(qkv_bias, BOTH).astype(F32)
    out_all = gather(out_weight, BOTH)

    def to_chunks(weight):
        scaled = (weight.astype(F32) * gain_two).astype(BF)
        return scaled.reshape(owned, seqs, parts, piece).transpose(2, 0, 1, 3)

    both = jnp.stack([to_chunks(gate_weight), to_chunks(up_weight)], axis=1)
    both = lax.all_to_all(both.reshape(parts, 2, owned, chunk), "ctx", 0, 0)
    both = lax.all_gather(both, "seq", axis=0)
    gate_chunk = both[:, :, 0].reshape(width, chunk)
    up_chunk = both[:, :, 1].reshape(width, chunk)
    down_chunk = gather(down_weight, "seq")
    cotangent = out_grad[0].astype(F32) * living
    cot_all = gather(cotangent.astype(BF), "ctx")

    inverse_one = inverse_rms(inputs)
    normed_one = (inputs * inverse_one).astype(BF)
    project = product(normed_one, qkv_all) + bias_all
    queries = rotate(project[:, :QDIM].reshape(rows, HEADS, HEAD), cosine, sine).astype(BF)
    own_keys = rotate(
        project[:, QDIM : QDIM + KVDIM].reshape(rows, KV_HEADS, HEAD), cosine, sine
    ).astype(BF)
    own_values = project[:, QDIM + KVDIM :].astype(BF).reshape(rows, KV_HEADS, HEAD)
    keys, values = gather(own_keys, "ctx"), gather(own_values, "ctx")
    key_pos = jnp.arange(rows * parts, dtype=jnp.int32)
    allowed = (key_pos[None, :] <= positions[:, None]) & (key_pos[None, :] < length)
    grouped = queries.reshape(rows, KV_HEADS, GROUP, HEAD)
    scores = jnp.einsum("qgha,kga->ghqk", grouped, keys, preferred_element_type=F32) * SCALE
    scores = jnp.where(allowed, scores, MASKED)
    largest = jnp.max(scores, axis=-1, keepdims=True)
    exponent = jnp.exp(scores - largest)
    summed = jnp.sum(exponent, axis=-1, keepdims=True)
    probs = exponent / summed
    probs_low = probs.astype(BF)
    attended = jnp.einsum("ghqk,kga->qgha", probs_low, values, preferred_element_type=F32)
    attended = attended.reshape(rows, QDIM).astype(BF)
    middle = inputs + product(attended, out_all)

    inverse_two = inverse_rms(middle)
    normed_two = gather((middle * inverse_two).astype(BF), "ctx")
    gate_pre = product(normed_two, gate_chunk)
    up_pre = product(normed_two, up_chunk)
    sig = jax.nn.sigmoid(gate_pre)
    activated = (gate_pre * sig * up_pre).astype(BF)
    grad_act = contract_cols(cot_all, down_chunk)
    grad_gate = (grad_act * up_pre * (sig + gate_pre * sig * (1.0 - sig))).astype(BF)
    grad_up = (grad_act * gate_pre * sig).astype(BF)
    scaled_two = contract_cols(grad_gate, gate_chunk) + contract_cols(grad_up, up_chunk)
    scaled_two = scatter(scaled_two.astype(BF), "ctx").astype(F32)
    branch = scatter(product(activated, down_chunk).astype(BF), "ctx").astype(F32)
    output = ((middle + branch) * living).astype(BF)
    grad_down = scatter(contract_rows(activated, cot_all).astype(BF), "seq").astype(F32)
    raw = jnp.stack([contract_rows(normed_two, grad_gate), contract_rows(normed_two, grad_up)], 1)
    raw = scatter(raw.astype(BF), "seq").reshape(parts, owned, 2, chunk)
    raw = lax.all_to_all(raw, "ctx", 0, 0).astype(F32)
    raw = raw.reshape(parts, owned, 2, seqs, piece).transpose(2, 1, 3, 0, 4)
    raw = raw.reshape(2, owned, hidden)
    grad_mlp_gain = jnp.sum(raw[0] * gate_weight.astype(F32) + raw[1] * up_weight.astype(F32), 1)

    grad_middle = cotangent + rms_back(middle, inverse_two, scaled_two)
    grad_branch = grad_middle.astype(BF)
    grad_out = scatter(contract_rows(attended, grad_branch).astype(BF), BOTH).astype(F32)
    grad_mixed = contract_cols(grad_branch, out_all).astype(BF)
    grad_mixed = grad_mixed.reshape(rows, KV_HEADS, GROUP, HEAD)
    grad_probs = jnp.einsum("qgha,kga->ghqk", grad_mixed, values, preferred_element_type=F32)
    inner = jnp.sum(probs * grad_probs, axis=-1, keepdims=True)
    grad_scores = (probs * (grad_probs - inner)).astype(BF)
    grad_q = jnp.einsum("ghqk,kga->qgha", grad_scores, keys, preferred_element_type=F32) * SCALE
    grad_k = jnp.einsum("ghqk,qgha->kga", grad_scores, grouped, preferred_element_type=F32) * SCALE
    grad_v = jnp.einsum("ghqk,qgha->kga", probs_low, grad_mixed, preferred_element_type=F32)
    grad_k = scatter(grad_k.astype(BF), "ctx").astype(F32)
    grad_v = scatter(grad_v.astype(BF), "ctx").astype(F32)
    grad_q = rotate(grad_q.reshape(rows, HEADS, HEAD), cosine, -sine).reshape(rows, QDIM)
    grad_k = rotate(grad_k, cosine, -sine).reshape(rows, KVDIM)
    grad_project = jnp.concatenate([grad_q, grad_k, grad_v.reshape(rows, KVDIM)], axis=1)
    grad_project = grad_project.astype(BF)
    raw_qkv = scatter(contract_rows(normed_one, grad_project).astype(BF), BOTH).astype(F32)
    grad_attn_gain = jnp.sum(raw_qkv * qkv_weight.astype(F32), axis=1)
    grad_bias = jnp.sum(grad_project.astype(F32), axis=0)
    qk_width = QDIM + KVDIM
    grad_qk_bias = scatter(grad_bias[:qk_width], BOTH)
    grad_value_bias = scatter(grad_bias[qk_width:], BOTH)
    scaled_one = contract_cols(grad_project, qkv_all)
    grad_inputs = (grad_middle + rms_back(inputs, inverse_one, scaled_one)).astype(BF)
    return (
        output[None],
        grad_inputs[None],
        grad_attn_gain,
        raw_qkv * gain_one,
        grad_qk_bias,
        grad_out,
        grad_mlp_gain,
        raw[0] * gain_two,
        raw[1] * gain_two,
        grad_down,
        grad_value_bias,
    )


class Place:
    def __init__(self, n):
        self.n = n
        self.s, self.c = lax.axis_index("seq"), lax.axis_index("ctx")
        self.me = self.s * n + self.c
        self.core = lax.rem(self.s, 2)
        self.sib = self.s + 1 - 2 * self.core
        self.far = lax.rem(self.s + 2, 4)
        half = self.c // 2
        self.pos = half + lax.rem(self.c, 2) * (n - 1 - 2 * half)
        self.nxt, self.prv = self.at(1), self.at(-1)
    def at(self, offset):
        p = lax.rem(self.pos + offset + 2 * self.n, self.n)
        return 2 * p + (p // (self.n // 2)) * (2 * self.n - 1 - 4 * p)

def send(src, dst, ssem, rsem, seq, ctx):
    copy = pltpu.make_async_remote_copy(src, dst, ssem, rsem, device_id=(seq, ctx), device_id_type=MESH)
    copy.start()

def arrived(dst, rsem, place):
    pltpu.make_async_remote_copy(dst, dst, rsem, rsem, device_id=(place.s, place.c), device_id_type=MESH).wait_recv()

def sent(src, ssem, place):
    pltpu.make_async_remote_copy(src, src, ssem, ssem, device_id=(place.s, place.c), device_id_type=MESH).wait_send()

def greet_all(place):
    barrier = pltpu.get_barrier_semaphore()
    def greet(d, z):
        pl.semaphore_signal(barrier, inc=1, device_id=(place.s, lax.rem(place.c + d, place.n)), device_id_type=MESH)
        return z
    lax.fori_loop(1, place.n, greet, 0)
    pl.semaphore_signal(barrier, inc=1, device_id=(place.sib, place.c), device_id_type=MESH)
    pl.semaphore_signal(barrier, inc=1, device_id=(place.far, place.c), device_id_type=MESH)

def enter(place):
    greet_all(place)
    pl.semaphore_wait(pltpu.get_barrier_semaphore(), place.n + 1)


def add_low(left, right):
    return (left.astype(F32) + right.astype(F32)).astype(BF)

def diagonal(n):
    return lax.broadcasted_iota(jnp.int32, (n, n), 0) == lax.broadcasted_iota(jnp.int32, (n, n), 1)

def column(row):
    return jnp.sum(jnp.where(diagonal(row.shape[1]), row.astype(F32), 0.0), axis=1, keepdims=True)

def as_row(values):
    return jnp.sum(jnp.where(diagonal(values.shape[0]), values, 0.0), axis=0, keepdims=True)

class RingGather:
    def __init__(self, pc, slots, ssem, rsem, index=None):
        self.pc, self.slots, self.ssem, self.rsem, self.index = pc, slots, ssem, rsem, index
        self.steps, self.half = pc.n // 2, slots.shape[2] // 2
        self.ways = ((0, -1, pc.nxt), (1, 1, pc.prv))
    def slot(self, offset):
        return self.index[offset] if self.index else self.pc.at(offset)
    def part(self, ref, f, t):
        return ref if t < self.steps - 1 else ref.at[:, pl.ds(f * self.half, self.half)]
    def hop(self, t, own=None):
        for f, sign, to in self.ways:
            src = self.slots.at[self.slot(sign * t)] if own is None else own
            there = self.slots.at[self.slot(sign * (t + 1) if self.index else sign * t)]
            send(self.part(src, f, t), self.part(there, f, t), self.ssem.at[f, t], self.rsem.at[f, t], self.pc.s, to)
    def turn(self, t):
        for f, sign, _ in self.ways:
            arrived(self.part(self.slots.at[self.slot(sign * (t + 1))], f, t), self.rsem.at[f, t], self.pc)
        if t + 1 < self.steps: self.hop(t + 1)
    def finish(self):
        for f in range(2):
            for t in range(self.steps): sent(self.part(self.slots.at[0], f, t), self.ssem.at[f, t], self.pc)

class RingSum:
    def __init__(self, pc, term, index, held_half, held, ssem, rsem, out):
        self.pc, self.term, self.index, self.out = pc, term, index, out
        self.held_half, self.held, self.ssem, self.rsem = held_half, held, ssem, rsem
        self.steps, self.half = pc.n // 2, term.shape[2] // 2
    def turn(self, t):
        pc, ahead = self.pc, self.steps - t
        for f, sign, to in ((0, 1, pc.nxt), (1, -1, pc.prv)):
            cols = slice(f * self.half, (f + 1) * self.half)
            i = self.index[sign * ahead]
            if t == 1:
                arrived(self.held_half.at[f], self.rsem.at[f, 0], pc)
                self.term[i, :, cols] = add_low(self.term[i, :, cols], self.held_half[f])
            elif t > 1:
                arrived(self.held.at[f, t - 2], self.rsem.at[f, t - 1], pc)
                if t < self.steps: self.term[i] = add_low(self.term[i], self.held[f, t - 2])
            if t == 0:
                src, dst = self.term.at[i, :, pl.ds(f * self.half, self.half)], self.held_half.at[f]
            elif t < self.steps:
                src, dst = self.term.at[i], self.held.at[f, t - 1]
            if t < self.steps: send(src, dst, self.ssem.at[f, t], self.rsem.at[f, t], pc.s, to)
        if t == self.steps:
            i = self.index[0]
            self.out[...] = self.term[i].astype(F32) + self.held[0, t - 2].astype(F32) + self.held[1, t - 2].astype(F32)
    def finish(self):
        for f in range(2):
            sent(self.held_half.at[f], self.ssem.at[f, 0], self.pc)
            for t in range(1, self.steps): sent(self.held.at[f, 0], self.ssem.at[f, t], self.pc)

class Spread:
    def __init__(self, pc, x_first, w, ss, rs, i):
        self.pc, self.x_first, self.w, self.ss, self.rs, self.i = pc, x_first, w, ss, rs, i
        self.y, self.x, self.z = pc.s // 2, lax.rem(pc.c, 2), pc.c // 2
        self.xp = pc.c + 1 - 2 * self.x
        self.deep = pc.n // 2
    def go(self, k, part, seq, ctx):
        send(part, part, self.ss.at[self.i, k], self.rs.at[self.i, k], seq, ctx)
    def come(self, k, part):
        arrived(part, self.rs.at[self.i, k], self.pc)
    def both(self, k, part, sib_k, seq, ctx, sib_part):
        self.go(k, part, seq, ctx)
        self.go(sib_k, sib_part, self.pc.sib, self.pc.c)
    def begin(self):
        own = self.w.at[self.y, self.pc.core, self.z, self.x]
        for d in range(1, self.deep):
            self.go(d - 1, own, self.pc.s, 2 * lax.rem(self.z + d, self.deep) + self.x)
    def stage1(self):
        pc, w, y, x = self.pc, self.w, self.y, self.x
        for d in range(1, self.deep):
            self.come(d - 1, w.at[y, pc.core, lax.rem(self.z + self.deep - d, self.deep), x])
        column = w.at[y, pc.core, :, x]
        if self.x_first: self.both(self.deep, column, self.deep + 2, pc.s, self.xp, column)
        else: self.both(self.deep, column, self.deep + 2, pc.far, pc.c, column)
    def stage2(self):
        pc, w, y, x = self.pc, self.w, self.y, self.x
        if self.x_first:
            new = w.at[y, pc.core, :, 1 - x]
            self.come(self.deep, new)
            self.both(self.deep + 1, w.at[y, pc.core], self.deep + 3, pc.far, pc.c, new)
        else:
            new = w.at[1 - y, pc.core, :, x]
            self.come(self.deep, new)
            self.both(self.deep + 1, w.at[:, pc.core, :, x], self.deep + 3, pc.s, self.xp, new)
    def stage3(self):
        pc, w, y, x = self.pc, self.w, self.y, self.x
        new = w.at[1 - y, pc.core] if self.x_first else w.at[:, pc.core, :, 1 - x]
        self.come(self.deep + 1, new)
        self.go(self.deep + 4, new, pc.sib, pc.c)
    def stage4(self):
        pc, w, y, x = self.pc, self.w, self.y, self.x
        other = 1 - pc.core
        self.come(self.deep + 2, w.at[y, other, :, x])
        self.come(self.deep + 3, w.at[y, other, :, 1 - x] if self.x_first else w.at[1 - y, other, :, x])
        self.come(self.deep + 4, w.at[1 - y, other] if self.x_first else w.at[:, other, :, 1 - x])
    def finish(self):
        w, four = self.w, self.w.at[0, 0, :, 0]
        eight = w.at[0, 0] if self.x_first else w.at[:, 0, :, 0]
        for d in range(1, self.deep): sent(w.at[0, 0, 0, 0], self.ss.at[self.i, d - 1], self.pc)
        for k, part in enumerate((four, eight, four, four, eight)): sent(part, self.ss.at[self.i, self.deep + k], self.pc)

def windows(n, piece, padded):
    for part in range(n):
        for plane in range(4):
            whole, packed = (plane * n + part) * piece, plane * padded
            first, packed_first = whole // 128 * 128, packed // 128 * 128
            span = -(-(whole + piece) // 128) * 128 - first
            packed_span = -(-(packed + piece) // 128) * 128 - packed_first
            yield part, whole - first, packed - packed_first, first, span, packed_first, packed_span

def shift_lanes(block, span, shift):
    if block.shape[1] < span:
        block = jnp.concatenate([block, jnp.zeros((block.shape[0], span - block.shape[1]), block.dtype)], 1)
    shift = shift % block.shape[1]
    return pltpu.roll(block, shift, 1) if shift else block

def place_back(raw, a, out):
    n, _, owned, chunk = raw.shape
    piece, padded = out.shape[1] // (4 * n), chunk // 4
    for part, at, packed_at, first, span, packed_first, packed_span in windows(n, piece, padded):
        block = raw[part, a, :, packed_first : packed_first + packed_span].astype(F32)
        block = shift_lanes(block, span, at - packed_at)[:, :span]
        lane = lax.broadcasted_iota(jnp.int32, block.shape, 1)
        here = (lane >= at) & (lane < at + piece)
        out[:, first : first + span] = jnp.where(here, block, out[:, first : first + span])

def place_out(weight, gain, a, packs):
    n, _, _, chunk = packs.shape
    owned = weight.shape[0]
    piece, padded = weight.shape[1] // (4 * n), chunk // 4
    for part in range(n): packs[part, a, :owned] = jnp.zeros((owned, chunk), BF)
    for part, at, packed_at, first, span, packed_first, packed_span in windows(n, piece, padded):
        block = weight[:, first : first + span].astype(F32) * gain
        block = shift_lanes(block, packed_span, packed_at - at)[:, :packed_span]
        lane = lax.broadcasted_iota(jnp.int32, block.shape, 1)
        here = (lane >= packed_at) & (lane < packed_at + piece)
        before = packs[part, a, :owned, packed_first : packed_first + packed_span].astype(F32)
        packs[part, a, :owned, packed_first : packed_first + packed_span] = jnp.where(here, block, before).astype(BF)


def rope(values, table_c, table_s):
    return values * table_c + pltpu.roll(values, HEAD // 2, 1) * table_s

def layer_kernel(n, length_ref, x_ref, og_ref, qw_ref, g1_ref, b_ref, gate_ref, up_ref, g2_ref, down, outw, tables,
                 qkv_all, out_all, kv_all, q_out, half_sum, dsum, att_out, mid_out, u_own, o_own,
                 gu_v, down_v, cot_v, n2_v, act_v, gg_v, gp_v, ut, uhh, uh, ot, ohh, oh, dgu_v, dd_v, r0g, r0d, r1d, w_o2,
                 kv_v, q_v, tab_v,
                 local, save, ss, rs, g_recv, g_send, g_own, g_far, g_sib, d_recv, d_far, d_sib, c_recv, c_send,
                 kz_s, kz_r, kx_s, kx_r, n_recv, n_send, u_recv, u_send, o_recv_, o_send_, gs0, gr0, gsave, ds0, dr0, ds1, dr1, dsave):
    pc = Place(n)
    greet_all(pc)
    me, s, c = pc.me, pc.s, pc.c
    y, x, z, xp = s // 2, lax.rem(c, 2), c // 2, c + 1 - 2 * lax.rem(c, 2)
    rows, width = x_ref.shape
    owned, piece = qw_ref.shape[0], down_v.shape[0] // 4
    length = length_ref[0]
    third, owners, deep = QDIM // 3, 4 * n, n // 2

    def g_slot(i): return gu_v.at[:, pl.ds(pl.multiple_of(i * owned, owned), owned), :]
    def pack(i): return act_v.at[i, :, pl.ds(0, owned), :]
    def d_slot(i): return down_v.at[pl.ds(pl.multiple_of(i * piece, piece), piece), :]

    kvw = 2 * KVDIM + HEAD
    def cut(ref, first, w): return ref.at[:, :, :, :, :, pl.ds(first, w)]
    w_kv = cut(dgu_v.at[0], 0, kvw)
    wide = (w_kv, cut(dgu_v.at[0], kvw, third), cut(dgu_v.at[1], 0, third), cut(dgu_v.at[1], third, third),
            cut(r0g, 0, width // 2), cut(r0g, width // 2, width // 4), w_o2)
    spreads = [Spread(pc, i % 2 == 0, w, ss, rs, i) for i, w in enumerate(wide)]
    kvs, q0, q1, q2, o0, o1, o2 = spreads
    outs = ((o0, 0, width // 2), (o1, width // 2, width // 4), (o2, width // 4 * 3, width // 4))
    pairs = n // 2
    offsets = [o for j in range(1, pairs) for o in (-j, j)] + [pairs, 0]
    index = {o: i for i, o in enumerate(offsets)}
    index[-pairs] = index[pairs]
    cring = RingGather(pc, cot_v, c_send, c_recv, index)
    nring = RingGather(pc, n2_v, n_send, n_recv, index)
    uring = RingSum(pc, ut, index, uhh, uh, u_send, u_recv, u_own)
    oring = RingSum(pc, ot, index, ohh, oh, o_send_, o_recv_, o_own)
    lc = [pltpu.make_async_copy(a, b, local.at[i]) for i, (a, b) in enumerate((
        (outw.at[:, pl.ds(0, width // 2)], wide[4].at[y, pc.core, z, x]), (outw.at[:, pl.ds(width // 2, width // 4)], wide[5].at[y, pc.core, z, x]),
        (outw.at[:, pl.ds(width // 4 * 3, width // 4)], w_o2.at[y, pc.core, z, x]), (tables.at[:, pl.ds(pl.multiple_of(c * rows, rows), rows), :], tab_v)))]
    for copy in lc: copy.start()
    g1 = column(g1_ref[...])
    def scaled(first, w): return (qw_ref[:, first : first + w].astype(F32) * g1).astype(BF)
    w_kv[y, pc.core, z, x, :, : 2 * KVDIM] = scaled(QDIM, 2 * KVDIM)
    share = b_ref.shape[1]
    bias = b_ref[...].astype(F32)
    rest = jnp.zeros((1, HEAD - share), F32)
    odd = lax.rem(me, 2) == 1
    row = jnp.where(odd, jnp.concatenate([rest, bias], 1), jnp.concatenate([bias, rest], 1))
    first_row = lax.broadcasted_iota(jnp.int32, (owned, HEAD), 0) == 0
    w_kv[y, pc.core, z, x, :, 2 * KVDIM :] = jnp.where(first_row, row, 0.0).astype(BF)
    for i, w in enumerate(wide[1:4]): w[y, pc.core, z, x] = scaled(i * third, third)
    slot_pos = c * rows + lax.broadcasted_iota(jnp.int32, (rows, width), 0)
    cot_v[index[0]] = jnp.where(slot_pos < length, og_ref[...].astype(F32), 0.0).astype(BF)
    g2 = column(g2_ref[...])
    place_out(gate_ref, g2, 0, act_v)
    place_out(up_ref, g2, 1, act_v)
    short = down[...].astype(F32)
    padding = jnp.zeros((piece - short.shape[0], width), F32)
    down_v[pl.ds(pl.multiple_of(s * piece, piece), piece), :] = jnp.concatenate([short, padding], 0).astype(BF)
    pl.semaphore_wait(pltpu.get_barrier_semaphore(), n + 1)
    def gu_turn(t):
        k = s * n + lax.rem(c + n - t, n)
        arrived(g_slot(k), g_recv.at[k], pc)
        send(g_slot(k), g_slot(k), g_far.at[lax.rem(c + n - t, n)], g_recv.at[k], pc.far, c)
        send(g_slot(k), g_slot(k), g_sib.at[k], g_recv.at[k], pc.sib, c)
    for p in (kvs, q0, q1, q2): p.begin()
    own_gu = pltpu.make_async_copy(pack(c), g_slot(me), local.at[5])
    own_gu.start()
    def feed(d, v):
        to = lax.rem(c + d, n)
        send(pack(to), g_slot(me), g_send.at[to], g_recv.at[me], s, to)
        return v
    lax.fori_loop(1, n, feed, 0)
    send(pack(c), g_slot(me), g_own.at[0], g_recv.at[me], pc.far, c)
    send(pack(c), g_slot(me), g_own.at[1], g_recv.at[me], pc.sib, c)
    send(d_slot(s), d_slot(s), d_far.at[0], d_recv.at[s], pc.far, c)
    send(d_slot(s), d_slot(s), d_sib.at[s], d_recv.at[s], pc.sib, c)
    xf = x_ref[...].astype(F32)
    att_out[...] = (xf * inverse_rms(xf)).astype(BF)
    kvs.stage1()
    q0.stage1()
    q1.stage1()
    kvs.stage2()
    q2.stage1()
    q0.stage2()
    kvs.stage3()
    q1.stage2()
    for copy in lc[:3]: copy.wait()
    o0.begin(); o1.begin(); o2.begin()
    q2.stage2()
    q0.stage3()
    q1.stage3()
    q2.stage3()
    gu_turn(1); gu_turn(2)
    kvs.stage4()
    lc[3].wait()
    tc, ts = tab_v[0], tab_v[1]
    xh = att_out[...]
    def bias_of(tile):
        d = 2 * tile
        def part(i):
            plane, place = i // n, i % n
            return w_kv[plane // 2, plane % 2, place // 2, place % 2, 0:1, 2 * KVDIM :].astype(F32)
        return part(d) + part(d + 1)
    kv = product(xh, w_kv[..., : 2 * KVDIM].reshape(owners * owned, 2 * KVDIM))
    for k in range(2 * KV_HEADS):
        lanes = slice(k * HEAD, (k + 1) * HEAD)
        one = kv[:, lanes] + bias_of(QDIM // HEAD + k)
        kv_v[z, x, :, lanes] = (rope(one, tc, ts) if k < KV_HEADS else one).astype(BF)
    own_kv = kv_v.at[z, x]
    for d in range(1, deep):
        send(own_kv, own_kv, kz_s.at[d], kz_r.at[d], s, 2 * lax.rem(z + d, deep) + x)
    send(own_kv, own_kv, kx_s.at[0], kx_r.at[0], s, xp)
    o0.stage1(); o1.stage1(); o2.stage1()
    for i, p in enumerate((q0, q1, q2)):
        p.stage4()
        r = product(xh, p.w[...].reshape(owners * owned, third))
        for k in range(third // HEAD):
            h = i * (third // HEAD) + k
            q_v[h] = rope(r[:, k * HEAD : (k + 1) * HEAD] + bias_of(h), tc, ts).astype(BF)
    for d in range(1, deep):
        block = kv_v.at[lax.rem(z + deep - d, deep), x]
        arrived(block, kz_r.at[d], pc)
        send(block, block, kx_s.at[d], kx_r.at[d], s, xp)
    cring.hop(0)
    o0.stage2(); o1.stage2(); o2.stage2()
    saves = [pltpu.make_async_copy(q_v, q_out, save.at[0])]
    for i, (p, first) in enumerate(((kvs, QDIM), (q0, 0), (q1, third), (q2, 2 * third))):
        saves.append(pltpu.make_async_copy(p.w, qkv_all.at[:, :, :, :, :, pl.ds(first, p.w.shape[5])], save.at[1 + i]))
    for copy in saves: copy.start()
    for d in range(deep):
        arrived(kv_v.at[lax.rem(z + deep - d, deep), 1 - x], kx_r.at[d], pc)

    total = n * rows
    at_row = c * rows + lax.broadcasted_iota(jnp.int32, (rows, total), 0)
    at_col = lax.broadcasted_iota(jnp.int32, (rows, total), 1)
    allowed = (at_col <= at_row) & (at_col < length)
    def heads(first, count):
        def head(h, v):
            col = pl.multiple_of(h // GROUP * HEAD, HEAD)
            key = kv_v[:, :, :, pl.ds(col, HEAD)].reshape(total, HEAD)
            val = kv_v[:, :, :, pl.ds(pl.multiple_of(KVDIM + col, HEAD), HEAD)].reshape(total, HEAD)
            scores = jnp.where(allowed, contract_cols(q_v[h], key) * SCALE, MASKED)
            e = jnp.exp(scores - jnp.max(scores, axis=1, keepdims=True))
            probs = (e * (1.0 / jnp.sum(e, axis=1, keepdims=True))).astype(BF)
            att_out[:, pl.ds(pl.multiple_of(h * HEAD, HEAD), HEAD)] = product(probs, val).astype(BF)
            return v
        lax.fori_loop(first, first + count, head, 0)
    o0.stage3(); o1.stage3(); o2.stage3()
    heads(0, GROUP)
    gu_turn(3); gu_turn(4)
    cring.turn(0)
    heads(GROUP, GROUP)
    gu_turn(5); gu_turn(6)
    own_gu.wait()
    for i in range(2): sent(pack(0), g_own.at[i], pc)
    def fed(d, v):
        sent(pack(0), g_send.at[lax.rem(c + d, n)], pc)
        return v
    lax.fori_loop(1, n, fed, 0)
    gu_turn(7)
    o0.stage4(); o1.stage4(); o2.stage4()
    saves2 = [pltpu.make_async_copy(kv_v, kv_all, save.at[5])]
    for i, (p, first, w) in enumerate(outs):
        saves2.append(pltpu.make_async_copy(p.w, out_all.at[:, :, :, :, :, pl.ds(first, w)], save.at[6 + i]))
    for copy in saves2: copy.start()
    cring.turn(1)
    att = att_out[...]
    for p, first, w in outs:
        lanes = slice(first, first + w)
        mid_out[:, lanes] = x_ref[:, lanes].astype(F32) + product(att, p.w[...].reshape(owners * owned, w))
    mid = mid_out[...]
    n2_v[index[0]] = (mid * inverse_rms(mid)).astype(BF)
    nring.hop(0)
    cring.turn(2)
    arrived(d_slot(pc.far), d_recv.at[pc.far], pc)
    send(d_slot(pc.far), d_slot(pc.far), d_sib.at[pc.far], d_recv.at[pc.far], pc.sib, c)
    def across(t):
        k = pc.far * n + lax.rem(c + n - t, n)
        arrived(g_slot(k), g_recv.at[k], pc)
        send(g_slot(k), g_slot(k), g_sib.at[k], g_recv.at[k], pc.sib, c)
    for t in range(n):
        if t == n - 1:
            for copy in saves + saves2: copy.wait()
            for p in spreads: p.finish()
        across(t)
        if t == 1: nring.turn(0)
        if t == 3: cring.turn(3)
        if t == 4: nring.turn(1)
    for plane in range(2):
        other = 2 * plane + 1 - pc.core
        arrived(d_slot(other), d_recv.at[other], pc)
        def come(t, v):
            i = other * n + t
            arrived(g_slot(i), g_recv.at[i], pc)
            return v
        lax.fori_loop(0, n, come, 0)
    tall, chunk = 2 * rows, gu_v.shape[2]
    def forward(j):
        pair = slice(2 * j, 2 * j + 2)
        normed = n2_v[pair].reshape(tall, width)
        gate = product(normed, gu_v[0])
        up = product(normed, gu_v[1])
        sig = jax.nn.sigmoid(gate)
        gs = gate * sig
        act = (gs * up).astype(BF)
        act_v[pair] = act.reshape(2, 2, rows // 2, chunk)
        gp_v[pair] = gs.astype(BF).reshape(2, rows, chunk)
        gg_v[pair] = (up * (sig + gs * (1.0 - sig))).astype(BF).reshape(2, rows, chunk)
        ot[pair] = product(act, down_v[...]).astype(BF).reshape(2, rows, width)
    def backward(j):
        pair = slice(2 * j, 2 * j + 2)
        grad = contract_cols(cot_v[pair].reshape(tall, width), down_v[...])
        gg = (grad * gg_v[pair].reshape(tall, chunk).astype(F32)).astype(BF)
        gp = (grad * gp_v[pair].reshape(tall, chunk).astype(F32)).astype(BF)
        gg_v[pair] = gg.reshape(2, rows, chunk)
        gp_v[pair] = gp.reshape(2, rows, chunk)
        ut[pair] = (contract_cols(gg, gu_v[0]) + contract_cols(gp, gu_v[1])).astype(BF).reshape(2, rows, width)

    all_rows = n * rows
    plane = n * owned
    core = pc.core
    tile = 384
    def cols_of(j): return pl.ds(j * tile, tile)
    wide_pieces = [(0, j, a) for j in range(chunk // tile) for a in range(2)]
    down_pieces = [(1, j, 0) for j in range(width // tile)]
    def compute(p):
        kind, j, a = p
        if kind == 0:
            lhs, rhs = n2_v[...].reshape(all_rows, width), (gg_v, gp_v)[a]
            grad = contract_rows(lhs, rhs[:, :, cols_of(j)].reshape(all_rows, tile))
            dgu_v[a, :, :, :, :, :, cols_of(j)] = grad.astype(BF).reshape(2, 2, deep, 2, owned, tile)
            send(dgu_v.at[a, :, 1 - core, :, :, :, cols_of(j)], r0g.at[a, :, :, :, :, cols_of(j)],
                 gs0.at[a, j], gr0.at[a, j], pc.sib, c)
        else:
            grad = contract_rows(act_v[...].reshape(all_rows, chunk), cot_v[:, :, cols_of(j)].reshape(all_rows, tile))
            dd_v[:, :, :, cols_of(j)] = grad.astype(BF).reshape(2, 2, piece, tile)
            send(dd_v.at[:, 1 - core, :, cols_of(j)], r0d.at[:, :, cols_of(j)], ds0.at[j], dr0.at[j], pc.sib, c)
    def add_core(p):
        kind, j, a = p
        cols = cols_of(j)
        if kind == 0:
            arrived(r0g.at[a, :, :, :, :, cols], gr0.at[a, j], pc)
            for k in range(2):
                r0g[a, k, :, :, :, cols] = add_low(r0g[a, k, :, :, :, cols], dgu_v[a, k, core, :, :, :, cols])
            copy = pltpu.make_async_copy(r0g.at[a, :, :, :, :, cols], half_sum.at[a, :, :, :, :, cols], gsave.at[a, j])
            copy.start()
            saves.append(copy)
        else:
            arrived(r0d.at[:, :, cols], dr0.at[j], pc)
            for k in range(2):
                r0d[k, :, cols] = add_low(r0d[k, :, cols], dd_v[k, core, :, cols])
            send(r0d.at[1 - y, :, cols], r1d.at[:, cols], ds1.at[j], dr1.at[j], pc.far, c)
    def add_far(p):
        _, j, _ = p
        cols = cols_of(j)
        arrived(r1d.at[:, cols], dr1.at[j], pc)
        r1d[:, cols] = add_low(r1d[:, cols], r0d[y, :, cols])
        copy = pltpu.make_async_copy(r1d.at[:, cols], dsum.at[:, cols], dsave.at[j])
        copy.start()
        saves.append(copy)
    saves.clear()
    forward(0)
    nring.turn(2)
    forward(1)
    nring.turn(3)
    forward(2)
    forward(3)
    backward(3)
    uring.turn(0)
    oring.turn(0)
    compute(down_pieces[0])
    compute(down_pieces[1])
    add_core(down_pieces[0])
    backward(2)
    uring.turn(1)
    add_core(down_pieces[1])
    compute(down_pieces[2])
    backward(1)
    uring.turn(2)
    oring.turn(1)
    add_core(down_pieces[2])
    compute(down_pieces[3])
    backward(0)
    uring.turn(3)
    add_core(down_pieces[3])
    for i, p in enumerate(wide_pieces):
        compute(p)
        if i: add_core(wide_pieces[i - 1])
        if i == 3: uring.turn(4)
        if i == 1: oring.turn(2)
        if i == 5: oring.turn(3)
    add_core(wide_pieces[-1])
    for p in down_pieces: add_far(p)
    oring.turn(4)
    for kind, j, a in wide_pieces + down_pieces:
        cols = cols_of(j)
        if kind == 0:
            sent(r0g.at[a, :, :, :, :, cols], gs0.at[a, j], pc)
        else:
            sent(r0d.at[:, :, cols], ds0.at[j], pc)
            sent(r1d.at[:, cols], ds1.at[j], pc)
    for copy in saves: copy.wait()
    nring.finish()
    uring.finish()
    oring.finish()
    cring.finish()
    for d in range(1, deep): sent(own_kv, kz_s.at[d], pc)
    for d in range(deep): sent(own_kv, kx_s.at[d], pc)
    sent(d_slot(0), d_far.at[0], pc)
    def left(t, v):
        sent(g_slot(0), g_sib.at[pc.far * n + t], pc)
        @pl.when(t > 0)
        def _():
            src = lax.rem(c + t, n)
            sent(g_slot(0), g_far.at[src], pc)
            sent(g_slot(0), g_sib.at[s * n + src], pc)
        return v
    lax.fori_loop(0, n, left, 0)
    sent(d_slot(0), d_sib.at[s], pc)
    sent(d_slot(0), d_sib.at[pc.far], pc)

def layer_call(n, length, x, og, qkv, gain_one, bias, gate, up, gain_two, down, outw, tables):
    N, m = 4 * n, n // 2
    rows, width = x.shape
    owned, piece = qkv.shape[0], -(-down.shape[0] // 32) * 32
    chunk = 4 * piece
    S, V = jax.ShapeDtypeStruct, pltpu.VMEM
    joint = QDIM + 2 * KVDIM + HEAD
    shapes = [S((2, 2, m, 2, owned, joint), BF), S((2, 2, m, 2, owned, width), BF), S((m, 2, rows, 2 * KVDIM), BF),
              S((HEADS, rows, HEAD), BF), S((2, 2, m, 2, owned, chunk), BF), S((piece, width), BF),
              S((rows, QDIM), BF), S((rows, width), F32), S((rows, width), F32), S((rows, width), F32)]
    anys = pl.BlockSpec(memory_space=pl.ANY)
    vmem = pl.BlockSpec(memory_space=pltpu.VMEM)
    all_rows = V((n, rows, width), BF)
    hidden = V((n, rows, chunk), BF)
    scratch = [V((2, N * owned, chunk), BF), V((4 * piece, width), BF), all_rows, all_rows, V((n, 2, rows // 2, chunk), BF), hidden, hidden,
               all_rows, V((2, rows, width // 2), BF), V((2, n // 2 - 1, rows, width), BF),
               all_rows, V((2, rows, width // 2), BF), V((2, n // 2 - 1, rows, width), BF),
               V((2, 2, 2, m, 2, owned, chunk), BF), V((2, 2, piece, width), BF), V((2, 2, m, 2, owned, chunk), BF),
               V((2, piece, width), BF), V((piece, width), BF),
               V((2, 2, m, 2, owned, width // 4), BF),
               V((m, 2, rows, 2 * KVDIM), BF), V((HEADS, rows, HEAD), BF), V((2, rows, HEAD), F32)]
    a, b = chunk // 384, width // 384
    scratch += [DMA((6,)), DMA((9,)), DMA((7, m + 5)), DMA((7, m + 5)), DMA((N,)), DMA((n,)), DMA((2,)), DMA((n,)), DMA((N,)),
                DMA((4,)), DMA((1,)), DMA((4,)), DMA((2, m)), DMA((2, m)), DMA((m,)), DMA((m,)), DMA((m,)), DMA((m,))]
    scratch += [DMA((2, m))] * 6 + [DMA((2, a))] * 3 + [DMA((b,))] * 5
    return pl.pallas_call(
        functools.partial(layer_kernel, n),
        out_shape=shapes,
        in_specs=[pl.BlockSpec(memory_space=pltpu.SMEM)] + [vmem] * 9 + [anys] * 2,
        out_specs=[anys] * 6 + [vmem] * 4,
        scratch_shapes=scratch,
        compiler_params=pltpu.CompilerParams(collective_id=0, has_side_effects=True, vmem_limit_bytes=63 * 2**20),
    )(length, x, og, qkv, gain_one, bias, gate, up, gain_two, down, outw, tables)


class Reduce:
    def __init__(self, pc, far_first, p, r0, r1, r2, r3, ss, rs, i):
        self.pc, self.far_first, self.p = pc, far_first, p
        self.r0, self.r1, self.r2, self.r3, self.ss, self.rs, self.i = r0, r1, r2, r3, ss, rs, i
        self.y, self.x, self.z = pc.s // 2, lax.rem(pc.c, 2), pc.c // 2
        self.xp = pc.c + 1 - 2 * self.x
    def go(self, k, src, dst, seq, ctx):
        send(src, dst, self.ss.at[self.i, k], self.rs.at[self.i, k], seq, ctx)
    def come(self, k, dst):
        arrived(dst, self.rs.at[self.i, k], self.pc)
    def stage0(self):
        pc = self.pc
        self.go(0, self.p.at[:, 1 - pc.core], self.r0, pc.sib, pc.c)
    def stage1(self):
        pc, r0 = self.pc, self.r0
        self.come(0, r0)
        r0[...] = add_low(r0[...], self.p[:, pc.core])
        if self.far_first: self.go(1, r0.at[1 - self.y], self.r1, pc.far, pc.c)
        else: self.go(1, r0.at[:, :, 1 - self.x], self.r1, pc.s, self.xp)
    def stage2(self):
        pc, r0, r1 = self.pc, self.r0, self.r1
        self.come(1, r1)
        if self.far_first:
            r1[...] = add_low(r1[...], r0[self.y])
            self.go(2, r1.at[:, 1 - self.x], self.r2, pc.s, self.xp)
        else:
            r1[...] = add_low(r1[...], r0[:, :, self.x])
            self.go(2, r1.at[1 - self.y], self.r2, pc.far, pc.c)
    def stage3(self):
        pc, r1, r2, n = self.pc, self.r1, self.r2, self.pc.n
        self.come(2, r2)
        r2[...] = add_low(r2[...], r1[:, self.x] if self.far_first else r1[self.y])
        def hand(d, w):
            to = lax.rem(self.z + d, n // 2)
            send(r2.at[to], self.r3.at[self.z], self.ss.at[self.i, 2 + d], self.rs.at[self.i, 2 + d], pc.s, 2 * to + self.x)
            return w
        lax.fori_loop(1, n // 2, hand, 0)
    def stage4(self):
        n = self.pc.n
        total = self.r2[self.z].astype(F32)
        for d in range(1, n // 2):
            src = lax.rem(self.z + n // 2 - d, n // 2)
            arrived(self.r3.at[src], self.rs.at[self.i, 2 + d], self.pc)
            total = total + self.r3[src].astype(F32)
        return total
    def finish(self):
        sent(self.r0, self.ss.at[self.i, 0], self.pc)
        sent(self.r1, self.ss.at[self.i, 1], self.pc)
        sent(self.r2, self.ss.at[self.i, 2], self.pc)
        for d in range(1, self.pc.n // 2):
            sent(self.r2.at[0], self.ss.at[self.i, 2 + d], self.pc)

def backward_kernel(n, length_ref, x_ref, og_ref, mid_ref, u_ref, o_ref, att_ref, q_ref, kv_ref, out_ref, gate_ref, up_ref, qw_ref, gain_ref, gain_one_ref, qkv_all, tables, half_sum,
                    y_out, dx_out, dout_out, dqkv_out, dbias_out, dgate_out, dup_out, dgain_out, dgain_one_out,
                    tab_v, gm_v, gb_v, dm_v, gp_v, p_v, gs_v, dkv_v, kx, kz, raw_v, r1_v, mine_v, dx_v, qkv_v, *rest):
    pieces = 7
    bufs, (local, kxs, kxr, kzs, kzr, gss, grs, fs, fr, ss, rs) = rest[: 5 * pieces], rest[5 * pieces :]
    pc = Place(n)
    s, c = pc.s, pc.c
    rows, width = x_ref.shape
    total = n * rows
    length = length_ref[0]
    x, z = lax.rem(c, 2), c // 2
    xp = c + 1 - 2 * x
    red = [Reduce(pc, i % 2 == 0, *bufs[5 * i : 5 * i + 5], ss, rs, i) for i in range(pieces)]
    tab = pltpu.make_async_copy(tables.at[:, pl.ds(pl.multiple_of(c * rows, rows), rows), :], tab_v, local.at[0])
    tab.start()
    y = s // 2
    mine = pltpu.make_async_copy(half_sum.at[:, y], mine_v, local.at[1])
    mine.start()
    weights = pltpu.make_async_copy(qkv_all, qkv_v, local.at[2])
    weights.start()
    enter(pc)
    owned = out_ref.shape[1]
    def cross(a):
        send(half_sum.at[a, 1 - y], r1_v.at[a], fs.at[a], fr.at[a], pc.far, c)
    def feed(a):
        arrived(r1_v.at[a], fr.at[a], pc)
        if a == 0:
            cross(1)
            mine.wait()
        r1_v[a] = add_low(r1_v[a], mine_v[a])
        def hand(d, w):
            to = lax.rem(c + d, n)
            send(r1_v.at[a, to // 2, lax.rem(to, 2)], raw_v.at[c, a], gss.at[a, to], grs.at[a, c], s, to)
            return w
        lax.fori_loop(1, n, hand, 0)
        raw_v[c, a] = r1_v[a, c // 2, lax.rem(c, 2)]
    def fed(a):
        def come(d, w):
            src = lax.rem(c + d, n)
            arrived(raw_v.at[src, a], grs.at[a, src], pc)
            return w
        lax.fori_loop(1, n, come, 0)
    cross(0)
    pos = c * rows + lax.broadcasted_iota(jnp.int32, (rows, width), 0)
    live = pos < length
    mid = mid_ref[...]
    gm = jnp.where(live, og_ref[...].astype(F32), 0.0) + rms_back(mid, inverse_rms(mid), u_ref[...])
    gm_v[...] = gm
    gb_v[...] = gm.astype(BF)
    y_out[...] = jnp.where(live, mid + o_ref[...], 0.0).astype(BF)
    owners = 4 * n
    def mix(j, w):
        weight = out_ref[pl.ds(j * 16, 16)].reshape(16 * owned, width)
        r = contract_cols(gb_v[...], weight).astype(BF)
        for k in range(16 * owned // HEAD):
            dm_v[j * (16 * owned // HEAD) + k] = r[:, k * HEAD : (k + 1) * HEAD]
        return w
    lax.fori_loop(0, owners // 16, mix, 0)
    gb = gb_v[...]
    for i in range(2):
        w = width // 2
        grad = contract_rows(att_ref[...], gb[:, i * w : (i + 1) * w])
        red[i].p[...] = grad.astype(BF).reshape(red[i].p.shape)
        red[i].stage0()
    tab.wait()
    tc, ts = tab_v[0], tab_v[1]

    at_row = c * rows + lax.broadcasted_iota(jnp.int32, (rows, total), 0)
    at_col = lax.broadcasted_iota(jnp.int32, (rows, total), 1)
    allowed = (at_col <= at_row) & (at_col < length)
    def group(g):
        key = kv_ref[:, :, g * HEAD : (g + 1) * HEAD].reshape(total, HEAD)
        val = kv_ref[:, :, KVDIM + g * HEAD : KVDIM + (g + 1) * HEAD].reshape(total, HEAD)
        def head(i, w):
            h = g * GROUP + i
            part = pl.ds(pl.multiple_of(i * rows, rows), rows)
            scores = jnp.where(allowed, contract_cols(q_ref[h], key) * SCALE, MASKED)
            e = jnp.exp(scores - jnp.max(scores, axis=1, keepdims=True))
            probs = e * (1.0 / jnp.sum(e, axis=1, keepdims=True))
            gprobs = contract_cols(dm_v[h], val)
            inner = jnp.sum(probs * gprobs, axis=1, keepdims=True)
            gs = (probs * (gprobs - inner)).astype(BF)
            p_v[part, :] = probs.astype(BF)
            gs_v[part, :] = gs
            dq = product(gs, key) * SCALE
            gp_v[:, pl.ds(pl.multiple_of(h * HEAD, HEAD), HEAD)] = (dq * tc - pltpu.roll(dq, HEAD // 2, 1) * ts).astype(BF)
            return w
        lax.fori_loop(0, GROUP, head, 0)
        mine = slice(g * GROUP, (g + 1) * GROUP)
        dk = contract_rows(gs_v[...], q_ref[mine].reshape(GROUP * rows, HEAD)) * SCALE
        dv = contract_rows(p_v[...], dm_v[mine].reshape(GROUP * rows, HEAD))
        lanes = slice(g * 2 * HEAD, g * 2 * HEAD + 2 * HEAD)
        dkv_v[:, :, :, lanes] = jnp.concatenate([dk, dv], 1).astype(BF).reshape(n // 2, 2, rows, 2 * HEAD)
        send(dkv_v.at[:, 1 - x, :, lanes], kx.at[:, :, lanes], kxs.at[g], kxr.at[g], s, xp)
    def kv_x(g):
        lanes = slice(g * 2 * HEAD, g * 2 * HEAD + 2 * HEAD)
        arrived(kx.at[:, :, lanes], kxr.at[g], pc)
        kx[:, :, lanes] = add_low(kx[:, :, lanes], dkv_v[:, x, :, lanes])
        for d in range(1, n // 2):
            to = lax.rem(z + d, n // 2)
            send(kx.at[to, :, lanes], kz.at[z, :, lanes], kzs.at[g, d], kzr.at[g, d], s, 2 * to + x)
    def kv_z(g):
        lanes = slice(g * 2 * HEAD, g * 2 * HEAD + 2 * HEAD)
        sumkv = kx[z, :, lanes].astype(F32)
        for d in range(1, n // 2):
            src = lax.rem(z + n // 2 - d, n // 2)
            arrived(kz.at[src, :, lanes], kzr.at[g, d], pc)
            sumkv = sumkv + kz[src, :, lanes].astype(F32)
        dk, dv = sumkv[:, :HEAD], sumkv[:, HEAD:]
        k0, v0 = QDIM + g * HEAD, QDIM + KVDIM + g * HEAD
        gp_v[:, k0 : k0 + HEAD] = (dk * tc - pltpu.roll(dk, HEAD // 2, 1) * ts).astype(BF)
        gp_v[:, v0 : v0 + HEAD] = dv.astype(BF)
    xin = x_ref[...].astype(F32)
    inverse = inverse_rms(xin)
    def joint(i, first, w):
        xh = (x_ref[...].astype(F32) * inverse).astype(BF)
        grad = contract_rows(xh, gp_v[:, first : first + w]).astype(BF)
        shape = red[i].p.shape[:-1] + (w,)
        red[i].p[..., :w] = grad.reshape(shape)
    group(0)
    red[0].stage1(); red[1].stage1()
    feed(0)
    group(1)
    kv_x(0)
    red[0].stage2(); red[1].stage2()
    third = QDIM // 3
    for i in range(3):
        joint(2 + i, i * third, third)
        red[2 + i].stage0()
        if i == 0: kv_x(1)
    red[0].stage3(); red[1].stage3()
    red[2].stage1(); red[3].stage1(); red[4].stage1()
    feed(1)
    kv_z(0); kv_z(1)
    joint(5, QDIM, KVDIM)
    joint(6, QDIM + KVDIM, KVDIM)
    red[6].stage0()
    sums = jnp.sum(gp_v[...].astype(F32), axis=0, keepdims=True)
    p5 = red[5].p
    qk_width = QDIM + KVDIM
    at = lax.broadcasted_iota(jnp.int32, (owned, HEAD), 0)
    for d in range(owners):
        tiles = (qk_width // owners * d // HEAD, qk_width // owners * d // HEAD + 1, (qk_width + KVDIM // owners * d) // HEAD)
        part = jnp.zeros((owned, HEAD), F32)
        for k, t in enumerate(tiles):
            part = jnp.where(at == k, sums[:, t * HEAD : t * HEAD + HEAD], part)
        plane = d // n
        p5[plane // 2, plane % 2, d % n // 2, d % 2, :, KVDIM:] = part.astype(BF)
    red[5].stage0()
    red[2].stage2(); red[3].stage2(); red[4].stage2()
    red[6].stage1(); red[5].stage1()
    qk = QDIM + 2 * KVDIM
    gp = gp_v[...]
    weights.wait()
    def back(j, w):
        weight = qkv_v[pl.ds(j * 16, 16), :, :qk].reshape(16 * owned, qk)
        cols = pl.ds(pl.multiple_of(j * 16 * owned, 16 * owned), 16 * owned)
        dx_v[:, cols] = contract_cols(gp, weight)
        return w
    lax.fori_loop(0, owners // 16, back, 0)
    red[2].stage3(); red[3].stage3(); red[4].stage3()
    red[6].stage2(); red[5].stage2()
    fed(0)
    place_back(raw_v, 0, dgate_out)
    dx_out[...] = (gm_v[...] + rms_back(x_ref[...].astype(F32), inverse, dx_v[...])).astype(BF)
    for i in range(2):
        dout_out[:, i * (width // 2) : (i + 1) * (width // 2)] = red[i].stage4()
    red[6].stage3(); red[5].stage3()
    fed(1)
    place_back(raw_v, 1, dup_out)
    gain = column(gain_ref[...])
    dgain_out[...] = as_row(jnp.sum(
        dgate_out[...] * gate_ref[...].astype(F32) + dup_out[...] * up_ref[...].astype(F32), axis=1, keepdims=True
    ))
    dgate_out[...] = dgate_out[...] * gain
    dup_out[...] = dup_out[...] * gain
    gain_one = column(gain_one_ref[...])
    rows_sum = jnp.zeros((owned, 1), F32)
    for i in range(3):
        cols = slice(i * third, (i + 1) * third)
        raw = red[2 + i].stage4()
        rows_sum = rows_sum + jnp.sum(raw * qw_ref[:, cols].astype(F32), axis=1, keepdims=True)
        dqkv_out[:, cols] = raw * gain_one
    for i, first in ((6, QDIM + KVDIM), (5, QDIM)):
        cols = slice(first, first + KVDIM)
        whole = red[i].stage4()
        raw = whole[:, :KVDIM]
        rows_sum = rows_sum + jnp.sum(raw * qw_ref[:, cols].astype(F32), axis=1, keepdims=True)
        dqkv_out[:, cols] = raw * gain_one
    dbias_out[...] = whole[:8, KVDIM:]
    dgain_one_out[...] = as_row(rows_sum)
    for r in red: r.finish()
    for a in range(2):
        sent(r1_v.at[a], fs.at[a], pc)
        def left(d, w):
            sent(raw_v.at[0, a], gss.at[a, lax.rem(c + d, n)], pc)
            return w
        lax.fori_loop(1, n, left, 0)
    for g in range(2):
        lanes = slice(g * 2 * HEAD, g * 2 * HEAD + 2 * HEAD)
        sent(kx.at[:, :, lanes], kxs.at[g], pc)
        for d in range(1, n // 2): sent(kx.at[0, :, lanes], kzs.at[g, d], pc)

def backward_call(n, length, x, og, mid, u, o, att, q, kv, out_all, gate, up, qkv, gain, gain_one, qkv_all, tables, half_sum):
    S, V = jax.ShapeDtypeStruct, pltpu.VMEM
    rows, width = x.shape
    owned = qkv_all.shape[1]
    anys = pl.BlockSpec(memory_space=pl.ANY)
    vmem = pl.BlockSpec(memory_space=pltpu.VMEM)
    m = n // 2
    scratch = [V((2, rows, HEAD), F32), V((rows, width), F32), V((rows, width), BF), V((HEADS, rows, HEAD), BF),
               V((rows, QDIM + 2 * KVDIM), BF), V((GROUP * rows, n * rows), BF), V((GROUP * rows, n * rows), BF),
               V((m, 2, rows, 2 * KVDIM), BF), V((m, rows, 2 * KVDIM), BF), V((m, rows, 2 * KVDIM), BF),
               V((n, 2, owned, half_sum.shape[-1]), BF), V((2,) + half_sum.shape[2:], BF), V((2,) + half_sum.shape[2:], BF),
               V((rows, width), F32), V(qkv_all.shape, BF)]
    for i, w in enumerate((width // 2, width // 2, QDIM // 3, QDIM // 3, QDIM // 3, KVDIM + HEAD, KVDIM)):
        one = (m, 2, owned, w) if i % 2 == 0 else (2, m, owned, w)
        scratch += [V((2, 2, m, 2, owned, w), BF), V((2, m, 2, owned, w), BF), V(one, BF), V((m, owned, w), BF), V((m, owned, w), BF)]
    scratch += [DMA((3,)), DMA((2,)), DMA((2,)), DMA((2, m)), DMA((2, m)), DMA((2, n)), DMA((2, n)), DMA((2,)), DMA((2,)), DMA((7, 2 + m)), DMA((7, 2 + m))]
    return pl.pallas_call(
        functools.partial(backward_kernel, n),
        out_shape=[S((rows, width), BF), S((rows, width), BF), S((owned, width), F32), S(qkv.shape, F32), S((8, HEAD), F32),
                   S(gate.shape, F32), S(gate.shape, F32), S((1, owned), F32), S((1, owned), F32)],
        in_specs=[pl.BlockSpec(memory_space=pltpu.SMEM)] + [vmem] * 14 + [anys] * 3,
        out_specs=[vmem] * 9,
        scratch_shapes=scratch,
        compiler_params=pltpu.CompilerParams(collective_id=2, has_side_effects=True, vmem_limit_bytes=62 * 2**20),
    )(length, x, og, mid, u, o, att, q, kv, out_all, gate, up, qkv, gain, gain_one, qkv_all, tables, half_sum)


def kernel_shards(
    tokens,
    lengths,
    attn_gain,
    qkv_weight,
    qkv_bias,
    out_weight,
    mlp_gain,
    gate_weight,
    up_weight,
    down_weight,
    out_grad,
):
    seqs, parts = lax.axis_size("seq"), lax.axis_size("ctx")
    rows, width = tokens.shape[1:]
    owned = gate_weight.shape[0]
    piece = down_weight.shape[0]
    owners = seqs * parts
    me = lax.axis_index("seq") * parts + lax.axis_index("ctx")
    gain_one, gain_two = attn_gain[None], mlp_gain[None]
    half = HEAD // 2
    frequency = np.float32(ROPE_BASE) ** (-np.arange(half, dtype=np.float32) * np.float32(2.0 / HEAD))
    angles = np.arange(rows * parts, dtype=np.float32)[:, None] * frequency.astype(np.float32)[None, :]
    cosine, sine = np.cos(angles), np.sin(angles)
    tables = jnp.asarray(np.stack([np.concatenate([cosine, cosine], 1), np.concatenate([-sine, sine], 1)]), F32)
    x, og = tokens[0], out_grad[0]
    qkv_all, out_all, kv_all, q, half_sum, grad_down, att, mid, u, o = layer_call(
        parts, lengths, x, og, qkv_weight, gain_one, qkv_bias[None], gate_weight, up_weight, gain_two,
        down_weight, out_weight, tables,
    )
    joint = qkv_all.shape[-1]
    output, grad_inputs, grad_out, grad_qkv, bias_rows, grad_gate, grad_up, grad_mlp_gain, grad_attn_gain = backward_call(
        parts, lengths, x, og, mid, u, o, att, q, kv_all.reshape(parts, rows, 2 * KVDIM),
        out_all.reshape(owners, owned, width), gate_weight, up_weight, qkv_weight, gain_two, gain_one,
        qkv_all.reshape(owners, owned, joint), tables, half_sum,
    )
    per, per_value = (QDIM + KVDIM) // owners, KVDIM // owners
    grad_qk_bias = lax.dynamic_slice_in_dim(bias_rows[:2].reshape(2 * HEAD), lax.rem(per * me, HEAD), per)
    grad_value_bias = lax.dynamic_slice_in_dim(bias_rows[2], lax.rem(per_value * me, HEAD), per_value)
    return (
        output[None],
        grad_inputs[None],
        grad_attn_gain[0],
        grad_qkv,
        grad_qk_bias,
        grad_out,
        grad_mlp_gain[0],
        grad_gate,
        grad_up,
        grad_down[:piece].astype(F32),
        grad_value_bias,
    )


def solution(mesh):
    seqs, parts = mesh.shape["seq"], mesh.shape["ctx"]
    tiled = seqs == 4 and parts == 8 and 1536 // (seqs * parts) % 16 == 0
    rows, vector = P(BOTH, None), P(BOTH)
    token = P("seq", "ctx", None)
    return jax.shard_map(
        kernel_shards if tiled else plain_shards,
        mesh=mesh,
        in_specs=(token, P("seq"), vector, rows, vector, rows, vector, rows, rows, rows, token),
        out_specs=(token, token, vector, rows, vector, rows, vector, rows, rows, rows, vector),
        check_vma=False,
    )
```
